32 devices in a mesh: row: 8 (over z, y), col: 4 (over x, core).
Axes of the slice: x: 2, y: 2, z: 4, core: 2. Of those that a mesh axis runs over, the one named last changes fastest.
Arguments:
- object_field: float32 [2, 4096, 2048], P(None, 'row', 'col'), may hold values from -6 to 6
- probe: float32 [2, 256, 256], replicated, may hold values from -6 to 6
- amplitudes: bfloat16 [8, 4, 2, 2, 256, 256], P('row', 'col'), may hold values from 0.29882812 to 6
- offsets: int32 [8, 4, 2, 2, 2], P('row', 'col'), may hold values from 0 to 511, as said below
Outputs:
- object_out: float32 [2, 4096, 2048], P(None, 'row', 'col')
- probe_out: float32 [2, 256, 256], replicated
The draws below stay inside these ranges and needn't reach their ends.
Inputs may be any that keep to these rules, and one draw needn't show every extreme that they name: `offsets`: every window lies inside the object of 4096 x 2048 cells.
All inputs are finite; a program needn't handle non-finite values.
Results may differ from the reference program's by a relative error of at most 0.0003.
Values sent between devices are 32-bit elements; how exact they have to be, the bound alone decides.
No kernel may reach another device: no remote copies, remote signals or barrier semaphores. Data moves between devices by JAX's collectives and lax.ppermute only.
A program may use at most 192 MiB of HBM per device.

```python
import math
import jax
import jax.numpy as jnp
from jax import lax

W = 256
TR = 512
TC = 512
SCANS = 2
ITERS = 2
NR = 4096
NC = 2048
N_ROW = 8
N_COL = 4


def draw_offsets(key, part):
    shape = (N_ROW, N_COL, ITERS, SCANS)
    key_rows = jax.random.fold_in(key, 11)
    key_cols = jax.random.fold_in(key, 23)
    first_rows = jax.random.randint(key_rows, shape, 0, TR)
    first_cols = jax.random.randint(key_cols, shape, 0, TC)
    tile_rows = lax.broadcasted_iota(jnp.int32, shape, 0)
    tile_cols = lax.broadcasted_iota(jnp.int32, shape, 1)
    sweeps = lax.broadcasted_iota(jnp.int32, shape, 2)
    scans = lax.broadcasted_iota(jnp.int32, shape, 3)
    first_rows = jnp.where(tile_rows == N_ROW - 1, jnp.minimum(first_rows, TR - W), first_rows)
    first_cols = jnp.where(tile_cols == N_COL - 1, jnp.minimum(first_cols, TC - W), first_cols)
    corner_tile = (tile_rows == 0) & (tile_cols == 0) & (sweeps == 0)
    far_mark = corner_tile & (scans == 0)
    near_mark = corner_tile & (scans == 1)
    first_rows = jnp.where(far_mark, TR - 1, jnp.where(near_mark, 0, first_rows))
    first_cols = jnp.where(far_mark, TC - 1, jnp.where(near_mark, 0, first_cols))
    return jnp.stack([first_rows, first_cols], axis=-1).astype(jnp.int32)


def steps_of(rng, dims, shards, smallest, high):
    def one(position, blocks):
        heights = jax.random.uniform(jax.random.fold_in(jax.random.fold_in(rng, 6), position), (blocks,), jnp.float32, smallest / len(shards), high / len(shards))
        return jnp.repeat(jnp.exp(heights), dims[position] // blocks).reshape((-1,) + (1,) * (len(dims) - position - 1))

    loudness = one(*shards[0])
    for cut in shards[1:]:
        loudness = loudness * one(*cut)
    return loudness


def centred(rng, extent, spread, reach, split=(), kind=jnp.bfloat16):
    values = jax.random.normal(rng, extent, jnp.float32) * spread
    if len(split) > 0:
        values = steps_of(rng, extent, split, -0.22, 0.18) * values
    return jnp.clip(values, min=-reach, max=reach).astype(kind)


def setup_inputs(seed: int = 0) -> dict:
    splits = jax.random.split(jax.random.key(seed), 5)
    object_field = centred(splits[0], (2, NR, NC), 1.0, 6.0, ((1, 8), (2, 4)), jnp.float32)
    probe = centred(splits[1], (2, W, W), 1.0, 6.0, (), jnp.float32)
    amplitudes = jnp.clip(jnp.exp(math.log(6.0) - 2.9996462 * jax.random.uniform(splits[2], (N_ROW, N_COL, ITERS, SCANS, W, W), jnp.float32) ** steps_of(splits[2], (N_ROW, N_COL, ITERS, SCANS, W, W), ((0, 8), (1, 4)), -0.2, 0.2)), 0.29882812, 6.0).astype(jnp.bfloat16)
    offsets = draw_offsets(jax.random.fold_in(splits[4], 71), 0)
    return {"object_field": object_field, "probe": probe, "amplitudes": amplitudes, "offsets": offsets}


softening = 0.1
object_damping = 0.5
probe_damping = 1.0

def reference(object_field, probe, amplitudes, offsets):
    base_rows = jnp.arange(N_ROW, dtype=jnp.int32)[:, None, None, None] * TR
    base_cols = jnp.arange(N_COL, dtype=jnp.int32)[None, :, None, None] * TC
    global_rows = (offsets[..., 0] + base_rows).astype(jnp.int32)
    global_cols = (offsets[..., 1] + base_cols).astype(jnp.int32)
    current_object = object_field
    current_probe = probe
    for sweep in range(ITERS):
        corner_rows = global_rows[:, :, sweep, :].reshape(-1)
        corner_cols = global_cols[:, :, sweep, :].reshape(-1)
        measured = amplitudes[:, :, sweep].reshape(-1, W, W)
        probe_complex = current_probe[0] + 1j * current_probe[1]
        intensity = current_probe[0] * current_probe[0] + current_probe[1] * current_probe[1]
        frozen_object = current_object

        def visit(number, carry):
            object_num, object_den, probe_num, probe_den = carry
            anchor = (jnp.int32(0), corner_rows[number], corner_cols[number])
            patch = lax.dynamic_slice(frozen_object, anchor, (2, W, W))
            patch_complex = patch[0] + 1j * patch[1]
            exit_wave = probe_complex * patch_complex
            farfield = jnp.fft.fft2(exit_wave, norm='ortho')
            modulus = jnp.real(farfield) ** 2 + jnp.imag(farfield) ** 2
            scaled = measured[number].astype(jnp.float32) / jnp.sqrt(modulus + softening)
            corrected = farfield * scaled
            difference = jnp.fft.ifft2(corrected, norm='ortho') - exit_wave
            object_term = jnp.conj(probe_complex) * difference
            probe_term = jnp.conj(patch_complex) * difference
            object_pair = jnp.stack([jnp.real(object_term), jnp.imag(object_term)])
            present = lax.dynamic_slice(object_num, anchor, (2, W, W))
            object_num = lax.dynamic_update_slice(object_num, present + object_pair, anchor)
            plane_anchor = (corner_rows[number], corner_cols[number])
            present_den = lax.dynamic_slice(object_den, plane_anchor, (W, W))
            object_den = lax.dynamic_update_slice(object_den, present_den + intensity, plane_anchor)
            probe_num = probe_num + jnp.stack([jnp.real(probe_term), jnp.imag(probe_term)])
            probe_den = probe_den + patch[0] * patch[0] + patch[1] * patch[1]
            return (object_num, object_den, probe_num, probe_den)
        initial = (jnp.zeros((2, NR, NC), jnp.float32), jnp.zeros((NR, NC), jnp.float32), jnp.zeros((2, W, W), jnp.float32), jnp.zeros((W, W), jnp.float32))
        object_num, object_den, probe_num, probe_den = lax.fori_loop(0, corner_rows.shape[0], visit, initial)
        current_object = frozen_object + object_num / (object_den + object_damping)[None]
        current_probe = current_probe + probe_num / (probe_den + probe_damping)[None]
    return (current_object, current_probe)
```

```python
import functools
import math

import jax
import jax.numpy as jnp
import ml_dtypes
import numpy as np
from jax import lax
from jax.experimental import pallas as pl
from jax.experimental.pallas import tpu as pltpu
from jax.sharding import PartitionSpec as P

softening = 0.1
object_damping = 0.5
probe_damping = 1.0
MIB = 1 << 20
lane = 128
VMEM = pltpu.VMEM
SMEM = pltpu.SMEM


def shifted(array, axis, by):
    peers = lax.axis_size(axis)
    pairs = [(i, i + by) for i in range(peers) if 0 <= i + by < peers]
    return lax.ppermute(array, axis, pairs)


def swapped(array, axis, mask):
    peers = lax.axis_size(axis)
    return lax.ppermute(array, axis, [(i, i ^ mask) for i in range(peers)])


def handed_on(array, axis):
    peers = lax.axis_size(axis)
    pairs = [(i, i + 2 - 4 * (i % 2)) for i in range(peers)]
    return lax.ppermute(array, axis, [(i, k) for i, k in pairs if 0 <= k < peers])


def dft_tables(length):
    index = np.arange(length)
    phase = (index[:, None] * index[None, :] % length) * (2.0 * math.pi / length)
    cosine = np.cos(phase) / math.sqrt(length)
    sine = np.sin(phase) / math.sqrt(length)
    full = np.block([[cosine, -sine], [sine, cosine]])
    high = full.astype(ml_dtypes.bfloat16)
    low = (full - high.astype(np.float64)).astype(ml_dtypes.bfloat16)
    return high, low, np.ascontiguousarray(high.T), np.ascontiguousarray(low.T)


def halves(value):
    high = value.astype(jnp.bfloat16)
    return high, (value - high.astype(jnp.float32)).astype(jnp.bfloat16)


def product(a, b):
    return jnp.dot(a, b, preferred_element_type=jnp.float32)


def left_product(high, low, real, imag):
    side = real.shape[0]
    real_high, real_low = halves(real)
    imag_high, imag_low = halves(imag)
    top = jnp.concatenate([real_high, imag_high], axis=0)
    rest = jnp.concatenate([real_low, imag_low], axis=0)
    out = product(high, top) + product(high, rest) + product(low, top)
    return out[:side], out[side:]


def right_product(real, imag, high, low):
    side = real.shape[1]
    real_high, real_low = halves(real)
    imag_high, imag_low = halves(imag)
    top = jnp.concatenate([real_high, imag_high], axis=1)
    rest = jnp.concatenate([real_low, imag_low], axis=1)
    out = product(top, high) + product(rest, high) + product(top, low)
    return out[:, :side], out[:, side:]


def split_column(column):
    return lax.div(column, lane), lax.rem(column, lane)


def taken(ref, plane, row, column, side):
    first, shift = split_column(column)
    count = side // lane + 1
    slabs = [ref[plane, first + k, pl.ds(row, side), :] for k in range(count)]
    return pltpu.roll(jnp.concatenate(slabs, axis=1), count * lane - shift, 1)[:, :side]


def turned(value, shift):
    side = value.shape[0]
    wide = jnp.concatenate([value, jnp.zeros((side, lane), jnp.float32)], axis=1)
    return pltpu.roll(wide, shift, 1)


def add_slabs(ref, lead, row, first, wide):
    side = wide.shape[0]
    for k in range(wide.shape[1] // lane):
        spot = lead + (first + k, pl.ds(row, side), slice(None))
        ref[spot] += wide[:, k * lane : (k + 1) * lane]


def columns(number):
    return slice(number * lane, (number + 1) * lane)


def scan_kernel(
    sweep, pieces, offsets_ref, probe_ref, amplitude_ref, ah_ref, al_ref, bh_ref, bl_ref, *refs
):
    if pieces:
        own_ref, right_ref, lower_ref, corner_ref = refs[:4]
        terms_refs, sums_ref, field_ref = refs[4:6], refs[6], refs[7]
        rows, cols = own_ref.shape[1:]
        slabs = cols // lane
        for plane in range(2):
            for k in range(slabs):
                field_ref[plane, k, :rows] = own_ref[plane, :, columns(k)]
                field_ref[plane, k, rows:] = lower_ref[plane, :, columns(k)]
            for k in range(right_ref.shape[2] // lane):
                field_ref[plane, slabs + k, :rows] = right_ref[plane, :, columns(k)]
                field_ref[plane, slabs + k, rows:] = corner_ref[plane, :, columns(k)]
    else:
        field_ref = refs[0]
        terms_refs, sums_ref = refs[1:3], refs[3]
    side = probe_ref.shape[1]
    probe_real, probe_imag = probe_ref[0], probe_ref[1]
    for scan in range(2):
        place = ((4 * 2 + sweep) * 2 + scan) * 2
        row, column = offsets_ref[place], offsets_ref[place + 1]
        patch_real = taken(field_ref, 0, row, column, side)
        patch_imag = taken(field_ref, 1, row, column, side)
        wave_real = probe_real * patch_real - probe_imag * patch_imag
        wave_imag = probe_real * patch_imag + probe_imag * patch_real
        mid = left_product(bh_ref[...], bl_ref[...], wave_real, wave_imag)
        far_real, far_imag = right_product(*mid, ah_ref[...], al_ref[...])
        scale = amplitude_ref[scan].astype(jnp.float32) * lax.rsqrt(
            far_real * far_real + far_imag * far_imag + softening
        )
        mid = left_product(ah_ref[...], al_ref[...], far_real * scale, far_imag * scale)
        back_real, back_imag = right_product(*mid, bh_ref[...], bl_ref[...])
        diff_real = back_real - wave_real
        diff_imag = back_imag - wave_imag
        terms_refs[scan][0] = probe_real * diff_real + probe_imag * diff_imag
        terms_refs[scan][1] = probe_real * diff_imag - probe_imag * diff_real
        sums = (
            patch_real * diff_real + patch_imag * diff_imag,
            patch_real * diff_imag - patch_imag * diff_real,
            patch_real * patch_real + patch_imag * patch_imag,
        )
        for number, value in enumerate(sums):
            if scan == 0:
                sums_ref[number] = value
            else:
                sums_ref[number] += value


def scan_step(sweep, offsets, probe, amplitudes, tables, *field):
    side = probe.shape[1]
    pieces = len(field) == 4
    shapes = [jax.ShapeDtypeStruct((2, side, side), jnp.float32)] * 2
    shapes.append(jax.ShapeDtypeStruct((3, side, side), jnp.float32))
    if pieces:
        rows, cols = field[0].shape[1:]
        shapes.append(jax.ShapeDtypeStruct((2, (cols + side) // lane, rows + side, lane), jnp.float32))
    return pl.pallas_call(
        functools.partial(scan_kernel, sweep, pieces),
        out_shape=shapes,
        in_specs=[pl.BlockSpec(memory_space=SMEM)] + [pl.BlockSpec(memory_space=VMEM)] * (6 + len(field)),
        out_specs=[pl.BlockSpec(memory_space=VMEM)] * len(shapes),
        compiler_params=pltpu.CompilerParams(vmem_limit_bytes=40 * MIB),
        name="scan",
    )(offsets, probe, amplitudes, *tables, *field)


def density_kernel(sweep, reach, offsets_ref, probe_ref, out_ref, total_ref):
    side = probe_ref.shape[1]
    slabs, height = out_ref.shape[:2]
    breadth = slabs * lane
    tile = height - side if reach else height
    span = breadth - side if reach else breadth
    total_ref[...] = jnp.zeros_like(total_ref)
    power = probe_ref[0] * probe_ref[0] + probe_ref[1] * probe_ref[1]
    steps = (-1, 0, 1) if reach else (-1, 0)
    for down in steps:
        for along in steps:
            for scan in range(2):
                place = ((((down + 1) * 3 + along + 1) * 2 + sweep) * 2 + scan) * 2
                row = offsets_ref[place] + side + down * tile
                column = offsets_ref[place + 1] + side + along * span

                @pl.when((row > 0) & (row < side + height) & (column > 0) & (column < side + breadth))
                def _():
                    first, shift = split_column(column)
                    add_slabs(total_ref, (), row, first, turned(power, shift))

    out_ref[...] = total_ref[side // lane : side // lane + slabs, side : side + height]


def density(sweep, reach, offsets, probe, tile):
    side = probe.shape[1]
    extra = side if reach else 0
    height, slabs = tile[0] + extra, (tile[1] + extra) // lane
    return pl.pallas_call(
        functools.partial(density_kernel, sweep, reach),
        out_shape=jax.ShapeDtypeStruct((slabs, height, lane), jnp.float32),
        in_specs=[pl.BlockSpec(memory_space=SMEM), pl.BlockSpec(memory_space=VMEM)],
        out_specs=pl.BlockSpec(memory_space=VMEM),
        scratch_shapes=[VMEM((slabs + 2 * side // lane + 1, height + 2 * side, lane), jnp.float32)],
        compiler_params=pltpu.CompilerParams(vmem_limit_bytes=24 * MIB),
        name="density",
    )(offsets, probe)


def add_windows(total_ref, offsets_ref, sweep, down, tile, side, limit, terms):
    for scan in range(2):
        place = ((((down + 1) * 3 + 1) * 2 + sweep) * 2 + scan) * 2
        row = offsets_ref[place] + side + down * tile
        first, shift = split_column(offsets_ref[place + 1])

        @pl.when((row > 0) & (row < side + limit))
        def _():
            for plane in range(2):
                add_slabs(total_ref, (plane,), row, first, turned(terms[scan][plane], shift))


def gather_kernel(sweep, tile, parity_ref, offsets_ref, *refs):
    own, partner, passed = refs[0:2], refs[2:4], refs[4:6]
    out_ref, left_ref, right_ref, total_ref = refs[6:]
    slabs, height = out_ref.shape[1:3]
    edge = left_ref.shape[1]
    side = edge * lane
    total_ref[...] = jnp.zeros_like(total_ref)
    odd = parity_ref[0] == 1
    add_windows(total_ref, offsets_ref, sweep, 0, tile, side, height, own)

    @pl.when(odd)
    def _():
        add_windows(total_ref, offsets_ref, sweep, -1, tile, side, height, partner)
        add_windows(total_ref, offsets_ref, sweep, 1, tile, side, height, passed)

    @pl.when(jnp.logical_not(odd))
    def _():
        add_windows(total_ref, offsets_ref, sweep, 1, tile, side, height, partner)
        add_windows(total_ref, offsets_ref, sweep, -1, tile, side, height, passed)

    out_ref[...] = total_ref[:, :, side : side + height]
    left_ref[...] = total_ref[:, :edge, side : side + height]
    right_ref[...] = total_ref[:, slabs - edge :, side : side + height]


def gather_all(sweep, parity, offsets, own, partner, passed, tile):
    side = own[0].shape[2]
    height, slabs = tile[0] + side, (tile[1] + side) // lane
    edge = jax.ShapeDtypeStruct((2, side // lane, height, lane), jnp.float32)
    return pl.pallas_call(
        functools.partial(gather_kernel, sweep, tile[0]),
        out_shape=[jax.ShapeDtypeStruct((2, slabs, height, lane), jnp.float32), edge, edge],
        in_specs=[pl.BlockSpec(memory_space=SMEM)] * 2 + [pl.BlockSpec(memory_space=VMEM)] * 6,
        out_specs=[pl.BlockSpec(memory_space=VMEM)] * 3,
        scratch_shapes=[VMEM((2, slabs, height + 2 * side, lane), jnp.float32)],
        compiler_params=pltpu.CompilerParams(vmem_limit_bytes=40 * MIB),
        name="gather",
    )(parity, offsets, *own, *partner, *passed)


def renew_kernel(field_ref, density_ref, terms_ref, left_ref, right_ref, out_ref):
    slabs = field_ref.shape[1]
    edge = left_ref.shape[1]
    for k in range(slabs):
        part = 1.0 / (density_ref[k] + object_damping)
        for plane in range(2):
            terms = terms_ref[plane, k]
            if k < edge:
                terms += left_ref[plane, k]
            if k >= slabs - edge:
                terms += right_ref[plane, k - (slabs - edge)]
            out_ref[plane, k] = field_ref[plane, k] + terms * part


def renew(field, dense, terms, left, right):
    return pl.pallas_call(
        renew_kernel,
        out_shape=jax.ShapeDtypeStruct(field.shape, jnp.float32),
        in_specs=[pl.BlockSpec(memory_space=VMEM)] * 5,
        out_specs=pl.BlockSpec(memory_space=VMEM),
        compiler_params=pltpu.CompilerParams(vmem_limit_bytes=40 * MIB),
        name="renew",
    )(field, dense, terms, left, right)


def settle_kernel(sweep, offsets_ref, *refs):
    own, upper = refs[0:2], refs[2:4]
    out_ref, right_ref, total_ref = refs[4:]
    slabs, tile = out_ref.shape[1:3]
    side = right_ref.shape[1] * lane
    total_ref[...] = jnp.zeros_like(total_ref)
    add_windows(total_ref, offsets_ref, sweep, 0, tile, side, tile, own)
    add_windows(total_ref, offsets_ref, sweep, -1, tile, side, tile, upper)
    out_ref[...] = total_ref[:, :slabs, side : side + tile]
    right_ref[...] = total_ref[:, slabs:, side : side + tile]


def settle(sweep, offsets, own, upper, tile):
    side = own[0].shape[2]
    slabs, edge = tile[1] // lane, side // lane
    return pl.pallas_call(
        functools.partial(settle_kernel, sweep),
        out_shape=[
            jax.ShapeDtypeStruct((2, slabs, tile[0], lane), jnp.float32),
            jax.ShapeDtypeStruct((2, edge, tile[0], lane), jnp.float32),
        ],
        in_specs=[pl.BlockSpec(memory_space=SMEM)] + [pl.BlockSpec(memory_space=VMEM)] * 4,
        out_specs=[pl.BlockSpec(memory_space=VMEM)] * 2,
        scratch_shapes=[VMEM((2, slabs + edge, tile[0] + 2 * side, lane), jnp.float32)],
        compiler_params=pltpu.CompilerParams(vmem_limit_bytes=40 * MIB),
        name="settle",
    )(offsets, *own, *upper)


def final_kernel(field_ref, density_ref, terms_ref, left_ref, out_ref):
    slabs, tile = terms_ref.shape[1:3]
    for k in range(slabs):
        part = 1.0 / (density_ref[k] + object_damping)
        for plane in range(2):
            terms = terms_ref[plane, k]
            if k < left_ref.shape[1]:
                terms += left_ref[plane, k]
            out_ref[plane, :, columns(k)] = field_ref[plane, k, :tile] + terms * part


def final(field, dense, terms, left):
    slabs, tile = terms.shape[1:3]
    return pl.pallas_call(
        final_kernel,
        out_shape=jax.ShapeDtypeStruct((2, tile, slabs * lane), jnp.float32),
        in_specs=[pl.BlockSpec(memory_space=VMEM)] * 4,
        out_specs=pl.BlockSpec(memory_space=VMEM),
        compiler_params=pltpu.CompilerParams(vmem_limit_bytes=40 * MIB),
        name="final",
    )(field, dense, terms, left)


def all_summed(value):
    steps = []
    for bit in range(int(math.log2(lax.axis_size("col")))):
        mine = lax.rem(lax.axis_index("col") >> bit, 2)
        half = value.shape[0] // 2
        kept = lax.dynamic_slice_in_dim(value, mine * half, half, 0)
        sent = lax.dynamic_slice_in_dim(value, (1 - mine) * half, half, 0)
        value = kept + swapped(sent, "col", 1 << bit)
        steps.append((bit, mine))
    for bit in range(int(math.log2(lax.axis_size("row")))):
        value = value + swapped(value, "row", 1 << bit)
    for bit, mine in reversed(steps):
        other = swapped(value, "col", 1 << bit)
        first = jnp.where(mine == 0, value, other)
        second = jnp.where(mine == 0, other, value)
        value = jnp.concatenate([first, second], axis=0)
    return value


def local(tables, object_field, probe, amplitudes, offsets):
    side = probe.shape[1]
    tile = object_field.shape[1:]
    own_offsets = offsets[0, 0].reshape(-1)
    measured = amplitudes[0, 0]
    parity = lax.rem(lax.axis_index("row"), 2).reshape(1)

    lower = shifted(object_field[:, :side, :], "row", -1)
    right = shifted(object_field[:, :, :side], "col", -1)
    column = jnp.concatenate([shifted(own_offsets, "row", 1), own_offsets, shifted(own_offsets, "row", -1)])
    near = jnp.stack([shifted(column, "col", 1), column, shifted(column, "col", -1)])
    near = near.reshape(3, 3, -1).transpose(1, 0, 2).reshape(-1)
    corner = shifted(lower[:, :, :side], "col", -1)

    dense = density(0, True, near, probe, tile)
    terms_0, terms_1, sums, field = scan_step(
        0, near, probe, measured[0], tables, object_field, right, lower, corner
    )
    own = (terms_0, terms_1)
    partner = [swapped(t, "row", 1) for t in own]
    passed = [handed_on(t, "row") for t in partner]
    total = all_summed(sums.reshape(-1, side)).reshape(3, side, side)
    probe = probe + total[:2] / (total[2] + probe_damping)[None]
    terms, to_left, to_right = gather_all(0, parity, near, own, partner, passed, tile)
    left = shifted(to_right, "col", 1)
    right = shifted(to_left, "col", -1)
    field = renew(field, dense, terms, left, right)

    dense = density(1, False, near, probe, tile)
    terms_0, terms_1, sums = scan_step(1, near, probe, measured[1], tables, field)
    own = (terms_0, terms_1)
    upper = [shifted(t, "row", 1) for t in own]
    total = all_summed(sums.reshape(-1, side)).reshape(3, side, side)
    probe = probe + total[:2] / (total[2] + probe_damping)[None]
    terms, to_right = settle(1, near, own, upper, tile)
    left = shifted(to_right, "col", 1)
    return final(field, dense, terms, left), probe


def solution(mesh):
    placed = (
        P(None, "row", "col"),
        P(),
        P("row", "col", None, None, None, None),
        P("row", "col", None, None, None),
    )

    def whole(object_field, probe, amplitudes, offsets):
        tables = tuple(jnp.asarray(t) for t in dft_tables(probe.shape[1]))
        body = jax.shard_map(
            lambda *args: local(args[:4], *args[4:]),
            mesh=mesh,
            in_specs=(P(),) * 4 + placed,
            out_specs=(P(None, "row", "col"), P()),
            check_vma=False,
        )
        return body(*tables, object_field, probe, amplitudes, offsets)

    return whole
```

```python
import functools
import math

import jax
import jax.numpy as jnp
import ml_dtypes
import numpy as np
from jax import lax
from jax.experimental import pallas as pl
from jax.experimental.pallas import tpu as pltpu
from jax.sharding import PartitionSpec as P

softening = 0.1
object_damping = 0.5
probe_damping = 1.0
MIB = 1 << 20
lane = 128
VMEM = pltpu.VMEM
SMEM = pltpu.SMEM


def shifted(array, axis, by):
    peers = lax.axis_size(axis)
    pairs = [(i, i + by) for i in range(peers) if 0 <= i + by < peers]
    return lax.ppermute(array, axis, pairs)


def swapped(array, axis, mask):
    peers = lax.axis_size(axis)
    return lax.ppermute(array, axis, [(i, i ^ mask) for i in range(peers)])


def dft_tables(length):
    index = np.arange(length)
    phase = (index[:, None] * index[None, :] % length) * (2.0 * math.pi / length)
    cosine = np.cos(phase) / math.sqrt(length)
    sine = np.sin(phase) / math.sqrt(length)
    full = np.block([[cosine, -sine], [sine, cosine]])
    high = full.astype(ml_dtypes.bfloat16)
    low = (full - high.astype(np.float64)).astype(ml_dtypes.bfloat16)
    return high, low, np.ascontiguousarray(high.T), np.ascontiguousarray(low.T)


def halves(value):
    high = value.astype(jnp.bfloat16)
    return high, (value - high.astype(jnp.float32)).astype(jnp.bfloat16)


def product(a, b):
    return jnp.dot(a, b, preferred_element_type=jnp.float32)


def left_product(high, low, real, imag):
    side = real.shape[0]
    real_high, real_low = halves(real)
    imag_high, imag_low = halves(imag)
    top = jnp.concatenate([real_high, imag_high], axis=0)
    rest = jnp.concatenate([real_low, imag_low], axis=0)
    out = product(high, top) + product(high, rest) + product(low, top)
    return out[:side], out[side:]


def right_product(real, imag, high, low):
    side = real.shape[1]
    real_high, real_low = halves(real)
    imag_high, imag_low = halves(imag)
    top = jnp.concatenate([real_high, imag_high], axis=1)
    rest = jnp.concatenate([real_low, imag_low], axis=1)
    out = product(top, high) + product(rest, high) + product(top, low)
    return out[:, :side], out[:, side:]


def split_column(column):
    return lax.div(column, lane), lax.rem(column, lane)


def taken(ref, plane, row, column, side):
    first, shift = split_column(column)
    count = side // lane + 1
    slabs = [ref[plane, first + k, pl.ds(row, side), :] for k in range(count)]
    return pltpu.roll(jnp.concatenate(slabs, axis=1), count * lane - shift, 1)[:, :side]


def turned(value, shift):
    side = value.shape[0]
    wide = jnp.concatenate([value, jnp.zeros((side, lane), jnp.float32)], axis=1)
    return pltpu.roll(wide, shift, 1)


def add_slabs(ref, lead, row, first, wide):
    side = wide.shape[0]
    for k in range(wide.shape[1] // lane):
        spot = lead + (first + k, pl.ds(row, side), slice(None))
        ref[spot] += wide[:, k * lane : (k + 1) * lane]


def columns(number):
    return slice(number * lane, (number + 1) * lane)


def whole_spec(count):
    return [pl.BlockSpec(memory_space=VMEM)] * count


def offsets_spec():
    return pl.BlockSpec(memory_space=SMEM)


def shape_of(*dims):
    return jax.ShapeDtypeStruct(dims, jnp.float32)


def cost(flops, moved):
    return pl.CostEstimate(flops=flops, bytes_accessed=moved, transcendentals=0)


def place_of(down, along, sweep, scan):
    return ((((down + 1) * 2 + along + 1) * 2 + sweep) * 2 + scan) * 2


def scan_kernel(
    sweep, flat, offsets_ref, probe_ref, amplitude_ref, ah_ref, al_ref, bh_ref, bl_ref, *refs
):
    own_ref, right_ref, first_ref, second_ref, corner_ref = refs[:5]
    terms_ref, down_first_ref, down_second_ref, beside_ref, cross_ref, sums_ref = refs[5:11]
    field_ref, total_ref = refs[11:]
    side = probe_ref.shape[1]
    edge = side // lane
    slabs, rows = terms_ref.shape[1:3]

    def slab(ref, plane, k):
        return ref[plane, :, columns(k)] if flat else ref[plane, k]

    for plane in range(2):
        for k in range(slabs):
            field_ref[plane, k, :rows] = slab(own_ref, plane, k)
        for k in range(edge):
            field_ref[plane, slabs + k, :rows] = slab(right_ref, plane, k)
            field_ref[plane, k, rows:] = slab(first_ref, plane, k)
            field_ref[plane, slabs + k, rows:] = slab(corner_ref, plane, k)
        for k in range(edge, slabs):
            field_ref[plane, k, rows:] = slab(second_ref, plane, k - edge)
    total_ref[...] = jnp.zeros_like(total_ref)
    probe_real, probe_imag = probe_ref[0], probe_ref[1]
    for scan in range(2):
        place = place_of(0, 0, sweep, scan)
        row, column = offsets_ref[place], offsets_ref[place + 1]
        first, shift = split_column(column)
        patch_real = taken(field_ref, 0, row, column, side)
        patch_imag = taken(field_ref, 1, row, column, side)
        wave_real = probe_real * patch_real - probe_imag * patch_imag
        wave_imag = probe_real * patch_imag + probe_imag * patch_real
        mid = left_product(bh_ref[...], bl_ref[...], wave_real, wave_imag)
        far_real, far_imag = right_product(*mid, ah_ref[...], al_ref[...])
        scale = amplitude_ref[scan].astype(jnp.float32) * lax.rsqrt(
            far_real * far_real + far_imag * far_imag + softening
        )
        mid = left_product(ah_ref[...], al_ref[...], far_real * scale, far_imag * scale)
        back_real, back_imag = right_product(*mid, bh_ref[...], bl_ref[...])
        diff_real = back_real - wave_real
        diff_imag = back_imag - wave_imag
        term_real = probe_real * diff_real + probe_imag * diff_imag
        term_imag = probe_real * diff_imag - probe_imag * diff_real
        add_slabs(total_ref, (0,), row, first, turned(term_real, shift))
        add_slabs(total_ref, (1,), row, first, turned(term_imag, shift))
        sums = (
            patch_real * diff_real + patch_imag * diff_imag,
            patch_real * diff_imag - patch_imag * diff_real,
            patch_real * patch_real + patch_imag * patch_imag,
        )
        for number, value in enumerate(sums):
            if scan == 0:
                sums_ref[number] = value
            else:
                sums_ref[number] += value
    terms_ref[...] = total_ref[:, :slabs, :rows]
    beside_ref[...] = total_ref[:, slabs:, :rows]
    cross_ref[...] = total_ref[:, slabs:, rows:]
    down_first_ref[...] = total_ref[:, :edge, rows:]
    down_second_ref[...] = total_ref[:, edge:slabs, rows:]


def scan_step(sweep, flat, offsets, probe, amplitudes, tables, *field):
    side = probe.shape[1]
    edge = side // lane
    rows = field[1].shape[1 if flat else 2]
    slabs = field[0].shape[2] // lane if flat else field[0].shape[1]
    shapes = [
        shape_of(2, slabs, rows, lane),
        shape_of(2, edge, side, lane),
        shape_of(2, slabs - edge, side, lane),
        shape_of(2, edge, rows, lane),
        shape_of(2, edge, side, lane),
        shape_of(3, side, side),
    ]
    return pl.pallas_call(
        functools.partial(scan_kernel, sweep, flat),
        out_shape=shapes,
        in_specs=[offsets_spec()] + whole_spec(6 + len(field)),
        out_specs=whole_spec(len(shapes)),
        scratch_shapes=[VMEM((2, slabs + edge, rows + side, lane), jnp.float32)] * 2,
        compiler_params=pltpu.CompilerParams(vmem_limit_bytes=22 * MIB),
        cost_estimate=cost(7_000_000_000, 12 * MIB),
        name="scan",
    )(offsets, probe, amplitudes, *tables, *field)


def density_kernel(sweep, offsets_ref, probe_ref, out_ref, total_ref):
    side = probe_ref.shape[1]
    slabs, tile = out_ref.shape[:2]
    span = slabs * lane
    total_ref[...] = jnp.zeros_like(total_ref)
    power = probe_ref[0] * probe_ref[0] + probe_ref[1] * probe_ref[1]
    for down in (-1, 0):
        for along in (-1, 0):
            for scan in range(2):
                place = place_of(down, along, sweep, scan)
                row = offsets_ref[place] + side + down * tile
                column = offsets_ref[place + 1] + side + along * span

                @pl.when((row > 0) & (column > 0))
                def _():
                    first, shift = split_column(column)
                    add_slabs(total_ref, (), row, first, turned(power, shift))

    out_ref[...] = total_ref[side // lane : side // lane + slabs, side : side + tile]


def density(sweep, offsets, probe, tile):
    side = probe.shape[1]
    slabs = tile[1] // lane
    return pl.pallas_call(
        functools.partial(density_kernel, sweep),
        out_shape=shape_of(slabs, tile[0], lane),
        in_specs=[offsets_spec()] + whole_spec(1),
        out_specs=whole_spec(1)[0],
        scratch_shapes=[VMEM((slabs + 2 * side // lane, tile[0] + 2 * side, lane), jnp.float32)],
        compiler_params=pltpu.CompilerParams(vmem_limit_bytes=8 * MIB),
        cost_estimate=cost(1_000_000, 6 * MIB),
        name="density",
    )(offsets, probe)


def renew_kernel(flat, last, *refs):
    field_ref, density_ref, terms_ref, left_ref, first_ref, second_ref = refs[:6]
    out_ref = refs[6]
    slabs, rows = terms_ref.shape[1:3]
    edge, side = first_ref.shape[1:3]
    for k in range(slabs):
        part = 1.0 / (density_ref[k] + object_damping)
        for plane in range(2):
            upper = first_ref[plane, k] if k < edge else second_ref[plane, k - edge]
            top = terms_ref[plane, k, :side] + upper
            rest = terms_ref[plane, k, side:]
            if k < edge:
                top += left_ref[plane, k, :side]
                rest += left_ref[plane, k, side:]
            before = field_ref[plane, :, columns(k)] if flat else field_ref[plane, k]
            top = before[:side] + top * part[:side]
            rest = before[side:] + rest * part[side:]
            if last:
                out_ref[plane, :side, columns(k)] = top
                out_ref[plane, side:, columns(k)] = rest
                continue
            out_ref[plane, k, :side] = top
            out_ref[plane, k, side:] = rest
            up_first_ref, up_second_ref, beside_ref = refs[7:]
            if k < edge:
                up_first_ref[plane, k] = top
                beside_ref[plane, k, :side] = top
                beside_ref[plane, k, side:] = rest
            else:
                up_second_ref[plane, k - edge] = top


def renew(flat, last, field, dense, terms, left, first, second):
    slabs, rows = terms.shape[1:3]
    edge, side = first.shape[1:3]
    if last:
        shapes = [shape_of(2, rows, slabs * lane)]
    else:
        shapes = [
            shape_of(2, slabs, rows, lane),
            shape_of(2, edge, side, lane),
            shape_of(2, slabs - edge, side, lane),
            shape_of(2, edge, rows, lane),
        ]
    return pl.pallas_call(
        functools.partial(renew_kernel, flat, last),
        out_shape=shapes,
        in_specs=whole_spec(6),
        out_specs=whole_spec(len(shapes)),
        compiler_params=pltpu.CompilerParams(vmem_limit_bytes=4 * MIB),
        cost_estimate=cost(4_000_000, 10 * MIB),
        name="renew",
    )(field, dense, terms, left, first, second)


def all_summed(value):
    steps = []
    for bit in range(int(math.log2(lax.axis_size("col")))):
        mine = lax.rem(lax.axis_index("col") >> bit, 2)
        half = value.shape[0] // 2
        kept = lax.dynamic_slice_in_dim(value, mine * half, half, 0)
        sent = lax.dynamic_slice_in_dim(value, (1 - mine) * half, half, 0)
        value = kept + swapped(sent, "col", 1 << bit)
        steps.append((bit, mine))
    for bit in range(int(math.log2(lax.axis_size("row")))):
        value = value + swapped(value, "row", 1 << bit)
    for bit, mine in reversed(steps):
        other = swapped(value, "col", 1 << bit)
        first = jnp.where(mine == 0, value, other)
        second = jnp.where(mine == 0, other, value)
        value = jnp.concatenate([first, second], axis=0)
    return value


def local(tables, object_field, probe, amplitudes, offsets):
    side = probe.shape[1]
    tile = object_field.shape[1:]
    measured = amplitudes[0, 0]
    own_offsets = offsets[0, 0].reshape(-1)

    first = shifted(object_field[:, :side, :side], "row", -1)
    second = shifted(object_field[:, :side, side:], "row", -1)
    right = shifted(object_field[:, :, :side], "col", -1)
    near = jnp.stack([shifted(own_offsets, "row", 1), own_offsets])
    near = jnp.stack([shifted(near, "col", 1), near], axis=1).reshape(-1)
    dense = density(0, near, probe, tile)
    first, dense = lax.optimization_barrier((first, dense))
    corner = shifted(first, "col", -1)
    field = object_field
    for sweep in range(offsets.shape[2]):
        flat = sweep == 0
        last = sweep == offsets.shape[2] - 1
        terms, down_first, down_second, beside, cross, sums = scan_step(
            sweep, flat, near, probe, measured[sweep], tables, field, right, first, second, corner
        )
        cross = shifted(cross, "col", 1)
        second = shifted(down_second, "row", 1)
        left = shifted(beside, "col", 1)
        total = all_summed(sums.reshape(-1, side)).reshape(3, side, side)
        first = shifted(down_first + cross, "row", 1)
        if sweep > 0:
            dense = density(sweep, near, probe, tile)
        probe = probe + total[:2] / (total[2] + probe_damping)[None]
        renewed = renew(flat, last, field, dense, terms, left, first, second)
        field = renewed[0]
        if not last:
            first = shifted(renewed[1], "row", -1)
            second = shifted(renewed[2], "row", -1)
            right = shifted(renewed[3], "col", -1)
            corner = shifted(first, "col", -1)
    return field, probe


def solution(mesh):
    placed = (
        P(None, "row", "col"),
        P(),
        P("row", "col", None, None, None, None),
        P("row", "col", None, None, None),
    )

    def whole(object_field, probe, amplitudes, offsets):
        tables = tuple(jnp.asarray(t) for t in dft_tables(probe.shape[1]))
        body = jax.shard_map(
            lambda *args: local(args[:4], *args[4:]),
            mesh=mesh,
            in_specs=(P(),) * 4 + placed,
            out_specs=(P(None, "row", "col"), P()),
            check_vma=False,
        )
        return body(*tables, object_field, probe, amplitudes, offsets)

    return whole
```

```python
import functools
import math

import jax
import jax.numpy as jnp
import ml_dtypes
import numpy as np
from jax import lax
from jax.experimental import pallas as pl
from jax.experimental.pallas import tpu as pltpu
from jax.sharding import PartitionSpec as P

softening = 0.1
object_damping = 0.5
probe_damping = 1.0
MIB = 1 << 20
lane = 128
SCAN_LIMIT = 24 * MIB
VMEM = pltpu.VMEM
SMEM = pltpu.SMEM


def shifted(array, axis, by):
    peers = lax.axis_size(axis)
    return lax.ppermute(array, axis, [(i, (i + by) % peers) for i in range(peers)])


def swapped(array, axis, mask):
    peers = lax.axis_size(axis)
    return lax.ppermute(array, axis, [(i, i ^ mask) for i in range(peers)])


def dft_table(length):
    index = np.arange(length)
    phase = (index[:, None] * index[None, :] % length) * (2.0 * math.pi / length)
    parts = []
    for value in (np.cos(phase) / math.sqrt(length), np.sin(phase) / math.sqrt(length)):
        high = value.astype(ml_dtypes.bfloat16)
        parts += [high, (value - high.astype(np.float64)).astype(ml_dtypes.bfloat16)]
    return np.stack(parts)


def halves(value):
    high = value.astype(jnp.bfloat16)
    return high, (value - high.astype(jnp.float32)).astype(jnp.bfloat16)


def product(a, b):
    return jnp.dot(a, b, preferred_element_type=jnp.float32)


def left_product(high, low, real, imag):
    side = real.shape[0]
    real_high, real_low = halves(real)
    imag_high, imag_low = halves(imag)
    top = jnp.concatenate([real_high, imag_high], axis=0)
    rest = jnp.concatenate([real_low, imag_low], axis=0)
    out = product(high, top) + product(high, rest) + product(low, top)
    return out[:side], out[side:]


def right_product(real, imag, high, low):
    side = real.shape[1]
    real_high, real_low = halves(real)
    imag_high, imag_low = halves(imag)
    top = jnp.concatenate([real_high, imag_high], axis=1)
    rest = jnp.concatenate([real_low, imag_low], axis=1)
    out = product(top, high) + product(rest, high) + product(top, low)
    return out[:, :side], out[:, side:]


def split_column(column):
    return lax.div(column, lane), lax.rem(column, lane)


def taken(ref, plane, row, column, side):
    first, shift = split_column(column)
    count = side // lane + 1
    slabs = [ref[plane, first + k, pl.ds(row, side), :] for k in range(count)]
    return pltpu.roll(jnp.concatenate(slabs, axis=1), count * lane - shift, 1)[:, :side]


def turned(value, shift):
    side = value.shape[0]
    wide = jnp.concatenate([value, jnp.zeros((side, lane), jnp.float32)], axis=1)
    return pltpu.roll(wide, shift, 1)


def add_slabs(ref, lead, row, first, wide):
    side = wide.shape[0]
    for k in range(wide.shape[1] // lane):
        spot = lead + (first + k, pl.ds(row, side), slice(None))
        ref[spot] += wide[:, k * lane : (k + 1) * lane]


def columns(number):
    return slice(number * lane, (number + 1) * lane)


def whole_spec(count):
    return [pl.BlockSpec(memory_space=VMEM)] * count


def offsets_spec():
    return pl.BlockSpec(memory_space=SMEM)


def shape_of(*dims):
    return jax.ShapeDtypeStruct(dims, jnp.float32)


def cost(flops, moved):
    return pl.CostEstimate(flops=flops, bytes_accessed=moved, transcendentals=0)


def place_of(down, along, sweep, scan):
    return ((((down + 1) * 2 + along + 1) * 2 + sweep) * 2 + scan) * 2


def halves_of(bit, half):
    mine = lax.rem(lax.axis_index("col") >> bit, 2)
    kept = pl.ds(pl.multiple_of(mine * half, 8), half)
    return kept, pl.ds(pl.multiple_of((1 - mine) * half, 8), half)


def scan_kernel(sweep, flat, offsets_ref, *refs):
    probe_hbm, amplitude_hbm, table_hbm, own_hbm, right_hbm, first_hbm, second_hbm, corner_hbm = refs[:8]
    terms_hbm, down_first_hbm, down_second_hbm, beside_hbm, cross_hbm, kept_hbm, sent_hbm = refs[8:15]
    field_ref, total_ref, probe_ref, amplitude_ref, table_ref, forth_ref, back_ref, sums_ref = refs[15:23]
    field_sem, small_sem, out_sem = refs[23:]
    side = probe_ref.shape[1]
    edge = side // lane
    slabs, rows = terms_hbm.shape[1:3]

    copies = []

    def fetch(source, target):
        copies.append(pltpu.make_async_copy(source, target, field_sem))

    small = [
        pltpu.make_async_copy(table_hbm, table_ref, small_sem.at[0]),
        pltpu.make_async_copy(probe_hbm, probe_ref, small_sem.at[1]),
        pltpu.make_async_copy(amplitude_hbm.at[sweep], amplitude_ref, small_sem.at[2]),
    ]
    if flat:
        for k in range(slabs):
            fetch(own_hbm.at[:, :, columns(k)], field_ref.at[:, k, :rows])
        for k in range(edge):
            fetch(right_hbm.at[:, :, columns(k)], field_ref.at[:, slabs + k, :rows])
            fetch(first_hbm.at[:, :, columns(k)], field_ref.at[:, k, rows:])
            fetch(corner_hbm.at[:, :, columns(k)], field_ref.at[:, slabs + k, rows:])
        for k in range(edge, slabs):
            fetch(second_hbm.at[:, :, columns(k - edge)], field_ref.at[:, k, rows:])
    else:
        fetch(own_hbm, field_ref.at[:, :slabs, :rows])
        fetch(right_hbm, field_ref.at[:, slabs:, :rows])
        fetch(first_hbm, field_ref.at[:, :edge, rows:])
        fetch(second_hbm, field_ref.at[:, edge:slabs, rows:])
        fetch(corner_hbm, field_ref.at[:, slabs:, rows:])
    small[0].start()
    for copy in copies:
        copy.start()
    for copy in small[1:]:
        copy.start()
    total_ref[...] = jnp.zeros_like(total_ref)
    small[0].wait()
    for part in range(2):
        cosine, sine = table_ref[part], table_ref[2 + part]
        forth_ref[part, :side, :side] = cosine
        forth_ref[part, side:, side:] = cosine
        forth_ref[part, :side, side:] = -sine
        forth_ref[part, side:, :side] = sine
        back_ref[part, :side, :side] = cosine
        back_ref[part, side:, side:] = cosine
        back_ref[part, :side, side:] = sine
        back_ref[part, side:, :side] = -sine
    for copy in small[1:]:
        copy.wait()
    for copy in copies:
        copy.wait()
    probe_real, probe_imag = probe_ref[0], probe_ref[1]
    for scan in range(2):
        place = place_of(0, 0, sweep, scan)
        row, column = offsets_ref[place], offsets_ref[place + 1]
        first, shift = split_column(column)
        patch_real = taken(field_ref, 0, row, column, side)
        patch_imag = taken(field_ref, 1, row, column, side)
        wave_real = probe_real * patch_real - probe_imag * patch_imag
        wave_imag = probe_real * patch_imag + probe_imag * patch_real
        mid = left_product(back_ref[0], back_ref[1], wave_real, wave_imag)
        far_real, far_imag = right_product(*mid, forth_ref[0], forth_ref[1])
        scale = amplitude_ref[scan].astype(jnp.float32) * lax.rsqrt(
            far_real * far_real + far_imag * far_imag + softening
        )
        mid = left_product(forth_ref[0], forth_ref[1], far_real * scale, far_imag * scale)
        back_real, back_imag = right_product(*mid, back_ref[0], back_ref[1])
        diff_real = back_real - wave_real
        diff_imag = back_imag - wave_imag
        term_real = probe_real * diff_real + probe_imag * diff_imag
        term_imag = probe_real * diff_imag - probe_imag * diff_real
        add_slabs(total_ref, (0,), row, first, turned(term_real, shift))
        add_slabs(total_ref, (1,), row, first, turned(term_imag, shift))
        sums = (
            patch_real * diff_real + patch_imag * diff_imag,
            patch_real * diff_imag - patch_imag * diff_real,
            patch_real * patch_real + patch_imag * patch_imag,
        )
        for number, value in enumerate(sums):
            spot = slice(number * side, (number + 1) * side)
            if scan == 0:
                sums_ref[spot] = value
            else:
                sums_ref[spot] += value
    kept, sent = halves_of(0, kept_hbm.shape[0])
    outs = [
        (sums_ref.at[sent], sent_hbm),
        (sums_ref.at[kept], kept_hbm),
        (total_ref.at[:, slabs:, rows:], cross_hbm),
        (total_ref.at[:, edge:slabs, rows:], down_second_hbm),
        (total_ref.at[:, :edge, rows:], down_first_hbm),
        (total_ref.at[:, slabs:, :rows], beside_hbm),
        (total_ref.at[:, :slabs, :rows], terms_hbm),
    ]
    outs = [pltpu.make_async_copy(source, target, out_sem) for source, target in outs]
    for copy in outs:
        copy.start()
    for copy in outs:
        copy.wait()


def scan_step(sweep, flat, offsets, probe, amplitudes, table, *field):
    side = probe.shape[1]
    edge = side // lane
    rows = field[1].shape[1 if flat else 2]
    slabs = field[0].shape[2] // lane if flat else field[0].shape[1]
    shapes = [
        shape_of(2, slabs, rows, lane),
        shape_of(2, edge, side, lane),
        shape_of(2, slabs - edge, side, lane),
        shape_of(2, edge, rows, lane),
        shape_of(2, edge, side, lane),
        shape_of(3 * side // 2, side),
        shape_of(3 * side // 2, side),
    ]
    return pl.pallas_call(
        functools.partial(scan_kernel, sweep, flat),
        out_shape=shapes,
        in_specs=[offsets_spec()] + [pl.BlockSpec(memory_space=pl.ANY)] * (3 + len(field)),
        out_specs=[pl.BlockSpec(memory_space=pl.ANY)] * len(shapes),
        scratch_shapes=[
            VMEM((2, slabs + edge, rows + side, lane), jnp.float32),
            VMEM((2, slabs + edge, rows + side, lane), jnp.float32),
            VMEM(probe.shape, jnp.float32),
            VMEM(amplitudes.shape[1:], amplitudes.dtype),
            VMEM(table.shape, table.dtype),
            VMEM((2, 2 * side, 2 * side), table.dtype),
            VMEM((2, 2 * side, 2 * side), table.dtype),
            VMEM((3 * side, side), jnp.float32),
            pltpu.SemaphoreType.DMA,
            pltpu.SemaphoreType.DMA((3,)),
            pltpu.SemaphoreType.DMA,
        ],
        compiler_params=pltpu.CompilerParams(vmem_limit_bytes=SCAN_LIMIT),
        cost_estimate=cost(7_000_000_000, 12 * MIB),
        name="scan",
    )(offsets, probe, amplitudes, table, *field)


def density_kernel(sweep, offsets_ref, probe_ref, out_ref, total_ref):
    side = probe_ref.shape[1]
    slabs, tile = out_ref.shape[:2]
    span = slabs * lane
    total_ref[...] = jnp.zeros_like(total_ref)
    power = probe_ref[0] * probe_ref[0] + probe_ref[1] * probe_ref[1]
    for down in (-1, 0):
        for along in (-1, 0):
            for scan in range(2):
                place = place_of(down, along, sweep, scan)
                row = offsets_ref[place] + side + down * tile
                column = offsets_ref[place + 1] + side + along * span

                @pl.when((row > 0) & (column > 0))
                def _():
                    first, shift = split_column(column)
                    add_slabs(total_ref, (), row, first, turned(power, shift))

    out_ref[...] = total_ref[side // lane : side // lane + slabs, side : side + tile]


def density(sweep, offsets, probe, tile):
    side = probe.shape[1]
    slabs = tile[1] // lane
    return pl.pallas_call(
        functools.partial(density_kernel, sweep),
        out_shape=shape_of(slabs, tile[0], lane),
        in_specs=[offsets_spec()] + whole_spec(1),
        out_specs=whole_spec(1)[0],
        scratch_shapes=[VMEM((slabs + 2 * side // lane, tile[0] + 2 * side, lane), jnp.float32)],
        compiler_params=pltpu.CompilerParams(vmem_limit_bytes=8 * MIB),
        cost_estimate=cost(1_000_000, 6 * MIB),
        name="density",
    )(offsets, probe)


def renew_kernel(flat, last, *refs):
    field_ref, density_ref, terms_ref, left_ref, first_ref, second_ref = refs[:6]
    out_ref = refs[6]
    slabs, rows = terms_ref.shape[1:3]
    edge, side = first_ref.shape[1:3]
    for k in range(slabs):
        part = 1.0 / (density_ref[k] + object_damping)
        for plane in range(2):
            upper = first_ref[plane, k] if k < edge else second_ref[plane, k - edge]
            top = terms_ref[plane, k, :side] + upper
            rest = terms_ref[plane, k, side:]
            if k < edge:
                top += left_ref[plane, k, :side]
                rest += left_ref[plane, k, side:]
            before = field_ref[plane, :, columns(k)] if flat else field_ref[plane, k]
            top = before[:side] + top * part[:side]
            rest = before[side:] + rest * part[side:]
            if last:
                out_ref[plane, :side, columns(k)] = top
                out_ref[plane, side:, columns(k)] = rest
                continue
            out_ref[plane, k, :side] = top
            out_ref[plane, k, side:] = rest
            up_first_ref, up_second_ref, beside_ref = refs[7:]
            if k < edge:
                up_first_ref[plane, k] = top
                beside_ref[plane, k, :side] = top
                beside_ref[plane, k, side:] = rest
            else:
                up_second_ref[plane, k - edge] = top


def renew(flat, last, field, dense, terms, left, first, second):
    slabs, rows = terms.shape[1:3]
    edge, side = first.shape[1:3]
    if last:
        shapes = [shape_of(2, rows, slabs * lane)]
    else:
        shapes = [
            shape_of(2, slabs, rows, lane),
            shape_of(2, edge, side, lane),
            shape_of(2, slabs - edge, side, lane),
            shape_of(2, edge, rows, lane),
        ]
    return pl.pallas_call(
        functools.partial(renew_kernel, flat, last),
        out_shape=shapes,
        in_specs=whole_spec(6),
        out_specs=whole_spec(len(shapes)),
        compiler_params=pltpu.CompilerParams(vmem_limit_bytes=4 * MIB),
        cost_estimate=cost(4_000_000, 10 * MIB),
        name="renew",
    )(field, dense, terms, left, first, second)


def fold_kernel(bit, value_ref, came_ref, kept_ref, sent_ref, total_ref):
    total_ref[...] = value_ref[...] + came_ref[...]
    kept, sent = halves_of(bit, kept_ref.shape[0])
    kept_ref[...] = total_ref[kept]
    sent_ref[...] = total_ref[sent]


def fold(bit, value, came):
    rows, side = value.shape
    return pl.pallas_call(
        functools.partial(fold_kernel, bit),
        out_shape=[shape_of(rows // 2, side)] * 2,
        in_specs=whole_spec(2),
        out_specs=whole_spec(2),
        scratch_shapes=[VMEM(value.shape, jnp.float32)],
        compiler_params=pltpu.CompilerParams(vmem_limit_bytes=4 * MIB),
        cost_estimate=cost(100_000, MIB),
        name="fold",
    )(value, came)


def join_kernel(bit, value_ref, other_ref, out_ref):
    kept, sent = halves_of(bit, value_ref.shape[0])
    out_ref[kept] = value_ref[...]
    out_ref[sent] = other_ref[...]


def join(bit, value, other):
    rows, side = value.shape
    return pl.pallas_call(
        functools.partial(join_kernel, bit),
        out_shape=shape_of(2 * rows, side),
        in_specs=whole_spec(2),
        out_specs=whole_spec(1)[0],
        compiler_params=pltpu.CompilerParams(vmem_limit_bytes=4 * MIB),
        cost_estimate=cost(100_000, MIB),
        name="join",
    )(value, other)


def illuminate_kernel(value_ref, other_ref, probe_ref, out_ref, total_ref):
    kept, sent = halves_of(0, value_ref.shape[0])
    total_ref[kept] = value_ref[...]
    total_ref[sent] = other_ref[...]
    side = probe_ref.shape[1]
    part = 1.0 / (total_ref[2 * side :] + probe_damping)
    out_ref[0] = probe_ref[0] + total_ref[:side] * part
    out_ref[1] = probe_ref[1] + total_ref[side : 2 * side] * part


def illuminate(value, other, probe):
    rows, side = value.shape
    return pl.pallas_call(
        illuminate_kernel,
        out_shape=shape_of(*probe.shape),
        in_specs=whole_spec(3),
        out_specs=whole_spec(1)[0],
        scratch_shapes=[VMEM((2 * rows, side), jnp.float32)],
        compiler_params=pltpu.CompilerParams(vmem_limit_bytes=6 * MIB),
        cost_estimate=cost(1_000_000, 2 * MIB),
        name="illuminate",
    )(value, other, probe)


def tied(*values):
    return lax.optimization_barrier(values)


def local(table, object_field, probe, amplitudes, offsets):
    side = probe.shape[1]
    tile = object_field.shape[1:]
    measured = amplitudes[0, 0]
    own_offsets = offsets[0, 0].reshape(-1)
    col_bits = int(math.log2(lax.axis_size("col")))
    row_bits = int(math.log2(lax.axis_size("row")))

    strip, whole = tied(object_field[:, :side, :side], object_field)
    first = shifted(strip, "row", -1)
    second = shifted(whole[:, :side, side:], "row", -1)
    right = shifted(object_field[:, :, :side], "col", -1)
    near = jnp.stack([shifted(own_offsets, "row", 1), own_offsets])
    near = jnp.stack([shifted(near, "col", 1), near], axis=1).reshape(-1)
    dense = density(0, near, probe, tile)
    first, dense = tied(first, dense)
    corner = shifted(first, "col", -1)
    field = object_field
    for sweep in range(offsets.shape[2]):
        flat = sweep == 0
        last = sweep == offsets.shape[2] - 1
        terms, down_first, down_second, beside, cross, kept, sent = scan_step(
            sweep, flat, near, probe, measured, table, field, right, first, second, corner
        )
        cross = shifted(cross, "col", 1)
        second = shifted(down_second, "row", 1)
        left = shifted(beside, "col", 1)
        came = swapped(sent, "col", 1)
        for bit in range(1, col_bits):
            kept, sent = fold(bit, kept, came)
            came = swapped(sent, "col", 1 << bit)
        came, cross = tied(came, cross)
        total = kept + came
        first = shifted(down_first + cross, "row", 1)
        for bit in range(row_bits):
            came = swapped(total, "row", 1 << bit)
            if bit == 0:
                came, second = tied(came, second)
            if bit == 1 and not last:
                came, first, left = tied(came, first, left)
            if bit == 2 and last:
                came, left = tied(came, left)
            total = total + came
        for bit in reversed(range(1, col_bits)):
            other = swapped(total, "col", 1 << bit)
            if last and bit == col_bits - 1:
                other, first = tied(other, first)
            total = join(bit, total, other)
        other = swapped(total, "col", 1)
        if sweep > 0:
            dense = density(sweep, near, probe, tile)
        probe = illuminate(total, other, probe)
        renewed = renew(flat, last, field, dense, terms, left, first, second)
        field = renewed[0]
        if not last:
            first = shifted(renewed[1], "row", -1)
            second = shifted(renewed[2], "row", -1)
            right = shifted(renewed[3], "col", -1)
            corner = shifted(first, "col", -1)
    return field, probe


def solution(mesh):
    placed = (
        P(None, "row", "col"),
        P(),
        P("row", "col", None, None, None, None),
        P("row", "col", None, None, None),
    )

    def whole(object_field, probe, amplitudes, offsets):
        table = jnp.asarray(dft_table(probe.shape[1]))
        body = jax.shard_map(
            local,
            mesh=mesh,
            in_specs=(P(),) + placed,
            out_specs=(P(None, "row", "col"), P()),
            check_vma=False,
        )
        return body(table, object_field, probe, amplitudes, offsets)

    return whole
```

```python
import functools
import math

import jax
import jax.numpy as jnp
import ml_dtypes
import numpy as np
from jax import lax
from jax.experimental import pallas as pl
from jax.experimental.pallas import tpu as pltpu
from jax.sharding import PartitionSpec as P

softening = 0.1
object_damping = 0.5
probe_damping = 1.0
MIB = 1 << 20
lane = 128
SCAN_LIMIT = 24 * MIB
VMEM = pltpu.VMEM
SMEM = pltpu.SMEM


def shifted(array, axis, by):
    peers = lax.axis_size(axis)
    return lax.ppermute(array, axis, [(i, (i + by) % peers) for i in range(peers)])


def swapped(array, axis, mask):
    peers = lax.axis_size(axis)
    return lax.ppermute(array, axis, [(i, i ^ mask) for i in range(peers)])


def handed_on(array, axis):
    peers = lax.axis_size(axis)
    return lax.ppermute(array, axis, [(i, (i + 2 - 4 * (i % 2)) % peers) for i in range(peers)])


def dft_tables(length):
    half = length // 2
    index = np.arange(half)
    parts = []
    for odd in range(2):
        phase = ((2 * index[:, None] + odd) * index[None, :] % length) * (2.0 * math.pi / length)
        real, imag = np.cos(phase) / math.sqrt(length), -np.sin(phase) / math.sqrt(length)
        full = np.block([[real, -imag], [imag, real]])
        for value in (full, full.T):
            high = value.astype(ml_dtypes.bfloat16)
            parts += [high, (value - high.astype(np.float64)).astype(ml_dtypes.bfloat16)]
    return np.stack(parts)


def halves(value):
    high = value.astype(jnp.bfloat16)
    return high, (value - high.astype(jnp.float32)).astype(jnp.bfloat16)


def product(a, b):
    return jnp.dot(a, b, preferred_element_type=jnp.float32)


def left_product(table_ref, number, data):
    top, rest = halves(data)
    high, low = table_ref[2 * number], table_ref[2 * number + 1]
    return product(high, top) + product(high, rest) + product(low, top)


def right_product(data, table_ref, number):
    top, rest = halves(data)
    high, low = table_ref[2 * number], table_ref[2 * number + 1]
    return product(top, high) + product(rest, high) + product(top, low)


def stacked(values, axis):
    return jnp.concatenate(values, axis=axis)


def forward(table_ref, real, imag):
    half = real.shape[0] // 2
    even = stacked([real[:half] + real[half:], imag[:half] + imag[half:]], 0)
    odd = stacked([real[:half] - real[half:], imag[:half] - imag[half:]], 0)
    even, odd = left_product(table_ref, 0, even), left_product(table_ref, 2, odd)
    real, imag = stacked([even[:half], odd[:half]], 0), stacked([even[half:], odd[half:]], 0)
    even = stacked([real[:, :half] + real[:, half:], imag[:, :half] + imag[:, half:]], 1)
    odd = stacked([real[:, :half] - real[:, half:], imag[:, :half] - imag[:, half:]], 1)
    even, odd = right_product(even, table_ref, 1), right_product(odd, table_ref, 3)
    return stacked([even[:, :half], odd[:, :half]], 1), stacked([even[:, half:], odd[:, half:]], 1)


def backward(table_ref, real, imag):
    half = real.shape[0] // 2
    even = left_product(table_ref, 1, stacked([real[:half], imag[:half]], 0))
    odd = left_product(table_ref, 3, stacked([real[half:], imag[half:]], 0))
    one, two = even + odd, even - odd
    real, imag = stacked([one[:half], two[:half]], 0), stacked([one[half:], two[half:]], 0)
    even = right_product(stacked([real[:, :half], imag[:, :half]], 1), table_ref, 0)
    odd = right_product(stacked([real[:, half:], imag[:, half:]], 1), table_ref, 2)
    one, two = even + odd, even - odd
    return stacked([one[:, :half], two[:, :half]], 1), stacked([one[:, half:], two[:, half:]], 1)


def reorder_kernel(amplitude_ref, out_ref):
    side = amplitude_ref.shape[3]
    half = side // 2

    def choice(axis):
        target = lax.broadcasted_iota(jnp.int32, (side, side), axis)
        source = lax.broadcasted_iota(jnp.int32, (side, side), 1 - axis)
        wanted = jnp.where(target < half, 2 * target, 2 * (target - half) + 1)
        return jnp.where(source == wanted, 1.0, 0.0).astype(jnp.bfloat16)

    rows, cols = choice(0), choice(1)
    for sweep in range(amplitude_ref.shape[0]):
        for scan in range(amplitude_ref.shape[1]):
            moved = product(rows, amplitude_ref[sweep, scan]).astype(jnp.bfloat16)
            out_ref[sweep, scan] = product(moved, cols).astype(jnp.bfloat16)


def reorder(amplitudes):
    return pl.pallas_call(
        reorder_kernel,
        out_shape=jax.ShapeDtypeStruct(amplitudes.shape, amplitudes.dtype),
        in_specs=[pl.BlockSpec(memory_space=VMEM)],
        out_specs=pl.BlockSpec(memory_space=VMEM),
        compiler_params=pltpu.CompilerParams(vmem_limit_bytes=8 * MIB),
        cost_estimate=pl.CostEstimate(flops=300_000_000, bytes_accessed=MIB, transcendentals=0),
        name="reorder",
    )(amplitudes)


def split_column(column):
    return lax.div(column, lane), lax.rem(column, lane)


def taken(ref, plane, row, column, side):
    first, shift = split_column(column)
    count = side // lane + 1
    slabs = [ref[plane, first + k, pl.ds(row, side), :] for k in range(count)]
    return pltpu.roll(jnp.concatenate(slabs, axis=1), count * lane - shift, 1)[:, :side]


def turned(value, shift):
    side = value.shape[0]
    wide = jnp.concatenate([value, jnp.zeros((side, lane), jnp.float32)], axis=1)
    return pltpu.roll(wide, shift, 1)


def add_slabs(ref, lead, row, first, wide):
    side = wide.shape[0]
    for k in range(wide.shape[1] // lane):
        spot = lead + (first + k, pl.ds(row, side), slice(None))
        ref[spot] += wide[:, k * lane : (k + 1) * lane]


def columns(number):
    return slice(number * lane, (number + 1) * lane)


def whole_spec(count):
    return [pl.BlockSpec(memory_space=VMEM)] * count


def offsets_spec():
    return pl.BlockSpec(memory_space=SMEM)


def shape_of(*dims):
    return jax.ShapeDtypeStruct(dims, jnp.float32)


def cost(flops, moved):
    return pl.CostEstimate(flops=flops, bytes_accessed=moved, transcendentals=0)


def corner_of(offsets_ref, down, along, sweep, scan):
    spot = (down + 1, along + 1, sweep, scan)
    return offsets_ref[spot + (0,)], offsets_ref[spot + (1,)]


def halves_of(bit, half):
    mine = lax.rem(lax.axis_index("col") >> bit, 2)
    kept = pl.ds(pl.multiple_of(mine * half, 8), half)
    return kept, pl.ds(pl.multiple_of((1 - mine) * half, 8), half)


def scan_kernel(sweep, last, counts, offsets_ref, *refs):
    inputs, outputs, scratch = counts
    probe_hbm, amplitude_hbm, table_hbm = refs[:3]
    field_in = refs[3:inputs]
    outs_hbm = refs[inputs : inputs + outputs]
    rest = refs[inputs + outputs :]
    probe_ref, amplitude_ref, table_ref, sums_ref, windows_ref = rest[:5]
    small_sem, field_sem, out_sem = rest[5:8]
    side = probe_ref.shape[1]
    copies = []

    def fetch(source, target):
        copies.append(pltpu.make_async_copy(source, target, field_sem))

    small = [
        pltpu.make_async_copy(table_hbm, table_ref, small_sem.at[0]),
        pltpu.make_async_copy(probe_hbm, probe_ref, small_sem.at[1]),
        pltpu.make_async_copy(amplitude_hbm.at[sweep], amplitude_ref, small_sem.at[2]),
    ]
    if last:
        field_ref = field_in[0]
    else:
        own_hbm, right_hbm, first_hbm, second_hbm, corner_hbm = field_in
        field_ref = rest[8]
        rows, edge = own_hbm.shape[1], side // lane
        slabs = own_hbm.shape[2] // lane
        for k in range(slabs):
            fetch(own_hbm.at[:, :, columns(k)], field_ref.at[:, k, :rows])
        for k in range(edge):
            fetch(right_hbm.at[:, :, columns(k)], field_ref.at[:, slabs + k, :rows])
            fetch(first_hbm.at[:, :, columns(k)], field_ref.at[:, k, rows:])
            fetch(corner_hbm.at[:, :, columns(k)], field_ref.at[:, slabs + k, rows:])
        for k in range(edge, slabs):
            fetch(second_hbm.at[:, :, columns(k - edge)], field_ref.at[:, k, rows:])
    small[0].start()
    for copy in copies:
        copy.start()
    for copy in small[1:]:
        copy.start()
    small[0].wait()
    for copy in small[1:]:
        copy.wait()
    for copy in copies:
        copy.wait()
    probe_real, probe_imag = probe_ref[0], probe_ref[1]
    pending = []
    for scan in range(2):
        row, column = offsets_ref[0, 0, sweep, scan, 0], offsets_ref[0, 0, sweep, scan, 1]
        patch_real = taken(field_ref, 0, row, column, side)
        patch_imag = taken(field_ref, 1, row, column, side)
        wave_real = probe_real * patch_real - probe_imag * patch_imag
        wave_imag = probe_real * patch_imag + probe_imag * patch_real
        far_real, far_imag = forward(table_ref, wave_real, wave_imag)
        scale = amplitude_ref[scan].astype(jnp.float32) * lax.rsqrt(
            far_real * far_real + far_imag * far_imag + softening
        )
        back_real, back_imag = backward(table_ref, far_real * scale, far_imag * scale)
        diff_real = back_real - wave_real
        diff_imag = back_imag - wave_imag
        term_real = probe_real * diff_real + probe_imag * diff_imag
        term_imag = probe_real * diff_imag - probe_imag * diff_real
        windows_ref[scan, 0] = term_real
        windows_ref[scan, 1] = term_imag
        copy = pltpu.make_async_copy(windows_ref.at[scan], outs_hbm[2].at[scan], out_sem)
        copy.start()
        pending.append(copy)
        sums = (
            patch_real * diff_real + patch_imag * diff_imag,
            patch_real * diff_imag - patch_imag * diff_real,
            patch_real * patch_real + patch_imag * patch_imag,
        )
        for number, value in enumerate(sums):
            spot = slice(number * side, (number + 1) * side)
            if scan == 0:
                sums_ref[spot] = value
            else:
                sums_ref[spot] += value
    kept, sent = halves_of(0, outs_hbm[0].shape[0])
    outs = [(sums_ref.at[sent], outs_hbm[1]), (sums_ref.at[kept], outs_hbm[0])]
    outs = [pltpu.make_async_copy(source, target, out_sem) for source, target in outs]
    for copy in outs:
        copy.start()
    for copy in pending + outs:
        copy.wait()


def scan_step(sweep, last, offsets, probe, amplitudes, table, *field):
    side = probe.shape[1]
    shapes = [shape_of(3 * side // 2, side)] * 2 + [shape_of(2, 2, side, side)]
    scratch = [
        VMEM(probe.shape, jnp.float32),
        VMEM(amplitudes.shape[1:], amplitudes.dtype),
        VMEM(table.shape, table.dtype),
        VMEM((3 * side, side), jnp.float32),
        VMEM((2, 2, side, side), jnp.float32),
        pltpu.SemaphoreType.DMA((3,)),
        pltpu.SemaphoreType.DMA,
        pltpu.SemaphoreType.DMA,
    ]
    if not last:
        rows, cols = field[0].shape[1:]
        scratch.append(VMEM((2, (cols + side) // lane, rows + side, lane), jnp.float32))
    anywhere = pl.BlockSpec(memory_space=pl.ANY)
    counts = (3 + len(field), len(shapes), len(scratch))
    return pl.pallas_call(
        functools.partial(scan_kernel, sweep, last, counts),
        out_shape=shapes,
        in_specs=[offsets_spec()] + [anywhere] * 3 + (whole_spec(1) if last else [anywhere] * len(field)),
        out_specs=[anywhere] * len(shapes),
        scratch_shapes=scratch,
        compiler_params=pltpu.CompilerParams(vmem_limit_bytes=SCAN_LIMIT),
        cost_estimate=cost(7_000_000_000, 12 * MIB),
        name="scan",
    )(offsets, probe, amplitudes, table, *field)


def place_kernel(sweep, offsets_ref, windows_ref, total_ref, *edge_refs):
    side = windows_ref.shape[2]
    edge = side // lane
    slabs, height = total_ref.shape[1:3]
    total_ref[...] = jnp.zeros_like(total_ref)
    for scan in range(2):
        row, column = offsets_ref[0, 0, sweep, scan, 0], offsets_ref[0, 0, sweep, scan, 1]
        first, shift = split_column(column)
        for plane in range(2):
            add_slabs(total_ref, (plane,), row, first, turned(windows_ref[scan, plane], shift))
    for ref, start in zip(edge_refs, (slabs - edge, 0)):
        ref[...] = total_ref[:, start : start + edge, side : height - side]


def place(sweep, offsets, windows, tile, sides):
    side = windows.shape[2]
    edge = side // lane
    height, slabs = tile[0] + side, tile[1] // lane + edge
    shapes = [shape_of(2, slabs, height, lane)] + [shape_of(2, edge, height - 2 * side, lane)] * sides
    return pl.pallas_call(
        functools.partial(place_kernel, sweep),
        out_shape=shapes,
        in_specs=[offsets_spec()] + whole_spec(1),
        out_specs=whole_spec(len(shapes)),
        compiler_params=pltpu.CompilerParams(vmem_limit_bytes=4 * MIB),
        cost_estimate=cost(1_000_000, 6 * MIB),
        name="place",
    )(offsets, windows)


def density_kernel(sweep, reach, offsets_ref, probe_ref, out_ref, total_ref):
    side = probe_ref.shape[1]
    slabs, height = out_ref.shape[:2]
    breadth = slabs * lane
    tile = height - side if reach else height
    span = breadth - side if reach else breadth
    total_ref[...] = jnp.zeros_like(total_ref)
    power = probe_ref[0] * probe_ref[0] + probe_ref[1] * probe_ref[1]
    steps = (-1, 0, 1) if reach else (-1, 0)
    for down in steps:
        for along in steps:
            for scan in range(2):
                row, column = corner_of(offsets_ref, down, along, sweep, scan)
                row += side + down * tile
                column += side + along * span

                @pl.when((row > 0) & (row < side + height) & (column > 0) & (column < side + breadth))
                def _():
                    first, shift = split_column(column)
                    add_slabs(total_ref, (), row, first, turned(power, shift))

    out_ref[...] = total_ref[side // lane : side // lane + slabs, side : side + height]


def density(sweep, reach, offsets, probe, tile):
    side = probe.shape[1]
    extra = side if reach else 0
    height, slabs = tile[0] + extra, (tile[1] + extra) // lane
    return pl.pallas_call(
        functools.partial(density_kernel, sweep, reach),
        out_shape=shape_of(slabs, height, lane),
        in_specs=[offsets_spec()] + whole_spec(1),
        out_specs=whole_spec(1)[0],
        scratch_shapes=[VMEM((slabs + 2 * side // lane, height + 2 * side, lane), jnp.float32)],
        compiler_params=pltpu.CompilerParams(vmem_limit_bytes=10 * MIB),
        cost_estimate=cost(1_000_000, 6 * MIB),
        name="density",
    )(offsets, probe)


def gather_kernel(sweep, below_of, offsets_ref, total_ref, windows_ref, all_ref, *refs):
    edge_refs, strip_ref = refs[:-1], refs[-1]
    slabs, side = all_ref.shape[1:3]
    height = total_ref.shape[2]
    edge = side // lane
    below = below_of()
    strip_ref[...] = jnp.zeros_like(strip_ref)
    for scan in range(2):
        row, column = corner_of(offsets_ref, 2 * below - 1, -1, sweep, scan)
        row += (2 * below - 1) * side
        first, shift = split_column(column)

        @pl.when((row > 0) & (row < 2 * side))
        def _():
            for plane in range(2):
                add_slabs(strip_ref, (plane,), row, first, turned(windows_ref[scan, plane], shift))

    base = pl.multiple_of(below * (height - side), 8)
    for plane in range(2):
        for k in range(slabs):
            value = strip_ref[plane, k, side : 2 * side] + total_ref[plane, k, pl.ds(base, side)]
            all_ref[plane, k] = value
            if k >= slabs - edge:
                edge_refs[0][plane, k - (slabs - edge)] = value
            elif k < edge and len(edge_refs) > 1:
                edge_refs[1][plane, k] = value


def partner_below():
    return 1 - lax.rem(lax.axis_index("row"), 2)


def other_below():
    return lax.rem(lax.axis_index("row"), 2)


def never_below():
    return jnp.int32(0)


def gather(sweep, below_of, offsets, total, windows, sides):
    side = windows.shape[2]
    slabs = total.shape[1]
    return pl.pallas_call(
        functools.partial(gather_kernel, sweep, below_of),
        out_shape=[shape_of(2, slabs, side, lane)] + [shape_of(2, side // lane, side, lane)] * sides,
        in_specs=[offsets_spec()] + whole_spec(2),
        out_specs=whole_spec(1 + sides),
        scratch_shapes=[VMEM((2, slabs, 3 * side, lane), jnp.float32)],
        compiler_params=pltpu.CompilerParams(vmem_limit_bytes=8 * MIB),
        cost_estimate=cost(1_000_000, 6 * MIB),
        name="gather",
    )(offsets, total, windows)


def widen_kernel(*refs):
    own_ref, right_ref, first_ref, second_ref, corner_ref, density_ref, total_ref = refs[:7]
    near_ref, far_ref, left_refs, right_refs, out_ref = refs[7], refs[8], refs[9:12], refs[12:15], refs[15]
    side = near_ref.shape[2]
    edge = side // lane
    slabs = out_ref.shape[1] - edge
    rows = out_ref.shape[2] - side
    odd = lax.rem(lax.axis_index("row"), 2) == 1
    for k in range(slabs + edge):
        for top, bottom in ((0, side), (side, rows), (rows, rows + side)):
            part = 1.0 / (density_ref[k, top:bottom] + object_damping)
            for plane in range(2):
                if top == rows:
                    if k < edge:
                        before = first_ref[plane, :, columns(k)]
                    elif k < slabs:
                        before = second_ref[plane, :, columns(k - edge)]
                    else:
                        before = corner_ref[plane, :, columns(k - slabs)]
                elif k < slabs:
                    before = own_ref[plane, top:bottom, columns(k)]
                else:
                    before = right_ref[plane, top:bottom, columns(k - slabs)]

                def picked(number, refs_of, at):
                    if top == side:
                        return refs_of[0][plane, at]
                    near, far = refs_of[1][plane, at], refs_of[2][plane, at]
                    return jnp.where(odd, near, far) if top == 0 else jnp.where(odd, far, near)

                if top == side:
                    terms = total_ref[plane, k, top:bottom]
                else:
                    terms = picked(0, (None, near_ref, far_ref), k)
                if k < edge:
                    terms += picked(0, left_refs, k)
                if k >= slabs:
                    terms += picked(0, right_refs, k - slabs)
                out_ref[plane, k, top:bottom] = before + terms * part


def widen(pieces, dense, total, near, far, left, right):
    return pl.pallas_call(
        widen_kernel,
        out_shape=shape_of(*total.shape),
        in_specs=whole_spec(15),
        out_specs=whole_spec(1)[0],
        compiler_params=pltpu.CompilerParams(vmem_limit_bytes=6 * MIB),
        cost_estimate=cost(4_000_000, 20 * MIB),
        name="widen",
    )(*pieces, dense, total, near, far, *left, *right)


def renew_kernel(field_ref, density_ref, total_ref, top_ref, left_top_ref, left_rest_ref, out_ref):
    slabs, rows = density_ref.shape[:2]
    edge, side = left_top_ref.shape[1:3]
    for k in range(slabs):
        part = 1.0 / (density_ref[k] + object_damping)
        for plane in range(2):
            top = top_ref[plane, k]
            rest = total_ref[plane, k, side:rows]
            if k < edge:
                top += left_top_ref[plane, k]
                rest += left_rest_ref[plane, k]
            out_ref[plane, :side, columns(k)] = field_ref[plane, k, :side] + top * part[:side]
            out_ref[plane, side:, columns(k)] = field_ref[plane, k, side:rows] + rest * part[side:]


def renew(field, dense, total, top, left_top, left_rest):
    slabs, rows = dense.shape[:2]
    return pl.pallas_call(
        renew_kernel,
        out_shape=shape_of(2, rows, slabs * lane),
        in_specs=whole_spec(6),
        out_specs=whole_spec(1)[0],
        compiler_params=pltpu.CompilerParams(vmem_limit_bytes=4 * MIB),
        cost_estimate=cost(4_000_000, 10 * MIB),
        name="renew",
    )(field, dense, total, top, left_top, left_rest)


def fold_kernel(bit, value_ref, came_ref, kept_ref, sent_ref, total_ref):
    total_ref[...] = value_ref[...] + came_ref[...]
    kept, sent = halves_of(bit, kept_ref.shape[0])
    kept_ref[...] = total_ref[kept]
    sent_ref[...] = total_ref[sent]


def fold(bit, value, came):
    rows, side = value.shape
    return pl.pallas_call(
        functools.partial(fold_kernel, bit),
        out_shape=[shape_of(rows // 2, side)] * 2,
        in_specs=whole_spec(2),
        out_specs=whole_spec(2),
        scratch_shapes=[VMEM(value.shape, jnp.float32)],
        compiler_params=pltpu.CompilerParams(vmem_limit_bytes=4 * MIB),
        cost_estimate=cost(100_000, MIB),
        name="fold",
    )(value, came)


def join_kernel(bit, value_ref, other_ref, out_ref):
    kept, sent = halves_of(bit, value_ref.shape[0])
    out_ref[kept] = value_ref[...]
    out_ref[sent] = other_ref[...]


def join(bit, value, other):
    rows, side = value.shape
    return pl.pallas_call(
        functools.partial(join_kernel, bit),
        out_shape=shape_of(2 * rows, side),
        in_specs=whole_spec(2),
        out_specs=whole_spec(1)[0],
        compiler_params=pltpu.CompilerParams(vmem_limit_bytes=4 * MIB),
        cost_estimate=cost(100_000, MIB),
        name="join",
    )(value, other)


def illuminate_kernel(value_ref, other_ref, probe_ref, out_ref, total_ref):
    kept, sent = halves_of(0, value_ref.shape[0])
    total_ref[kept] = value_ref[...]
    total_ref[sent] = other_ref[...]
    side = probe_ref.shape[1]
    part = 1.0 / (total_ref[2 * side :] + probe_damping)
    out_ref[0] = probe_ref[0] + total_ref[:side] * part
    out_ref[1] = probe_ref[1] + total_ref[side : 2 * side] * part


def illuminate(value, other, probe):
    rows, side = value.shape
    return pl.pallas_call(
        illuminate_kernel,
        out_shape=shape_of(*probe.shape),
        in_specs=whole_spec(3),
        out_specs=whole_spec(1)[0],
        scratch_shapes=[VMEM((2 * rows, side), jnp.float32)],
        compiler_params=pltpu.CompilerParams(vmem_limit_bytes=6 * MIB),
        cost_estimate=cost(1_000_000, 2 * MIB),
        name="illuminate",
    )(value, other, probe)


def tied(*values):
    return lax.optimization_barrier(values)


def local(table, object_field, probe, amplitudes, offsets):
    side = probe.shape[1]
    tile = object_field.shape[1:]
    measured = reorder(amplitudes[0, 0])
    col_bits = int(math.log2(lax.axis_size("col")))
    row_bits = int(math.log2(lax.axis_size("row")))

    strip, rest = tied(object_field[:, :side, :side], object_field)
    first = shifted(strip, "row", -1)
    second = shifted(rest[:, :side, side:], "row", -1)
    right = shifted(object_field[:, :, :side], "col", -1)
    near = jnp.concatenate([shifted(offsets, "row", 1), offsets, shifted(offsets, "row", -1)], axis=0)
    first, near = tied(first, near)
    corner = shifted(first, "col", -1)
    pieces = (object_field, right, first, second, corner)

    kept, sent, own = scan_step(0, False, offsets, probe, measured, table, *pieces)
    total, middle_right, middle_left = place(0, offsets, own, tile, 2)
    around = jnp.concatenate([shifted(near, "col", 1), near, shifted(near, "col", -1)], axis=1)
    dense = density(0, True, around, probe, tile)
    partner = swapped(own, "row", 1)
    came = swapped(sent, "col", 1)
    for bit in range(1, col_bits):
        kept, sent = fold(bit, kept, came)
        came = swapped(sent, "col", 1 << bit)
    came, middle_left, middle_right, around = tied(came, middle_left, middle_right, around)
    sums = kept + came
    right_strips = [shifted(middle_left, "col", -1)]
    left_strips = [shifted(middle_right, "col", 1)]
    for bit in reversed(range(1, row_bits)):
        came = swapped(sums, "row", 1 << bit)
        if bit == row_bits - 1:
            came, dense = tied(came, dense)
        sums = sums + came
    sums, partner, left_strips[0], right_strips[0] = tied(
        sums, partner, left_strips[0], right_strips[0]
    )
    passed = handed_on(partner, "row")
    near_all, near_right, near_left = gather(0, partner_below, near, total, partner, 2)
    right_strips.append(shifted(near_left, "col", -1))
    left_strips.append(shifted(near_right, "col", 1))
    sums = sums + swapped(sums, "row", 1)
    for bit in reversed(range(1, col_bits)):
        sums = join(bit, sums, swapped(sums, "col", 1 << bit))
    probe = illuminate(sums, swapped(sums, "col", 1), probe)
    passed, probe, left_strips[1], right_strips[1] = tied(passed, probe, left_strips[1], right_strips[1])
    far_all, far_right, far_left = gather(0, other_below, near, total, passed, 2)
    right_strips.append(shifted(far_left, "col", -1))
    left_strips.append(shifted(far_right, "col", 1))
    field = widen(pieces, dense, total, near_all, far_all, left_strips, right_strips)

    kept, sent, own = scan_step(1, True, offsets, probe, measured, table, field)
    total, middle_right = place(1, offsets, own, tile, 1)
    dense = density(1, False, around, probe, tile)
    upper = shifted(own, "row", 1)
    came = swapped(sent, "col", 1)
    for bit in range(1, col_bits):
        kept, sent = fold(bit, kept, came)
        came = swapped(sent, "col", 1 << bit)
    came, middle_right, dense = tied(came, middle_right, dense)
    sums = kept + came
    left_rest = shifted(middle_right, "col", 1)
    sums, upper, left_rest = tied(sums, upper, left_rest)
    top, right_top = gather(1, never_below, near, total, upper, 1)
    left_top = shifted(right_top, "col", 1)
    for bit in range(row_bits):
        sums = sums + swapped(sums, "row", 1 << bit)
    sums, left_top = tied(sums, left_top)
    for bit in reversed(range(1, col_bits)):
        sums = join(bit, sums, swapped(sums, "col", 1 << bit))
    other = swapped(sums, "col", 1)
    return renew(field, dense, total, top, left_top, left_rest), illuminate(sums, other, probe)


def solution(mesh):
    placed = (
        P(None, "row", "col"),
        P(),
        P("row", "col", None, None, None, None),
        P("row", "col", None, None, None),
    )

    def whole(object_field, probe, amplitudes, offsets):
        table = jnp.asarray(dft_tables(probe.shape[1]))
        body = jax.shard_map(
            local,
            mesh=mesh,
            in_specs=(P(),) + placed,
            out_specs=(P(None, "row", "col"), P()),
            check_vma=False,
        )
        return body(table, object_field, probe, amplitudes, offsets)

    return whole
```

```python
import functools
import math

import jax
import jax.numpy as jnp
import ml_dtypes
import numpy as np
from jax import lax
from jax.experimental import pallas as pl
from jax.experimental.pallas import tpu as pltpu
from jax.sharding import PartitionSpec as P

softening = 0.1
object_damping = 0.5
probe_damping = 1.0
MIB = 1 << 20
lane = 128
SCAN_LIMIT = 24 * MIB
VMEM = pltpu.VMEM
SMEM = pltpu.SMEM


def shifted(array, axis, by):
    peers = lax.axis_size(axis)
    return lax.ppermute(array, axis, [(i, (i + by) % peers) for i in range(peers)])


def swapped(array, axis, mask):
    peers = lax.axis_size(axis)
    return lax.ppermute(array, axis, [(i, i ^ mask) for i in range(peers)])


def handed_on(array, axis):
    peers = lax.axis_size(axis)
    return lax.ppermute(array, axis, [(i, (i + 2 - 4 * (i % 2)) % peers) for i in range(peers)])


def dft_tables(length):
    half = length // 2
    index = np.arange(half)
    parts = []
    for odd in range(2):
        phase = ((2 * index[:, None] + odd) * index[None, :] % length) * (2.0 * math.pi / length)
        real, imag = np.cos(phase) / math.sqrt(length), -np.sin(phase) / math.sqrt(length)
        full = np.block([[real, -imag], [imag, real]])
        for value in (full, full.T):
            high = value.astype(ml_dtypes.bfloat16)
            parts += [high, (value - high.astype(np.float64)).astype(ml_dtypes.bfloat16)]
    return np.stack(parts)


def halves(value):
    high = value.astype(jnp.bfloat16)
    return high, (value - high.astype(jnp.float32)).astype(jnp.bfloat16)


def product(a, b):
    return jnp.dot(a, b, preferred_element_type=jnp.float32)


def left_product(table_ref, number, data):
    top, rest = halves(data)
    high, low = table_ref[2 * number], table_ref[2 * number + 1]
    return product(high, top) + product(high, rest) + product(low, top)


def right_product(data, table_ref, number):
    top, rest = halves(data)
    high, low = table_ref[2 * number], table_ref[2 * number + 1]
    return product(top, high) + product(rest, high) + product(top, low)


def stacked(values, axis):
    return jnp.concatenate(values, axis=axis)


def forward(table_ref, real, imag):
    half = real.shape[0] // 2
    even = stacked([real[:half] + real[half:], imag[:half] + imag[half:]], 0)
    odd = stacked([real[:half] - real[half:], imag[:half] - imag[half:]], 0)
    even, odd = left_product(table_ref, 0, even), left_product(table_ref, 2, odd)
    real, imag = stacked([even[:half], odd[:half]], 0), stacked([even[half:], odd[half:]], 0)
    even = stacked([real[:, :half] + real[:, half:], imag[:, :half] + imag[:, half:]], 1)
    odd = stacked([real[:, :half] - real[:, half:], imag[:, :half] - imag[:, half:]], 1)
    even, odd = right_product(even, table_ref, 1), right_product(odd, table_ref, 3)
    return stacked([even[:, :half], odd[:, :half]], 1), stacked([even[:, half:], odd[:, half:]], 1)


def backward(table_ref, real, imag):
    half = real.shape[0] // 2
    even = left_product(table_ref, 1, stacked([real[:half], imag[:half]], 0))
    odd = left_product(table_ref, 3, stacked([real[half:], imag[half:]], 0))
    one, two = even + odd, even - odd
    real, imag = stacked([one[:half], two[:half]], 0), stacked([one[half:], two[half:]], 0)
    even = right_product(stacked([real[:, :half], imag[:, :half]], 1), table_ref, 0)
    odd = right_product(stacked([real[:, half:], imag[:, half:]], 1), table_ref, 2)
    one, two = even + odd, even - odd
    return stacked([one[:, :half], two[:, :half]], 1), stacked([one[:, half:], two[:, half:]], 1)


def reorder_kernel(amplitude_ref, out_ref):
    side = amplitude_ref.shape[3]
    half = side // 2

    def choice(axis):
        target = lax.broadcasted_iota(jnp.int32, (side, side), axis)
        source = lax.broadcasted_iota(jnp.int32, (side, side), 1 - axis)
        wanted = jnp.where(target < half, 2 * target, 2 * (target - half) + 1)
        return jnp.where(source == wanted, 1.0, 0.0).astype(jnp.bfloat16)

    rows, cols = choice(0), choice(1)
    for sweep in range(amplitude_ref.shape[0]):
        for scan in range(amplitude_ref.shape[1]):
            moved = product(rows, amplitude_ref[sweep, scan]).astype(jnp.bfloat16)
            out_ref[sweep, scan] = product(moved, cols).astype(jnp.bfloat16)


def reorder(amplitudes):
    return pl.pallas_call(
        reorder_kernel,
        out_shape=jax.ShapeDtypeStruct(amplitudes.shape, amplitudes.dtype),
        in_specs=[pl.BlockSpec(memory_space=VMEM)],
        out_specs=pl.BlockSpec(memory_space=VMEM),
        compiler_params=pltpu.CompilerParams(vmem_limit_bytes=8 * MIB),
        cost_estimate=pl.CostEstimate(flops=300_000_000, bytes_accessed=MIB, transcendentals=0),
        name="reorder",
    )(amplitudes)


def split_column(column):
    return lax.div(column, lane), lax.rem(column, lane)


def taken(ref, plane, row, column, side):
    first, shift = split_column(column)
    count = side // lane + 1
    slabs = [ref[plane, first + k, pl.ds(row, side), :] for k in range(count)]
    return pltpu.roll(jnp.concatenate(slabs, axis=1), count * lane - shift, 1)[:, :side]


def turned(value, shift):
    side = value.shape[0]
    wide = jnp.concatenate([value, jnp.zeros((side, lane), jnp.float32)], axis=1)
    return pltpu.roll(wide, shift, 1)


def add_slabs(ref, lead, row, first, wide):
    side = wide.shape[0]
    for k in range(wide.shape[1] // lane):
        spot = lead + (first + k, pl.ds(row, side), slice(None))
        ref[spot] += wide[:, k * lane : (k + 1) * lane]


def columns(number):
    return slice(number * lane, (number + 1) * lane)


def whole_spec(count):
    return [pl.BlockSpec(memory_space=VMEM)] * count


def offsets_spec():
    return pl.BlockSpec(memory_space=SMEM)


def shape_of(*dims):
    return jax.ShapeDtypeStruct(dims, jnp.float32)


def cost(flops, moved):
    return pl.CostEstimate(flops=flops, bytes_accessed=moved, transcendentals=0)


def corner_of(offsets_ref, down, along, sweep, scan):
    spot = (down + 1, along + 1, sweep, scan)
    return offsets_ref[spot + (0,)], offsets_ref[spot + (1,)]


def halves_of(bit, half):
    mine = lax.rem(lax.axis_index("col") >> bit, 2)
    kept = pl.ds(pl.multiple_of(mine * half, 8), half)
    return kept, pl.ds(pl.multiple_of((1 - mine) * half, 8), half)


def scan_kernel(sweep, last, counts, offsets_ref, *refs):
    inputs, outputs, scratch = counts
    probe_hbm, amplitude_hbm, table_hbm = refs[:3]
    field_in = refs[3:inputs]
    outs_hbm = refs[inputs : inputs + outputs]
    rest = refs[inputs + outputs :]
    probe_ref, amplitude_ref, table_ref, sums_ref, windows_ref = rest[:5]
    small_sem, field_sem, out_sem = rest[5:8]
    side = probe_ref.shape[1]
    copies = []

    def fetch(source, target):
        copies.append(pltpu.make_async_copy(source, target, field_sem))

    small = [
        pltpu.make_async_copy(table_hbm, table_ref, small_sem.at[0]),
        pltpu.make_async_copy(probe_hbm, probe_ref, small_sem.at[1]),
        pltpu.make_async_copy(amplitude_hbm.at[sweep], amplitude_ref, small_sem.at[2]),
    ]
    if last:
        field_ref = field_in[0]
    else:
        own_hbm, right_hbm, first_hbm, second_hbm, corner_hbm = field_in
        field_ref = rest[8]
        rows, edge = own_hbm.shape[1], side // lane
        slabs = own_hbm.shape[2] // lane
        for k in range(slabs):
            fetch(own_hbm.at[:, :, columns(k)], field_ref.at[:, k, :rows])
        for k in range(edge):
            fetch(right_hbm.at[:, :, columns(k)], field_ref.at[:, slabs + k, :rows])
            fetch(first_hbm.at[:, :, columns(k)], field_ref.at[:, k, rows:])
            fetch(corner_hbm.at[:, :, columns(k)], field_ref.at[:, slabs + k, rows:])
        for k in range(edge, slabs):
            fetch(second_hbm.at[:, :, columns(k - edge)], field_ref.at[:, k, rows:])
    small[0].start()
    for copy in copies:
        copy.start()
    for copy in small[1:]:
        copy.start()
    small[0].wait()
    for copy in small[1:]:
        copy.wait()
    for copy in copies:
        copy.wait()
    probe_real, probe_imag = probe_ref[0], probe_ref[1]
    pending = []
    for scan in range(2):
        row, column = offsets_ref[0, 0, sweep, scan, 0], offsets_ref[0, 0, sweep, scan, 1]
        patch_real = taken(field_ref, 0, row, column, side)
        patch_imag = taken(field_ref, 1, row, column, side)
        wave_real = probe_real * patch_real - probe_imag * patch_imag
        wave_imag = probe_real * patch_imag + probe_imag * patch_real
        far_real, far_imag = forward(table_ref, wave_real, wave_imag)
        scale = amplitude_ref[scan].astype(jnp.float32) * lax.rsqrt(
            far_real * far_real + far_imag * far_imag + softening
        )
        back_real, back_imag = backward(table_ref, far_real * scale, far_imag * scale)
        diff_real = back_real - wave_real
        diff_imag = back_imag - wave_imag
        term_real = probe_real * diff_real + probe_imag * diff_imag
        term_imag = probe_real * diff_imag - probe_imag * diff_real
        windows_ref[scan, 0] = term_real
        windows_ref[scan, 1] = term_imag
        copy = pltpu.make_async_copy(windows_ref.at[scan], outs_hbm[2].at[scan], out_sem)
        copy.start()
        pending.append(copy)
        sums = (
            patch_real * diff_real + patch_imag * diff_imag,
            patch_real * diff_imag - patch_imag * diff_real,
            patch_real * patch_real + patch_imag * patch_imag,
        )
        for number, value in enumerate(sums):
            spot = slice(number * side, (number + 1) * side)
            if scan == 0:
                sums_ref[spot] = value
            else:
                sums_ref[spot] += value
    kept, sent = halves_of(0, outs_hbm[0].shape[0])
    outs = [(sums_ref.at[sent], outs_hbm[1]), (sums_ref.at[kept], outs_hbm[0])]
    outs = [pltpu.make_async_copy(source, target, out_sem) for source, target in outs]
    for copy in outs:
        copy.start()
    for copy in pending + outs:
        copy.wait()


def scan_step(sweep, last, offsets, probe, amplitudes, table, *field):
    side = probe.shape[1]
    shapes = [shape_of(3 * side // 2, side)] * 2 + [shape_of(2, 2, side, side)]
    scratch = [
        VMEM(probe.shape, jnp.float32),
        VMEM(amplitudes.shape[1:], amplitudes.dtype),
        VMEM(table.shape, table.dtype),
        VMEM((3 * side, side), jnp.float32),
        VMEM((2, 2, side, side), jnp.float32),
        pltpu.SemaphoreType.DMA((3,)),
        pltpu.SemaphoreType.DMA,
        pltpu.SemaphoreType.DMA,
    ]
    if not last:
        rows, cols = field[0].shape[1:]
        scratch.append(VMEM((2, (cols + side) // lane, rows + side, lane), jnp.float32))
    anywhere = pl.BlockSpec(memory_space=pl.ANY)
    counts = (3 + len(field), len(shapes), len(scratch))
    return pl.pallas_call(
        functools.partial(scan_kernel, sweep, last, counts),
        out_shape=shapes,
        in_specs=[offsets_spec()] + [anywhere] * 3 + (whole_spec(1) if last else [anywhere] * len(field)),
        out_specs=[anywhere] * len(shapes),
        scratch_shapes=scratch,
        compiler_params=pltpu.CompilerParams(vmem_limit_bytes=SCAN_LIMIT),
        cost_estimate=cost(7_000_000_000, 12 * MIB),
        name="scan",
    )(offsets, probe, amplitudes, table, *field)


def place_kernel(sweep, offsets_ref, windows_ref, total_ref, *edge_refs):
    side = windows_ref.shape[2]
    edge = side // lane
    slabs, height = total_ref.shape[1:3]
    total_ref[...] = jnp.zeros_like(total_ref)
    for scan in range(2):
        row, column = offsets_ref[0, 0, sweep, scan, 0], offsets_ref[0, 0, sweep, scan, 1]
        first, shift = split_column(column)
        for plane in range(2):
            add_slabs(total_ref, (plane,), row, first, turned(windows_ref[scan, plane], shift))
    for ref, start in zip(edge_refs, (slabs - edge, 0)):
        ref[...] = total_ref[:, start : start + edge, side : height - side]


def place(sweep, offsets, windows, tile, sides):
    side = windows.shape[2]
    edge = side // lane
    height, slabs = tile[0] + side, tile[1] // lane + edge
    shapes = [shape_of(2, slabs, height, lane)] + [shape_of(2, edge, height - 2 * side, lane)] * sides
    return pl.pallas_call(
        functools.partial(place_kernel, sweep),
        out_shape=shapes,
        in_specs=[offsets_spec()] + whole_spec(1),
        out_specs=whole_spec(len(shapes)),
        compiler_params=pltpu.CompilerParams(vmem_limit_bytes=4 * MIB),
        cost_estimate=cost(1_000_000, 6 * MIB),
        name="place",
    )(offsets, windows)


def density_kernel(sweep, reach, offsets_ref, probe_ref, out_ref, total_ref):
    side = probe_ref.shape[1]
    slabs, height = out_ref.shape[:2]
    breadth = slabs * lane
    tile = height - side if reach else height
    span = breadth - side if reach else breadth
    total_ref[...] = jnp.zeros_like(total_ref)
    power = probe_ref[0] * probe_ref[0] + probe_ref[1] * probe_ref[1]
    steps = (-1, 0, 1) if reach else (-1, 0)
    for down in steps:
        for along in steps:
            for scan in range(2):
                row, column = corner_of(offsets_ref, down, along, sweep, scan)
                row += side + down * tile
                column += side + along * span

                @pl.when((row > 0) & (row < side + height) & (column > 0) & (column < side + breadth))
                def _():
                    first, shift = split_column(column)
                    add_slabs(total_ref, (), row, first, turned(power, shift))

    out_ref[...] = total_ref[side // lane : side // lane + slabs, side : side + height]


def density(sweep, reach, offsets, probe, tile):
    side = probe.shape[1]
    extra = side if reach else 0
    height, slabs = tile[0] + extra, (tile[1] + extra) // lane
    return pl.pallas_call(
        functools.partial(density_kernel, sweep, reach),
        out_shape=shape_of(slabs, height, lane),
        in_specs=[offsets_spec()] + whole_spec(1),
        out_specs=whole_spec(1)[0],
        scratch_shapes=[VMEM((slabs + 2 * side // lane, height + 2 * side, lane), jnp.float32)],
        compiler_params=pltpu.CompilerParams(vmem_limit_bytes=10 * MIB),
        cost_estimate=cost(1_000_000, 6 * MIB),
        name="density",
    )(offsets, probe)


def gather_kernel(sweep, below_of, offsets_ref, total_ref, windows_ref, all_ref, *refs):
    edge_refs, strip_ref = refs[:-1], refs[-1]
    slabs, side = all_ref.shape[1:3]
    height = total_ref.shape[2]
    edge = side // lane
    below = below_of()
    strip_ref[...] = jnp.zeros_like(strip_ref)
    for scan in range(2):
        row, column = corner_of(offsets_ref, 2 * below - 1, -1, sweep, scan)
        row += (2 * below - 1) * side
        first, shift = split_column(column)

        @pl.when((row > 0) & (row < 2 * side))
        def _():
            for plane in range(2):
                add_slabs(strip_ref, (plane,), row, first, turned(windows_ref[scan, plane], shift))

    base = pl.multiple_of(below * (height - side), 8)
    for plane in range(2):
        for k in range(slabs):
            value = strip_ref[plane, k, side : 2 * side] + total_ref[plane, k, pl.ds(base, side)]
            all_ref[plane, k] = value
            if k >= slabs - edge:
                edge_refs[0][plane, k - (slabs - edge)] = value
            elif k < edge and len(edge_refs) > 1:
                edge_refs[1][plane, k] = value


def partner_below():
    return 1 - lax.rem(lax.axis_index("row"), 2)


def other_below():
    return lax.rem(lax.axis_index("row"), 2)


def never_below():
    return jnp.int32(0)


def gather(sweep, below_of, offsets, total, windows, sides):
    side = windows.shape[2]
    slabs = total.shape[1]
    return pl.pallas_call(
        functools.partial(gather_kernel, sweep, below_of),
        out_shape=[shape_of(2, slabs, side, lane)] + [shape_of(2, side // lane, side, lane)] * sides,
        in_specs=[offsets_spec()] + whole_spec(2),
        out_specs=whole_spec(1 + sides),
        scratch_shapes=[VMEM((2, slabs, 3 * side, lane), jnp.float32)],
        compiler_params=pltpu.CompilerParams(vmem_limit_bytes=8 * MIB),
        cost_estimate=cost(1_000_000, 6 * MIB),
        name="gather",
    )(offsets, total, windows)


def widen_kernel(*refs):
    own_ref, right_ref, first_ref, second_ref, corner_ref, density_ref, total_ref = refs[:7]
    near_ref, far_ref, left_refs, right_refs, out_ref = refs[7], refs[8], refs[9:12], refs[12:15], refs[15]
    side = near_ref.shape[2]
    edge = side // lane
    slabs = out_ref.shape[1] - edge
    rows = out_ref.shape[2] - side
    odd = lax.rem(lax.axis_index("row"), 2) == 1
    for k in range(slabs + edge):
        for top, bottom in ((0, side), (side, rows), (rows, rows + side)):
            part = 1.0 / (density_ref[k, top:bottom] + object_damping)
            for plane in range(2):
                if top == rows:
                    if k < edge:
                        before = first_ref[plane, :, columns(k)]
                    elif k < slabs:
                        before = second_ref[plane, :, columns(k - edge)]
                    else:
                        before = corner_ref[plane, :, columns(k - slabs)]
                elif k < slabs:
                    before = own_ref[plane, top:bottom, columns(k)]
                else:
                    before = right_ref[plane, top:bottom, columns(k - slabs)]

                def picked(number, refs_of, at):
                    if top == side:
                        return refs_of[0][plane, at]
                    near, far = refs_of[1][plane, at], refs_of[2][plane, at]
                    return jnp.where(odd, near, far) if top == 0 else jnp.where(odd, far, near)

                if top == side:
                    terms = total_ref[plane, k, top:bottom]
                else:
                    terms = picked(0, (None, near_ref, far_ref), k)
                if k < edge:
                    terms += picked(0, left_refs, k)
                if k >= slabs:
                    terms += picked(0, right_refs, k - slabs)
                out_ref[plane, k, top:bottom] = before + terms * part


def widen(pieces, dense, total, near, far, left, right):
    return pl.pallas_call(
        widen_kernel,
        out_shape=shape_of(*total.shape),
        in_specs=whole_spec(15),
        out_specs=whole_spec(1)[0],
        compiler_params=pltpu.CompilerParams(vmem_limit_bytes=6 * MIB),
        cost_estimate=cost(4_000_000, 20 * MIB),
        name="widen",
    )(*pieces, dense, total, near, far, *left, *right)


def renew_kernel(field_ref, density_ref, total_ref, top_ref, left_top_ref, left_rest_ref, out_ref):
    slabs, rows = density_ref.shape[:2]
    edge, side = left_top_ref.shape[1:3]
    for k in range(slabs):
        part = 1.0 / (density_ref[k] + object_damping)
        for plane in range(2):
            top = top_ref[plane, k]
            rest = total_ref[plane, k, side:rows]
            if k < edge:
                top += left_top_ref[plane, k]
                rest += left_rest_ref[plane, k]
            out_ref[plane, :side, columns(k)] = field_ref[plane, k, :side] + top * part[:side]
            out_ref[plane, side:, columns(k)] = field_ref[plane, k, side:rows] + rest * part[side:]


def renew(field, dense, total, top, left_top, left_rest):
    slabs, rows = dense.shape[:2]
    return pl.pallas_call(
        renew_kernel,
        out_shape=shape_of(2, rows, slabs * lane),
        in_specs=whole_spec(6),
        out_specs=whole_spec(1)[0],
        compiler_params=pltpu.CompilerParams(vmem_limit_bytes=4 * MIB),
        cost_estimate=cost(4_000_000, 10 * MIB),
        name="renew",
    )(field, dense, total, top, left_top, left_rest)


def fold_kernel(bit, value_ref, came_ref, kept_ref, sent_ref, total_ref):
    total_ref[...] = value_ref[...] + came_ref[...]
    kept, sent = halves_of(bit, kept_ref.shape[0])
    kept_ref[...] = total_ref[kept]
    sent_ref[...] = total_ref[sent]


def fold(bit, value, came):
    rows, side = value.shape
    return pl.pallas_call(
        functools.partial(fold_kernel, bit),
        out_shape=[shape_of(rows // 2, side)] * 2,
        in_specs=whole_spec(2),
        out_specs=whole_spec(2),
        scratch_shapes=[VMEM(value.shape, jnp.float32)],
        compiler_params=pltpu.CompilerParams(vmem_limit_bytes=4 * MIB),
        cost_estimate=cost(100_000, MIB),
        name="fold",
    )(value, came)


def join_kernel(bit, value_ref, other_ref, out_ref):
    kept, sent = halves_of(bit, value_ref.shape[0])
    out_ref[kept] = value_ref[...]
    out_ref[sent] = other_ref[...]


def join(bit, value, other):
    rows, side = value.shape
    return pl.pallas_call(
        functools.partial(join_kernel, bit),
        out_shape=shape_of(2 * rows, side),
        in_specs=whole_spec(2),
        out_specs=whole_spec(1)[0],
        compiler_params=pltpu.CompilerParams(vmem_limit_bytes=4 * MIB),
        cost_estimate=cost(100_000, MIB),
        name="join",
    )(value, other)


def illuminate_kernel(value_ref, other_ref, probe_ref, out_ref, total_ref):
    kept, sent = halves_of(0, value_ref.shape[0])
    total_ref[kept] = value_ref[...]
    total_ref[sent] = other_ref[...]
    side = probe_ref.shape[1]
    part = 1.0 / (total_ref[2 * side :] + probe_damping)
    out_ref[0] = probe_ref[0] + total_ref[:side] * part
    out_ref[1] = probe_ref[1] + total_ref[side : 2 * side] * part


def illuminate(value, other, probe):
    rows, side = value.shape
    return pl.pallas_call(
        illuminate_kernel,
        out_shape=shape_of(*probe.shape),
        in_specs=whole_spec(3),
        out_specs=whole_spec(1)[0],
        scratch_shapes=[VMEM((2 * rows, side), jnp.float32)],
        compiler_params=pltpu.CompilerParams(vmem_limit_bytes=6 * MIB),
        cost_estimate=cost(1_000_000, 2 * MIB),
        name="illuminate",
    )(value, other, probe)


def tied(*values):
    return lax.optimization_barrier(values)


def local(table, object_field, probe, amplitudes, offsets):
    side = probe.shape[1]
    tile = object_field.shape[1:]
    measured = reorder(amplitudes[0, 0])
    col_bits = int(math.log2(lax.axis_size("col")))
    row_bits = int(math.log2(lax.axis_size("row")))

    strip, rest = tied(object_field[:, :side, :side], object_field)
    first = shifted(strip, "row", -1)
    second = shifted(rest[:, :side, side:], "row", -1)
    right = shifted(object_field[:, :, :side], "col", -1)
    near = jnp.concatenate([shifted(offsets, "row", 1), offsets, shifted(offsets, "row", -1)], axis=0)
    first, near = tied(first, near)
    corner = shifted(first, "col", -1)
    pieces = (object_field, right, first, second, corner)

    kept, sent, own = scan_step(0, False, offsets, probe, measured, table, *pieces)
    total, middle_right, middle_left = place(0, offsets, own, tile, 2)
    around = jnp.concatenate([shifted(near, "col", 1), near, shifted(near, "col", -1)], axis=1)
    dense = density(0, True, around, probe, tile)
    partner = swapped(own, "row", 1)
    came = swapped(sent, "col", 1)
    for bit in range(1, col_bits):
        kept, sent = fold(bit, kept, came)
        came = swapped(sent, "col", 1 << bit)
    came, around = tied(came, around)
    sums = kept + came
    for bit in reversed(range(1, row_bits)):
        came = swapped(sums, "row", 1 << bit)
        if bit == row_bits - 1:
            came, dense, middle_left, middle_right = tied(came, dense, middle_left, middle_right)
        sums = sums + came
    right_strips = [shifted(middle_left, "col", -1)]
    left_strips = [shifted(middle_right, "col", 1)]
    sums, partner = tied(sums, partner)
    passed = handed_on(partner, "row")
    near_all, near_right, near_left = gather(0, partner_below, near, total, partner, 2)
    right_strips.append(shifted(near_left, "col", -1))
    left_strips.append(shifted(near_right, "col", 1))
    sums = sums + swapped(sums, "row", 1)
    for bit in reversed(range(1, col_bits)):
        other = swapped(sums, "col", 1 << bit)
        if bit == col_bits - 1:
            other, left_strips[0], right_strips[0] = tied(other, left_strips[0], right_strips[0])
        sums = join(bit, sums, other)
    probe = illuminate(sums, swapped(sums, "col", 1), probe)
    passed, probe, left_strips[1], right_strips[1] = tied(passed, probe, left_strips[1], right_strips[1])
    far_all, far_right, far_left = gather(0, other_below, near, total, passed, 2)
    right_strips.append(shifted(far_left, "col", -1))
    left_strips.append(shifted(far_right, "col", 1))
    field = widen(pieces, dense, total, near_all, far_all, left_strips, right_strips)

    kept, sent, own = scan_step(1, True, offsets, probe, measured, table, field)
    total, middle_right = place(1, offsets, own, tile, 1)
    dense = density(1, False, around, probe, tile)
    upper = shifted(own, "row", 1)
    came = swapped(sent, "col", 1)
    for bit in range(1, col_bits):
        kept, sent = fold(bit, kept, came)
        came = swapped(sent, "col", 1 << bit)
    came, middle_right, dense = tied(came, middle_right, dense)
    sums = kept + came
    left_rest = shifted(middle_right, "col", 1)
    sums, upper, left_rest = tied(sums, upper, left_rest)
    top, right_top = gather(1, never_below, near, total, upper, 1)
    left_top = shifted(right_top, "col", 1)
    for bit in range(row_bits):
        sums = sums + swapped(sums, "row", 1 << bit)
    sums, left_top = tied(sums, left_top)
    field = renew(field, dense, total, top, left_top, left_rest)
    for bit in reversed(range(1, col_bits)):
        other = swapped(sums, "col", 1 << bit)
        if bit == 1:
            other, field = tied(other, field)
        sums = join(bit, sums, other)
    return field, illuminate(sums, swapped(sums, "col", 1), probe)


def solution(mesh):
    placed = (
        P(None, "row", "col"),
        P(),
        P("row", "col", None, None, None, None),
        P("row", "col", None, None, None),
    )

    def whole(object_field, probe, amplitudes, offsets):
        table = jnp.asarray(dft_tables(probe.shape[1]))
        body = jax.shard_map(
            local,
            mesh=mesh,
            in_specs=(P(),) + placed,
            out_specs=(P(None, "row", "col"), P()),
            check_vma=False,
        )
        return body(table, object_field, probe, amplitudes, offsets)

    return whole
```

```python
import functools
import math

import jax
import jax.numpy as jnp
import ml_dtypes
import numpy as np
from jax import lax
from jax.experimental import pallas as pl
from jax.experimental.pallas import tpu as pltpu
from jax.sharding import PartitionSpec as P

softening = 0.1
object_damping = 0.5
probe_damping = 1.0
MIB = 1 << 20
lane = 128
SCAN_LIMIT = 24 * MIB
VMEM = pltpu.VMEM
SMEM = pltpu.SMEM


def shifted(array, axis, by):
    peers = lax.axis_size(axis)
    return lax.ppermute(array, axis, [(i, (i + by) % peers) for i in range(peers)])


def swapped(array, axis, mask):
    peers = lax.axis_size(axis)
    return lax.ppermute(array, axis, [(i, i ^ mask) for i in range(peers)])


def handed_on(array, axis):
    peers = lax.axis_size(axis)
    return lax.ppermute(array, axis, [(i, (i + 2 - 4 * (i % 2)) % peers) for i in range(peers)])


def swapped_outward(array, axis):
    peers = lax.axis_size(axis)
    pairs = [(i, i + 1) for i in range(1, peers - 1, 2)]
    return lax.ppermute(array, axis, pairs + [(k, i) for i, k in pairs])


def dft_tables(length):
    half = length // 2
    index = np.arange(half)
    parts = []
    for odd in range(2):
        phase = ((2 * index[:, None] + odd) * index[None, :] % length) * (2.0 * math.pi / length)
        real, imag = np.cos(phase) / math.sqrt(length), -np.sin(phase) / math.sqrt(length)
        full = np.block([[real, -imag], [imag, real]])
        for value in (full, full.T):
            high = value.astype(ml_dtypes.bfloat16)
            parts += [high, (value - high.astype(np.float64)).astype(ml_dtypes.bfloat16)]
    return np.stack(parts)


def halves(value):
    high = value.astype(jnp.bfloat16)
    return high, (value - high.astype(jnp.float32)).astype(jnp.bfloat16)


def product(a, b):
    return jnp.dot(a, b, preferred_element_type=jnp.float32)


def left_product(table_ref, number, data):
    top, rest = halves(data)
    high, low = table_ref[2 * number], table_ref[2 * number + 1]
    return product(high, top) + product(high, rest) + product(low, top)


def right_product(data, table_ref, number):
    top, rest = halves(data)
    high, low = table_ref[2 * number], table_ref[2 * number + 1]
    return product(top, high) + product(rest, high) + product(top, low)


def stacked(values, axis):
    return jnp.concatenate(values, axis=axis)


def forward(table_ref, real, imag):
    half = real.shape[0] // 2
    even = stacked([real[:half] + real[half:], imag[:half] + imag[half:]], 0)
    odd = stacked([real[:half] - real[half:], imag[:half] - imag[half:]], 0)
    even, odd = left_product(table_ref, 0, even), left_product(table_ref, 2, odd)
    real, imag = stacked([even[:half], odd[:half]], 0), stacked([even[half:], odd[half:]], 0)
    even = stacked([real[:, :half] + real[:, half:], imag[:, :half] + imag[:, half:]], 1)
    odd = stacked([real[:, :half] - real[:, half:], imag[:, :half] - imag[:, half:]], 1)
    even, odd = right_product(even, table_ref, 1), right_product(odd, table_ref, 3)
    return stacked([even[:, :half], odd[:, :half]], 1), stacked([even[:, half:], odd[:, half:]], 1)


def backward(table_ref, real, imag):
    half = real.shape[0] // 2
    even = left_product(table_ref, 1, stacked([real[:half], imag[:half]], 0))
    odd = left_product(table_ref, 3, stacked([real[half:], imag[half:]], 0))
    one, two = even + odd, even - odd
    real, imag = stacked([one[:half], two[:half]], 0), stacked([one[half:], two[half:]], 0)
    even = right_product(stacked([real[:, :half], imag[:, :half]], 1), table_ref, 0)
    odd = right_product(stacked([real[:, half:], imag[:, half:]], 1), table_ref, 2)
    one, two = even + odd, even - odd
    return stacked([one[:, :half], two[:, :half]], 1), stacked([one[:, half:], two[:, half:]], 1)


def reorder_kernel(amplitude_ref, out_ref):
    side = amplitude_ref.shape[3]
    half = side // 2

    def choice(axis):
        target = lax.broadcasted_iota(jnp.int32, (side, side), axis)
        source = lax.broadcasted_iota(jnp.int32, (side, side), 1 - axis)
        wanted = jnp.where(target < half, 2 * target, 2 * (target - half) + 1)
        return jnp.where(source == wanted, 1.0, 0.0).astype(jnp.bfloat16)

    rows, cols = choice(0), choice(1)
    for sweep in range(amplitude_ref.shape[0]):
        for scan in range(amplitude_ref.shape[1]):
            moved = product(rows, amplitude_ref[sweep, scan]).astype(jnp.bfloat16)
            out_ref[sweep, scan] = product(moved, cols).astype(jnp.bfloat16)


def reorder(amplitudes):
    return pl.pallas_call(
        reorder_kernel,
        out_shape=jax.ShapeDtypeStruct(amplitudes.shape, amplitudes.dtype),
        in_specs=[pl.BlockSpec(memory_space=VMEM)],
        out_specs=pl.BlockSpec(memory_space=VMEM),
        compiler_params=pltpu.CompilerParams(vmem_limit_bytes=8 * MIB),
        cost_estimate=pl.CostEstimate(flops=300_000_000, bytes_accessed=MIB, transcendentals=0),
        name="reorder",
    )(amplitudes)


def split_column(column):
    return lax.div(column, lane), lax.rem(column, lane)


def taken(ref, plane, row, column, side):
    first, shift = split_column(column)
    count = side // lane + 1
    slabs = [ref[plane, first + k, pl.ds(row, side), :] for k in range(count)]
    return pltpu.roll(jnp.concatenate(slabs, axis=1), count * lane - shift, 1)[:, :side]


def turned(value, shift):
    side = value.shape[0]
    wide = jnp.concatenate([value, jnp.zeros((side, lane), jnp.float32)], axis=1)
    return pltpu.roll(wide, shift, 1)


def add_slabs(ref, lead, row, first, wide):
    side = wide.shape[0]
    for k in range(wide.shape[1] // lane):
        spot = lead + (first + k, pl.ds(row, side), slice(None))
        ref[spot] += wide[:, k * lane : (k + 1) * lane]


def columns(number):
    return slice(number * lane, (number + 1) * lane)


def whole_spec(count):
    return [pl.BlockSpec(memory_space=VMEM)] * count


def offsets_spec():
    return pl.BlockSpec(memory_space=SMEM)


def shape_of(*dims):
    return jax.ShapeDtypeStruct(dims, jnp.float32)


def cost(flops, moved):
    return pl.CostEstimate(flops=flops, bytes_accessed=moved, transcendentals=0)


def corner_of(offsets_ref, down, along, sweep, scan):
    spot = (down + 1, along + 1, sweep, scan)
    return offsets_ref[spot + (0,)], offsets_ref[spot + (1,)]


def halves_of(bit, half):
    mine = lax.rem(lax.axis_index("col") >> bit, 2)
    kept = pl.ds(pl.multiple_of(mine * half, 8), half)
    return kept, pl.ds(pl.multiple_of((1 - mine) * half, 8), half)


def scan_kernel(sweep, last, counts, offsets_ref, *refs):
    inputs, outputs, scratch = counts
    probe_hbm, amplitude_hbm, table_hbm = refs[:3]
    field_in = refs[3:inputs]
    outs_hbm = refs[inputs : inputs + outputs]
    rest = refs[inputs + outputs :]
    probe_ref, amplitude_ref, table_ref, sums_ref, windows_ref = rest[:5]
    small_sem, field_sem, out_sem = rest[5:8]
    side = probe_ref.shape[1]
    copies = []

    def fetch(source, target):
        copies.append(pltpu.make_async_copy(source, target, field_sem))

    small = [
        pltpu.make_async_copy(table_hbm, table_ref, small_sem.at[0]),
        pltpu.make_async_copy(probe_hbm, probe_ref, small_sem.at[1]),
        pltpu.make_async_copy(amplitude_hbm.at[sweep], amplitude_ref, small_sem.at[2]),
    ]
    if last:
        field_ref = field_in[0]
    else:
        own_hbm, right_hbm, first_hbm, second_hbm, corner_hbm = field_in
        field_ref = rest[8]
        rows, edge = own_hbm.shape[1], side // lane
        slabs = own_hbm.shape[2] // lane
        for k in range(slabs):
            fetch(own_hbm.at[:, :, columns(k)], field_ref.at[:, k, :rows])
        for k in range(edge):
            fetch(right_hbm.at[:, :, columns(k)], field_ref.at[:, slabs + k, :rows])
            fetch(first_hbm.at[:, :, columns(k)], field_ref.at[:, k, rows:])
            fetch(corner_hbm.at[:, :, columns(k)], field_ref.at[:, slabs + k, rows:])
        for k in range(edge, slabs):
            fetch(second_hbm.at[:, :, columns(k - edge)], field_ref.at[:, k, rows:])
    small[0].start()
    for copy in copies:
        copy.start()
    for copy in small[1:]:
        copy.start()
    small[0].wait()
    for copy in small[1:]:
        copy.wait()
    for copy in copies:
        copy.wait()
    probe_real, probe_imag = probe_ref[0], probe_ref[1]
    pending = []
    for scan in range(2):
        row, column = offsets_ref[0, 0, sweep, scan, 0], offsets_ref[0, 0, sweep, scan, 1]
        patch_real = taken(field_ref, 0, row, column, side)
        patch_imag = taken(field_ref, 1, row, column, side)
        wave_real = probe_real * patch_real - probe_imag * patch_imag
        wave_imag = probe_real * patch_imag + probe_imag * patch_real
        far_real, far_imag = forward(table_ref, wave_real, wave_imag)
        scale = amplitude_ref[scan].astype(jnp.float32) * lax.rsqrt(
            far_real * far_real + far_imag * far_imag + softening
        )
        back_real, back_imag = backward(table_ref, far_real * scale, far_imag * scale)
        diff_real = back_real - wave_real
        diff_imag = back_imag - wave_imag
        term_real = probe_real * diff_real + probe_imag * diff_imag
        term_imag = probe_real * diff_imag - probe_imag * diff_real
        windows_ref[scan, 0] = term_real
        windows_ref[scan, 1] = term_imag
        copy = pltpu.make_async_copy(windows_ref.at[scan], outs_hbm[2].at[scan], out_sem)
        copy.start()
        pending.append(copy)
        sums = (
            patch_real * diff_real + patch_imag * diff_imag,
            patch_real * diff_imag - patch_imag * diff_real,
            patch_real * patch_real + patch_imag * patch_imag,
        )
        for number, value in enumerate(sums):
            spot = slice(number * side, (number + 1) * side)
            if scan == 0:
                sums_ref[spot] = value
            else:
                sums_ref[spot] += value
    kept, sent = halves_of(0, outs_hbm[0].shape[0])
    outs = [(sums_ref.at[sent], outs_hbm[1]), (sums_ref.at[kept], outs_hbm[0])]
    outs = [pltpu.make_async_copy(source, target, out_sem) for source, target in outs]
    for copy in outs:
        copy.start()
    for copy in pending + outs:
        copy.wait()


def scan_step(sweep, last, offsets, probe, amplitudes, table, *field):
    side = probe.shape[1]
    shapes = [shape_of(3 * side // 2, side)] * 2 + [shape_of(2, 2, side, side)]
    scratch = [
        VMEM(probe.shape, jnp.float32),
        VMEM(amplitudes.shape[1:], amplitudes.dtype),
        VMEM(table.shape, table.dtype),
        VMEM((3 * side, side), jnp.float32),
        VMEM((2, 2, side, side), jnp.float32),
        pltpu.SemaphoreType.DMA((3,)),
        pltpu.SemaphoreType.DMA,
        pltpu.SemaphoreType.DMA,
    ]
    if not last:
        rows, cols = field[0].shape[1:]
        scratch.append(VMEM((2, (cols + side) // lane, rows + side, lane), jnp.float32))
    anywhere = pl.BlockSpec(memory_space=pl.ANY)
    counts = (3 + len(field), len(shapes), len(scratch))
    return pl.pallas_call(
        functools.partial(scan_kernel, sweep, last, counts),
        out_shape=shapes,
        in_specs=[offsets_spec()] + [anywhere] * 3 + (whole_spec(1) if last else [anywhere] * len(field)),
        out_specs=[anywhere] * len(shapes),
        scratch_shapes=scratch,
        compiler_params=pltpu.CompilerParams(vmem_limit_bytes=SCAN_LIMIT),
        cost_estimate=cost(7_000_000_000, 12 * MIB),
        name="scan",
    )(offsets, probe, amplitudes, table, *field)


def edge_starts(count, slabs, edge):
    if count < 2:
        return [slabs - edge] * count
    odd = lax.rem(lax.axis_index("col"), 2)
    return [(1 - odd) * (slabs - edge), odd * (slabs - edge)]


def place_kernel(sweep, offsets_ref, windows_ref, total_ref, *edge_refs):
    side = windows_ref.shape[2]
    edge = side // lane
    slabs, height = total_ref.shape[1:3]
    total_ref[...] = jnp.zeros_like(total_ref)
    for scan in range(2):
        row, column = offsets_ref[0, 0, sweep, scan, 0], offsets_ref[0, 0, sweep, scan, 1]
        first, shift = split_column(column)
        for plane in range(2):
            add_slabs(total_ref, (plane,), row, first, turned(windows_ref[scan, plane], shift))
    for ref, start in zip(edge_refs, edge_starts(len(edge_refs), slabs, edge)):
        ref[...] = total_ref[:, pl.ds(start, edge), side : height - side]


def place(sweep, offsets, windows, tile, sides):
    side = windows.shape[2]
    edge = side // lane
    height, slabs = tile[0] + side, tile[1] // lane + edge
    shapes = [shape_of(2, slabs, height, lane)] + [shape_of(2, edge, height - 2 * side, lane)] * sides
    return pl.pallas_call(
        functools.partial(place_kernel, sweep),
        out_shape=shapes,
        in_specs=[offsets_spec()] + whole_spec(1),
        out_specs=whole_spec(len(shapes)),
        compiler_params=pltpu.CompilerParams(vmem_limit_bytes=4 * MIB),
        cost_estimate=cost(1_000_000, 6 * MIB),
        name="place",
    )(offsets, windows)


def density_kernel(sweep, reach, offsets_ref, probe_ref, out_ref, total_ref):
    side = probe_ref.shape[1]
    slabs, height = out_ref.shape[:2]
    breadth = slabs * lane
    tile = height - side if reach else height
    span = breadth - side if reach else breadth
    total_ref[...] = jnp.zeros_like(total_ref)
    power = probe_ref[0] * probe_ref[0] + probe_ref[1] * probe_ref[1]
    steps = (-1, 0, 1) if reach else (-1, 0)
    for down in steps:
        for along in steps:
            for scan in range(2):
                row, column = corner_of(offsets_ref, down, along, sweep, scan)
                row += side + down * tile
                column += side + along * span

                @pl.when((row > 0) & (row < side + height) & (column > 0) & (column < side + breadth))
                def _():
                    first, shift = split_column(column)
                    add_slabs(total_ref, (), row, first, turned(power, shift))

    out_ref[...] = total_ref[side // lane : side // lane + slabs, side : side + height]


def density(sweep, reach, offsets, probe, tile):
    side = probe.shape[1]
    extra = side if reach else 0
    height, slabs = tile[0] + extra, (tile[1] + extra) // lane
    return pl.pallas_call(
        functools.partial(density_kernel, sweep, reach),
        out_shape=shape_of(slabs, height, lane),
        in_specs=[offsets_spec()] + whole_spec(1),
        out_specs=whole_spec(1)[0],
        scratch_shapes=[VMEM((slabs + 2 * side // lane, height + 2 * side, lane), jnp.float32)],
        compiler_params=pltpu.CompilerParams(vmem_limit_bytes=10 * MIB),
        cost_estimate=cost(1_000_000, 6 * MIB),
        name="density",
    )(offsets, probe)


def gather_kernel(sweep, below_of, offsets_ref, total_ref, windows_ref, all_ref, *refs):
    edge_refs, strip_ref = refs[:-1], refs[-1]
    slabs, side = all_ref.shape[1:3]
    height = total_ref.shape[2]
    edge = side // lane
    below = below_of()
    strip_ref[...] = jnp.zeros_like(strip_ref)
    for scan in range(2):
        row, column = corner_of(offsets_ref, 2 * below - 1, -1, sweep, scan)
        row += (2 * below - 1) * side
        first, shift = split_column(column)

        @pl.when((row > 0) & (row < 2 * side))
        def _():
            for plane in range(2):
                add_slabs(strip_ref, (plane,), row, first, turned(windows_ref[scan, plane], shift))

    base = pl.multiple_of(below * (height - side), 8)
    for plane in range(2):
        for k in range(slabs):
            all_ref[plane, k] = strip_ref[plane, k, side : 2 * side] + total_ref[plane, k, pl.ds(base, side)]
    for ref, start in zip(edge_refs, edge_starts(len(edge_refs), slabs, edge)):
        ref[...] = all_ref[:, pl.ds(start, edge)]


def partner_below():
    return 1 - lax.rem(lax.axis_index("row"), 2)


def other_below():
    return lax.rem(lax.axis_index("row"), 2)


def never_below():
    return jnp.int32(0)


def gather(sweep, below_of, offsets, total, windows, sides):
    side = windows.shape[2]
    slabs = total.shape[1]
    return pl.pallas_call(
        functools.partial(gather_kernel, sweep, below_of),
        out_shape=[shape_of(2, slabs, side, lane)] + [shape_of(2, side // lane, side, lane)] * sides,
        in_specs=[offsets_spec()] + whole_spec(2),
        out_specs=whole_spec(1 + sides),
        scratch_shapes=[VMEM((2, slabs, 3 * side, lane), jnp.float32)],
        compiler_params=pltpu.CompilerParams(vmem_limit_bytes=8 * MIB),
        cost_estimate=cost(1_000_000, 6 * MIB),
        name="gather",
    )(offsets, total, windows)


def widen_kernel(*refs):
    own_ref, right_ref, first_ref, second_ref, corner_ref, density_ref, total_ref = refs[:7]
    near_ref, far_ref, inner_refs, outer_refs, out_ref = refs[7], refs[8], refs[9:12], refs[12:15], refs[15]
    side = near_ref.shape[2]
    edge = side // lane
    slabs = out_ref.shape[1] - edge
    rows = out_ref.shape[2] - side
    odd = lax.rem(lax.axis_index("row"), 2) == 1
    odd_col = lax.rem(lax.axis_index("col"), 2) == 1
    even_col = jnp.logical_not(odd_col)
    for k in range(slabs + edge):
        for top, bottom in ((0, side), (side, rows), (rows, rows + side)):
            part = 1.0 / (density_ref[k, top:bottom] + object_damping)
            for plane in range(2):
                if top == rows:
                    if k < edge:
                        before = first_ref[plane, :, columns(k)]
                    elif k < slabs:
                        before = second_ref[plane, :, columns(k - edge)]
                    else:
                        before = corner_ref[plane, :, columns(k - slabs)]
                elif k < slabs:
                    before = own_ref[plane, top:bottom, columns(k)]
                else:
                    before = right_ref[plane, top:bottom, columns(k - slabs)]

                def picked(near, far):
                    return jnp.where(odd, near, far) if top == 0 else jnp.where(odd, far, near)

                def beside(outward, at):
                    if top == side:
                        return jnp.where(outward, outer_refs[0][plane, at], inner_refs[0][plane, at])
                    near = jnp.where(outward, outer_refs[1][plane, at], inner_refs[1][plane, at])
                    far = jnp.where(outward, outer_refs[2][plane, at], inner_refs[2][plane, at])
                    return picked(near, far)

                if top == side:
                    terms = total_ref[plane, k, top:bottom]
                else:
                    terms = picked(near_ref[plane, k], far_ref[plane, k])
                if k < edge:
                    terms += beside(even_col, k)
                if k >= slabs:
                    terms += beside(odd_col, k - slabs)
                out_ref[plane, k, top:bottom] = before + terms * part


def widen(pieces, dense, total, near, far, inner, outer):
    return pl.pallas_call(
        widen_kernel,
        out_shape=shape_of(*total.shape),
        in_specs=whole_spec(15),
        out_specs=whole_spec(1)[0],
        compiler_params=pltpu.CompilerParams(vmem_limit_bytes=6 * MIB),
        cost_estimate=cost(4_000_000, 20 * MIB),
        name="widen",
    )(*pieces, dense, total, near, far, *inner, *outer)


def renew_kernel(field_ref, density_ref, total_ref, top_ref, left_top_ref, left_rest_ref, out_ref):
    slabs, rows = density_ref.shape[:2]
    edge, side = left_top_ref.shape[1:3]
    for k in range(slabs):
        part = 1.0 / (density_ref[k] + object_damping)
        for plane in range(2):
            top = top_ref[plane, k]
            rest = total_ref[plane, k, side:rows]
            if k < edge:
                top += left_top_ref[plane, k]
                rest += left_rest_ref[plane, k]
            out_ref[plane, :side, columns(k)] = field_ref[plane, k, :side] + top * part[:side]
            out_ref[plane, side:, columns(k)] = field_ref[plane, k, side:rows] + rest * part[side:]


def renew(field, dense, total, top, left_top, left_rest):
    slabs, rows = dense.shape[:2]
    return pl.pallas_call(
        renew_kernel,
        out_shape=shape_of(2, rows, slabs * lane),
        in_specs=whole_spec(6),
        out_specs=whole_spec(1)[0],
        compiler_params=pltpu.CompilerParams(vmem_limit_bytes=4 * MIB),
        cost_estimate=cost(4_000_000, 10 * MIB),
        name="renew",
    )(field, dense, total, top, left_top, left_rest)


def fold_kernel(bit, value_ref, came_ref, kept_ref, sent_ref, total_ref):
    total_ref[...] = value_ref[...] + came_ref[...]
    kept, sent = halves_of(bit, kept_ref.shape[0])
    kept_ref[...] = total_ref[kept]
    sent_ref[...] = total_ref[sent]


def fold(bit, value, came):
    rows, side = value.shape
    return pl.pallas_call(
        functools.partial(fold_kernel, bit),
        out_shape=[shape_of(rows // 2, side)] * 2,
        in_specs=whole_spec(2),
        out_specs=whole_spec(2),
        scratch_shapes=[VMEM(value.shape, jnp.float32)],
        compiler_params=pltpu.CompilerParams(vmem_limit_bytes=4 * MIB),
        cost_estimate=cost(100_000, MIB),
        name="fold",
    )(value, came)


def join_kernel(bit, value_ref, other_ref, out_ref):
    kept, sent = halves_of(bit, value_ref.shape[0])
    out_ref[kept] = value_ref[...]
    out_ref[sent] = other_ref[...]


def join(bit, value, other):
    rows, side = value.shape
    return pl.pallas_call(
        functools.partial(join_kernel, bit),
        out_shape=shape_of(2 * rows, side),
        in_specs=whole_spec(2),
        out_specs=whole_spec(1)[0],
        compiler_params=pltpu.CompilerParams(vmem_limit_bytes=4 * MIB),
        cost_estimate=cost(100_000, MIB),
        name="join",
    )(value, other)


def illuminate_kernel(value_ref, other_ref, probe_ref, out_ref, total_ref):
    kept, sent = halves_of(0, value_ref.shape[0])
    total_ref[kept] = value_ref[...]
    total_ref[sent] = other_ref[...]
    side = probe_ref.shape[1]
    part = 1.0 / (total_ref[2 * side :] + probe_damping)
    out_ref[0] = probe_ref[0] + total_ref[:side] * part
    out_ref[1] = probe_ref[1] + total_ref[side : 2 * side] * part


def illuminate(value, other, probe):
    rows, side = value.shape
    return pl.pallas_call(
        illuminate_kernel,
        out_shape=shape_of(*probe.shape),
        in_specs=whole_spec(3),
        out_specs=whole_spec(1)[0],
        scratch_shapes=[VMEM((2 * rows, side), jnp.float32)],
        compiler_params=pltpu.CompilerParams(vmem_limit_bytes=6 * MIB),
        cost_estimate=cost(1_000_000, 2 * MIB),
        name="illuminate",
    )(value, other, probe)


def tied(*values):
    return lax.optimization_barrier(values)


def local(table, object_field, probe, amplitudes, offsets):
    side = probe.shape[1]
    tile = object_field.shape[1:]
    measured = reorder(amplitudes[0, 0])
    col_bits = int(math.log2(lax.axis_size("col")))
    row_bits = int(math.log2(lax.axis_size("row")))

    strip, rest = tied(object_field[:, :side, :side], object_field)
    first = shifted(strip, "row", -1)
    second = shifted(rest[:, :side, side:], "row", -1)
    right = shifted(object_field[:, :, :side], "col", -1)
    near = jnp.concatenate([shifted(offsets, "row", 1), offsets, shifted(offsets, "row", -1)], axis=0)
    first, near = tied(first, near)
    corner = shifted(first, "col", -1)
    pieces = (object_field, right, first, second, corner)

    kept, sent, own = scan_step(0, False, offsets, probe, measured, table, *pieces)
    total, middle_inner, middle_outer = place(0, offsets, own, tile, 2)
    around = jnp.concatenate([shifted(near, "col", 1), near, shifted(near, "col", -1)], axis=1)
    dense = density(0, True, around, probe, tile)
    partner = swapped(own, "row", 1)
    came = swapped(sent, "col", 1)
    for bit in range(1, col_bits):
        kept, sent = fold(bit, kept, came)
        came = swapped(sent, "col", 1 << bit)
    came, around = tied(came, around)
    sums = kept + came
    for bit in reversed(range(1, row_bits)):
        came = swapped(sums, "row", 1 << bit)
        if bit == row_bits - 1:
            came, dense, middle_inner, middle_outer = tied(came, dense, middle_inner, middle_outer)
        sums = sums + came
    inner_strips = [swapped(middle_inner, "col", 1)]
    outer_strips = [swapped_outward(middle_outer, "col")]
    sums, partner = tied(sums, partner)
    passed = handed_on(partner, "row")
    near_all, near_inner, near_outer = gather(0, partner_below, near, total, partner, 2)
    inner_strips.append(swapped(near_inner, "col", 1))
    outer_strips.append(swapped_outward(near_outer, "col"))
    sums = sums + swapped(sums, "row", 1)
    for bit in reversed(range(1, col_bits)):
        other = swapped(sums, "col", 1 << bit)
        if bit == col_bits - 1:
            other, outer_strips[0], inner_strips[0] = tied(other, outer_strips[0], inner_strips[0])
        sums = join(bit, sums, other)
    probe = illuminate(sums, swapped(sums, "col", 1), probe)
    passed, probe, outer_strips[1], inner_strips[1] = tied(passed, probe, outer_strips[1], inner_strips[1])
    far_all, far_inner, far_outer = gather(0, other_below, near, total, passed, 2)
    inner_strips.append(swapped(far_inner, "col", 1))
    outer_strips.append(swapped_outward(far_outer, "col"))
    field = widen(pieces, dense, total, near_all, far_all, inner_strips, outer_strips)

    kept, sent, own = scan_step(1, True, offsets, probe, measured, table, field)
    total, middle_right = place(1, offsets, own, tile, 1)
    dense = density(1, False, around, probe, tile)
    upper = shifted(own, "row", 1)
    came = swapped(sent, "col", 1)
    for bit in range(1, col_bits):
        kept, sent = fold(bit, kept, came)
        came = swapped(sent, "col", 1 << bit)
    came, middle_right, dense = tied(came, middle_right, dense)
    sums = kept + came
    left_rest = shifted(middle_right, "col", 1)
    sums, upper, left_rest = tied(sums, upper, left_rest)
    top, right_top = gather(1, never_below, near, total, upper, 1)
    left_top = shifted(right_top, "col", 1)
    for bit in range(row_bits):
        sums = sums + swapped(sums, "row", 1 << bit)
    sums, left_top = tied(sums, left_top)
    field = renew(field, dense, total, top, left_top, left_rest)
    for bit in reversed(range(1, col_bits)):
        other = swapped(sums, "col", 1 << bit)
        if bit == 1:
            other, field = tied(other, field)
        sums = join(bit, sums, other)
    return field, illuminate(sums, swapped(sums, "col", 1), probe)


def solution(mesh):
    placed = (
        P(None, "row", "col"),
        P(),
        P("row", "col", None, None, None, None),
        P("row", "col", None, None, None),
    )

    def whole(object_field, probe, amplitudes, offsets):
        table = jnp.asarray(dft_tables(probe.shape[1]))
        body = jax.shard_map(
            local,
            mesh=mesh,
            in_specs=(P(),) + placed,
            out_specs=(P(None, "row", "col"), P()),
            check_vma=False,
        )
        return body(table, object_field, probe, amplitudes, offsets)

    return whole
```

```python
import functools
import math

import jax
import jax.numpy as jnp
import ml_dtypes
import numpy as np
from jax import lax
from jax.experimental import pallas as pl
from jax.experimental.pallas import tpu as pltpu
from jax.sharding import PartitionSpec as P

softening = 0.1
object_damping = 0.5
probe_damping = 1.0
MIB = 1 << 20
lane = 128
SCAN_LIMIT = 24 * MIB
VMEM = pltpu.VMEM
SMEM = pltpu.SMEM


def shifted(array, axis, by):
    peers = lax.axis_size(axis)
    return lax.ppermute(array, axis, [(i, (i + by) % peers) for i in range(peers)])


def swapped(array, axis, mask):
    peers = lax.axis_size(axis)
    return lax.ppermute(array, axis, [(i, i ^ mask) for i in range(peers)])


def handed_on(array, axis):
    peers = lax.axis_size(axis)
    return lax.ppermute(array, axis, [(i, (i + 2 - 4 * (i % 2)) % peers) for i in range(peers)])


def swapped_outward(array, axis):
    peers = lax.axis_size(axis)
    pairs = [(i, i + 1) for i in range(1, peers - 1, 2)]
    return lax.ppermute(array, axis, pairs + [(k, i) for i, k in pairs])


def dft_tables(length):
    half = length // 2
    index = np.arange(half)
    parts = []
    for odd in range(2):
        phase = ((2 * index[:, None] + odd) * index[None, :] % length) * (2.0 * math.pi / length)
        real, imag = np.cos(phase) / math.sqrt(length), -np.sin(phase) / math.sqrt(length)
        full = np.block([[real, -imag], [imag, real]])
        for value in (full, full.T):
            high = value.astype(ml_dtypes.bfloat16)
            parts += [high, (value - high.astype(np.float64)).astype(ml_dtypes.bfloat16)]
    return np.stack(parts)


def halves(value):
    high = value.astype(jnp.bfloat16)
    return high, (value - high.astype(jnp.float32)).astype(jnp.bfloat16)


def product(a, b):
    return jnp.dot(a, b, preferred_element_type=jnp.float32)


def left_product(table_ref, number, data):
    top, rest = halves(data)
    high, low = table_ref[2 * number], table_ref[2 * number + 1]
    return product(high, top) + product(high, rest) + product(low, top)


def right_product(data, table_ref, number):
    top, rest = halves(data)
    high, low = table_ref[2 * number], table_ref[2 * number + 1]
    return product(top, high) + product(rest, high) + product(top, low)


def stacked(values, axis):
    return jnp.concatenate(values, axis=axis)


def forward(table_ref, real, imag):
    half = real.shape[0] // 2
    even = stacked([real[:half] + real[half:], imag[:half] + imag[half:]], 0)
    odd = stacked([real[:half] - real[half:], imag[:half] - imag[half:]], 0)
    even, odd = left_product(table_ref, 0, even), left_product(table_ref, 2, odd)
    real, imag = stacked([even[:half], odd[:half]], 0), stacked([even[half:], odd[half:]], 0)
    even = stacked([real[:, :half] + real[:, half:], imag[:, :half] + imag[:, half:]], 1)
    odd = stacked([real[:, :half] - real[:, half:], imag[:, :half] - imag[:, half:]], 1)
    even, odd = right_product(even, table_ref, 1), right_product(odd, table_ref, 3)
    return stacked([even[:, :half], odd[:, :half]], 1), stacked([even[:, half:], odd[:, half:]], 1)


def backward(table_ref, real, imag):
    half = real.shape[0] // 2
    even = left_product(table_ref, 1, stacked([real[:half], imag[:half]], 0))
    odd = left_product(table_ref, 3, stacked([real[half:], imag[half:]], 0))
    one, two = even + odd, even - odd
    real, imag = stacked([one[:half], two[:half]], 0), stacked([one[half:], two[half:]], 0)
    even = right_product(stacked([real[:, :half], imag[:, :half]], 1), table_ref, 0)
    odd = right_product(stacked([real[:, half:], imag[:, half:]], 1), table_ref, 2)
    one, two = even + odd, even - odd
    return stacked([one[:, :half], two[:, :half]], 1), stacked([one[:, half:], two[:, half:]], 1)


def reorder_kernel(amplitude_ref, out_ref):
    side = amplitude_ref.shape[3]
    half = side // 2

    def choice(axis):
        target = lax.broadcasted_iota(jnp.int32, (side, side), axis)
        source = lax.broadcasted_iota(jnp.int32, (side, side), 1 - axis)
        wanted = jnp.where(target < half, 2 * target, 2 * (target - half) + 1)
        return jnp.where(source == wanted, 1.0, 0.0).astype(jnp.bfloat16)

    rows, cols = choice(0), choice(1)
    for sweep in range(amplitude_ref.shape[0]):
        for scan in range(amplitude_ref.shape[1]):
            moved = product(rows, amplitude_ref[sweep, scan]).astype(jnp.bfloat16)
            out_ref[sweep, scan] = product(moved, cols).astype(jnp.bfloat16)


def reorder(amplitudes):
    return pl.pallas_call(
        reorder_kernel,
        out_shape=jax.ShapeDtypeStruct(amplitudes.shape, amplitudes.dtype),
        in_specs=[pl.BlockSpec(memory_space=VMEM)],
        out_specs=pl.BlockSpec(memory_space=VMEM),
        compiler_params=pltpu.CompilerParams(vmem_limit_bytes=8 * MIB),
        cost_estimate=pl.CostEstimate(flops=300_000_000, bytes_accessed=MIB, transcendentals=0),
        name="reorder",
    )(amplitudes)


def split_column(column):
    return lax.div(column, lane), lax.rem(column, lane)


def taken(ref, plane, row, column, side):
    first, shift = split_column(column)
    count = side // lane + 1
    slabs = [ref[plane, first + k, pl.ds(row, side), :] for k in range(count)]
    return pltpu.roll(jnp.concatenate(slabs, axis=1), count * lane - shift, 1)[:, :side]


def turned(value, shift):
    side = value.shape[0]
    wide = jnp.concatenate([value, jnp.zeros((side, lane), jnp.float32)], axis=1)
    return pltpu.roll(wide, shift, 1)


def add_slabs(ref, lead, row, first, wide):
    side = wide.shape[0]
    for k in range(wide.shape[1] // lane):
        spot = lead + (first + k, pl.ds(row, side), slice(None))
        ref[spot] += wide[:, k * lane : (k + 1) * lane]


def columns(number):
    return slice(number * lane, (number + 1) * lane)


def whole_spec(count):
    return [pl.BlockSpec(memory_space=VMEM)] * count


def offsets_spec():
    return pl.BlockSpec(memory_space=SMEM)


def shape_of(*dims):
    return jax.ShapeDtypeStruct(dims, jnp.float32)


def cost(flops, moved):
    return pl.CostEstimate(flops=flops, bytes_accessed=moved, transcendentals=0)


def corner_of(offsets_ref, down, along, sweep, scan):
    spot = (down + 1, along + 1, sweep, scan)
    return offsets_ref[spot + (0,)], offsets_ref[spot + (1,)]


def halves_of(bit, half):
    mine = lax.rem(lax.axis_index("col") >> bit, 2)
    kept = pl.ds(pl.multiple_of(mine * half, 8), half)
    return kept, pl.ds(pl.multiple_of((1 - mine) * half, 8), half)


def scan_kernel(sweep, last, counts, offsets_ref, *refs):
    inputs, outputs, scratch = counts
    probe_hbm, amplitude_hbm, table_hbm = refs[:3]
    field_in = refs[3:inputs]
    outs_hbm = refs[inputs : inputs + outputs]
    rest = refs[inputs + outputs :]
    probe_ref, amplitude_ref, table_ref, sums_ref, windows_ref = rest[:5]
    small_sem, field_sem, out_sem = rest[5:8]
    side = probe_ref.shape[1]
    copies = []

    def fetch(source, target):
        copies.append(pltpu.make_async_copy(source, target, field_sem))

    small = [
        pltpu.make_async_copy(table_hbm, table_ref, small_sem.at[0]),
        pltpu.make_async_copy(probe_hbm, probe_ref, small_sem.at[1]),
        pltpu.make_async_copy(amplitude_hbm.at[sweep], amplitude_ref, small_sem.at[2]),
    ]
    if last:
        field_ref = field_in[0]
    else:
        own_hbm, right_hbm, first_hbm, second_hbm, corner_hbm = field_in
        field_ref = rest[8]
        rows, edge = own_hbm.shape[1], side // lane
        slabs = own_hbm.shape[2] // lane
        for k in range(slabs):
            fetch(own_hbm.at[:, :, columns(k)], field_ref.at[:, k, :rows])
        for k in range(edge):
            fetch(right_hbm.at[:, :, columns(k)], field_ref.at[:, slabs + k, :rows])
            fetch(first_hbm.at[:, :, columns(k)], field_ref.at[:, k, rows:])
            fetch(corner_hbm.at[:, :, columns(k)], field_ref.at[:, slabs + k, rows:])
        for k in range(edge, slabs):
            fetch(second_hbm.at[:, :, columns(k - edge)], field_ref.at[:, k, rows:])
    small[0].start()
    for copy in copies:
        copy.start()
    for copy in small[1:]:
        copy.start()
    small[0].wait()
    for copy in small[1:]:
        copy.wait()
    for copy in copies:
        copy.wait()
    probe_real, probe_imag = probe_ref[0], probe_ref[1]
    pending = []
    for scan in range(2):
        row, column = offsets_ref[0, 0, sweep, scan, 0], offsets_ref[0, 0, sweep, scan, 1]
        patch_real = taken(field_ref, 0, row, column, side)
        patch_imag = taken(field_ref, 1, row, column, side)
        wave_real = probe_real * patch_real - probe_imag * patch_imag
        wave_imag = probe_real * patch_imag + probe_imag * patch_real
        far_real, far_imag = forward(table_ref, wave_real, wave_imag)
        scale = amplitude_ref[scan].astype(jnp.float32) * lax.rsqrt(
            far_real * far_real + far_imag * far_imag + softening
        )
        back_real, back_imag = backward(table_ref, far_real * scale, far_imag * scale)
        diff_real = back_real - wave_real
        diff_imag = back_imag - wave_imag
        term_real = probe_real * diff_real + probe_imag * diff_imag
        term_imag = probe_real * diff_imag - probe_imag * diff_real
        windows_ref[scan, 0] = term_real
        windows_ref[scan, 1] = term_imag
        copy = pltpu.make_async_copy(windows_ref.at[scan], outs_hbm[2].at[scan], out_sem)
        copy.start()
        pending.append(copy)
        sums = (
            patch_real * diff_real + patch_imag * diff_imag,
            patch_real * diff_imag - patch_imag * diff_real,
            patch_real * patch_real + patch_imag * patch_imag,
        )
        for number, value in enumerate(sums):
            if scan == 0:
                sums_ref[number] = value
            else:
                sums_ref[number] += value
    kept, sent = halves_of(0, outs_hbm[0].shape[1])
    outs = [(sums_ref.at[:, sent], outs_hbm[1]), (sums_ref.at[:, kept], outs_hbm[0])]
    outs = [pltpu.make_async_copy(source, target, out_sem) for source, target in outs]
    for copy in outs:
        copy.start()
    for copy in pending + outs:
        copy.wait()


def scan_step(sweep, last, offsets, probe, amplitudes, table, *field):
    side = probe.shape[1]
    shapes = [shape_of(3, side // 2, side)] * 2 + [shape_of(2, 2, side, side)]
    scratch = [
        VMEM(probe.shape, jnp.float32),
        VMEM(amplitudes.shape[1:], amplitudes.dtype),
        VMEM(table.shape, table.dtype),
        VMEM((3, side, side), jnp.float32),
        VMEM((2, 2, side, side), jnp.float32),
        pltpu.SemaphoreType.DMA((3,)),
        pltpu.SemaphoreType.DMA,
        pltpu.SemaphoreType.DMA,
    ]
    if not last:
        rows, cols = field[0].shape[1:]
        scratch.append(VMEM((2, (cols + side) // lane, rows + side, lane), jnp.float32))
    anywhere = pl.BlockSpec(memory_space=pl.ANY)
    counts = (3 + len(field), len(shapes), len(scratch))
    return pl.pallas_call(
        functools.partial(scan_kernel, sweep, last, counts),
        out_shape=shapes,
        in_specs=[offsets_spec()] + [anywhere] * 3 + (whole_spec(1) if last else [anywhere] * len(field)),
        out_specs=[anywhere] * len(shapes),
        scratch_shapes=scratch,
        compiler_params=pltpu.CompilerParams(vmem_limit_bytes=SCAN_LIMIT),
        cost_estimate=cost(7_000_000_000, 12 * MIB),
        name="scan",
    )(offsets, probe, amplitudes, table, *field)


def edge_starts(count, slabs, edge):
    if count < 2:
        return [slabs - edge] * count
    odd = lax.rem(lax.axis_index("col"), 2)
    return [(1 - odd) * (slabs - edge), odd * (slabs - edge)]


def place_kernel(sweep, offsets_ref, windows_ref, total_ref, *edge_refs):
    side = windows_ref.shape[2]
    edge = side // lane
    slabs, height = total_ref.shape[1:3]
    total_ref[...] = jnp.zeros_like(total_ref)
    for scan in range(2):
        row, column = offsets_ref[0, 0, sweep, scan, 0], offsets_ref[0, 0, sweep, scan, 1]
        first, shift = split_column(column)
        for plane in range(2):
            add_slabs(total_ref, (plane,), row, first, turned(windows_ref[scan, plane], shift))
    for ref, start in zip(edge_refs, edge_starts(len(edge_refs), slabs, edge)):
        ref[...] = total_ref[:, pl.ds(start, edge), side : height - side]


def place(sweep, offsets, windows, tile, sides):
    side = windows.shape[2]
    edge = side // lane
    height, slabs = tile[0] + side, tile[1] // lane + edge
    shapes = [shape_of(2, slabs, height, lane)] + [shape_of(2, edge, height - 2 * side, lane)] * sides
    return pl.pallas_call(
        functools.partial(place_kernel, sweep),
        out_shape=shapes,
        in_specs=[offsets_spec()] + whole_spec(1),
        out_specs=whole_spec(len(shapes)),
        compiler_params=pltpu.CompilerParams(vmem_limit_bytes=4 * MIB),
        cost_estimate=cost(1_000_000, 6 * MIB),
        name="place",
    )(offsets, windows)


def density_kernel(sweep, reach, offsets_ref, probe_ref, out_ref, total_ref):
    side = probe_ref.shape[1]
    slabs, height = out_ref.shape[:2]
    breadth = slabs * lane
    tile = height - side if reach else height
    span = breadth - side if reach else breadth
    total_ref[...] = jnp.zeros_like(total_ref)
    power = probe_ref[0] * probe_ref[0] + probe_ref[1] * probe_ref[1]
    steps = (-1, 0, 1) if reach else (-1, 0)
    for down in steps:
        for along in steps:
            for scan in range(2):
                row, column = corner_of(offsets_ref, down, along, sweep, scan)
                row += side + down * tile
                column += side + along * span

                @pl.when((row > 0) & (row < side + height) & (column > 0) & (column < side + breadth))
                def _():
                    first, shift = split_column(column)
                    add_slabs(total_ref, (), row, first, turned(power, shift))

    out_ref[...] = total_ref[side // lane : side // lane + slabs, side : side + height]


def density(sweep, reach, offsets, probe, tile):
    side = probe.shape[1]
    extra = side if reach else 0
    height, slabs = tile[0] + extra, (tile[1] + extra) // lane
    return pl.pallas_call(
        functools.partial(density_kernel, sweep, reach),
        out_shape=shape_of(slabs, height, lane),
        in_specs=[offsets_spec()] + whole_spec(1),
        out_specs=whole_spec(1)[0],
        scratch_shapes=[VMEM((slabs + 2 * side // lane, height + 2 * side, lane), jnp.float32)],
        compiler_params=pltpu.CompilerParams(vmem_limit_bytes=10 * MIB),
        cost_estimate=cost(1_000_000, 6 * MIB),
        name="density",
    )(offsets, probe)


def gather_kernel(sweep, below_of, offsets_ref, total_ref, windows_ref, all_ref, *refs):
    edge_refs, strip_ref = refs[:-1], refs[-1]
    slabs, side = all_ref.shape[1:3]
    height = total_ref.shape[2]
    edge = side // lane
    below = below_of()
    strip_ref[...] = jnp.zeros_like(strip_ref)
    for scan in range(2):
        row, column = corner_of(offsets_ref, 2 * below - 1, -1, sweep, scan)
        row += (2 * below - 1) * side
        first, shift = split_column(column)

        @pl.when((row > 0) & (row < 2 * side))
        def _():
            for plane in range(2):
                add_slabs(strip_ref, (plane,), row, first, turned(windows_ref[scan, plane], shift))

    base = pl.multiple_of(below * (height - side), 8)
    for plane in range(2):
        for k in range(slabs):
            all_ref[plane, k] = strip_ref[plane, k, side : 2 * side] + total_ref[plane, k, pl.ds(base, side)]
    for ref, start in zip(edge_refs, edge_starts(len(edge_refs), slabs, edge)):
        ref[...] = all_ref[:, pl.ds(start, edge)]


def partner_below():
    return 1 - lax.rem(lax.axis_index("row"), 2)


def other_below():
    return lax.rem(lax.axis_index("row"), 2)


def never_below():
    return jnp.int32(0)


def gather(sweep, below_of, offsets, total, windows, sides):
    side = windows.shape[2]
    slabs = total.shape[1]
    return pl.pallas_call(
        functools.partial(gather_kernel, sweep, below_of),
        out_shape=[shape_of(2, slabs, side, lane)] + [shape_of(2, side // lane, side, lane)] * sides,
        in_specs=[offsets_spec()] + whole_spec(2),
        out_specs=whole_spec(1 + sides),
        scratch_shapes=[VMEM((2, slabs, 3 * side, lane), jnp.float32)],
        compiler_params=pltpu.CompilerParams(vmem_limit_bytes=8 * MIB),
        cost_estimate=cost(1_000_000, 6 * MIB),
        name="gather",
    )(offsets, total, windows)


def widen_kernel(*refs):
    own_ref, right_ref, first_ref, second_ref, corner_ref, density_ref, total_ref = refs[:7]
    near_ref, far_ref, inner_refs, outer_refs, out_ref = refs[7], refs[8], refs[9:12], refs[12:15], refs[15]
    side = near_ref.shape[2]
    edge = side // lane
    slabs = out_ref.shape[1] - edge
    rows = out_ref.shape[2] - side
    odd = lax.rem(lax.axis_index("row"), 2) == 1
    odd_col = lax.rem(lax.axis_index("col"), 2) == 1
    even_col = jnp.logical_not(odd_col)
    for k in range(slabs + edge):
        for top, bottom in ((0, side), (side, rows), (rows, rows + side)):
            part = 1.0 / (density_ref[k, top:bottom] + object_damping)
            for plane in range(2):
                if top == rows:
                    if k < edge:
                        before = first_ref[plane, :, columns(k)]
                    elif k < slabs:
                        before = second_ref[plane, :, columns(k - edge)]
                    else:
                        before = corner_ref[plane, :, columns(k - slabs)]
                elif k < slabs:
                    before = own_ref[plane, top:bottom, columns(k)]
                else:
                    before = right_ref[plane, top:bottom, columns(k - slabs)]

                def picked(near, far):
                    return jnp.where(odd, near, far) if top == 0 else jnp.where(odd, far, near)

                def beside(outward, at):
                    if top == side:
                        return jnp.where(outward, outer_refs[0][plane, at], inner_refs[0][plane, at])
                    near = jnp.where(outward, outer_refs[1][plane, at], inner_refs[1][plane, at])
                    far = jnp.where(outward, outer_refs[2][plane, at], inner_refs[2][plane, at])
                    return picked(near, far)

                if top == side:
                    terms = total_ref[plane, k, top:bottom]
                else:
                    terms = picked(near_ref[plane, k], far_ref[plane, k])
                if k < edge:
                    terms += beside(even_col, k)
                if k >= slabs:
                    terms += beside(odd_col, k - slabs)
                out_ref[plane, k, top:bottom] = before + terms * part


def widen(pieces, dense, total, near, far, inner, outer):
    return pl.pallas_call(
        widen_kernel,
        out_shape=shape_of(*total.shape),
        in_specs=whole_spec(15),
        out_specs=whole_spec(1)[0],
        compiler_params=pltpu.CompilerParams(vmem_limit_bytes=6 * MIB),
        cost_estimate=cost(4_000_000, 20 * MIB),
        name="widen",
    )(*pieces, dense, total, near, far, *inner, *outer)


def renew_kernel(field_ref, density_ref, total_ref, top_ref, left_top_ref, left_rest_ref, out_ref):
    slabs, rows = density_ref.shape[:2]
    edge, side = left_top_ref.shape[1:3]
    for k in range(slabs):
        part = 1.0 / (density_ref[k] + object_damping)
        for plane in range(2):
            top = top_ref[plane, k]
            rest = total_ref[plane, k, side:rows]
            if k < edge:
                top += left_top_ref[plane, k]
                rest += left_rest_ref[plane, k]
            out_ref[plane, :side, columns(k)] = field_ref[plane, k, :side] + top * part[:side]
            out_ref[plane, side:, columns(k)] = field_ref[plane, k, side:rows] + rest * part[side:]


def renew(field, dense, total, top, left_top, left_rest):
    slabs, rows = dense.shape[:2]
    return pl.pallas_call(
        renew_kernel,
        out_shape=shape_of(2, rows, slabs * lane),
        in_specs=whole_spec(6),
        out_specs=whole_spec(1)[0],
        compiler_params=pltpu.CompilerParams(vmem_limit_bytes=4 * MIB),
        cost_estimate=cost(4_000_000, 10 * MIB),
        name="renew",
    )(field, dense, total, top, left_top, left_rest)


def fold_kernel(bit, value_ref, came_ref, kept_ref, sent_ref, total_ref):
    total_ref[...] = value_ref[...] + came_ref[...]
    kept, sent = halves_of(bit, kept_ref.shape[1])
    kept_ref[...] = total_ref[:, kept]
    sent_ref[...] = total_ref[:, sent]


def fold(bit, value, came):
    planes, rows, side = value.shape
    return pl.pallas_call(
        functools.partial(fold_kernel, bit),
        out_shape=[shape_of(planes, rows // 2, side)] * 2,
        in_specs=whole_spec(2),
        out_specs=whole_spec(2),
        scratch_shapes=[VMEM(value.shape, jnp.float32)],
        compiler_params=pltpu.CompilerParams(vmem_limit_bytes=4 * MIB),
        cost_estimate=cost(100_000, MIB),
        name="fold",
    )(value, came)


def join_kernel(bit, value_ref, other_ref, out_ref):
    kept, sent = halves_of(bit, value_ref.shape[1])
    out_ref[:, kept] = value_ref[...]
    out_ref[:, sent] = other_ref[...]


def join(bit, value, other):
    planes, rows, side = value.shape
    return pl.pallas_call(
        functools.partial(join_kernel, bit),
        out_shape=shape_of(planes, 2 * rows, side),
        in_specs=whole_spec(2),
        out_specs=whole_spec(1)[0],
        compiler_params=pltpu.CompilerParams(vmem_limit_bytes=4 * MIB),
        cost_estimate=cost(100_000, MIB),
        name="join",
    )(value, other)


def illuminate_kernel(bits, sums_ref, probe_ref, out_ref):
    rows = sums_ref.shape[1]
    start, half = 0, probe_ref.shape[1]
    for bit in range(bits):
        half //= 2
        start += lax.rem(lax.axis_index("col") >> bit, 2) * half
    spot = pl.ds(pl.multiple_of(start, 8), rows)
    part = 1.0 / (sums_ref[2] + probe_damping)
    for plane in range(2):
        out_ref[plane] = probe_ref[plane, spot] + sums_ref[plane] * part


def illuminate(bits, sums, probe):
    return pl.pallas_call(
        functools.partial(illuminate_kernel, bits),
        out_shape=shape_of(2, *sums.shape[1:]),
        in_specs=whole_spec(2),
        out_specs=whole_spec(1)[0],
        compiler_params=pltpu.CompilerParams(vmem_limit_bytes=4 * MIB),
        cost_estimate=cost(100_000, MIB),
        name="illuminate",
    )(sums, probe)


def tied(*values):
    return lax.optimization_barrier(values)


def local(table, object_field, probe, amplitudes, offsets):
    side = probe.shape[1]
    tile = object_field.shape[1:]
    measured = reorder(amplitudes[0, 0])
    col_bits = int(math.log2(lax.axis_size("col")))
    row_bits = int(math.log2(lax.axis_size("row")))

    strip, rest = tied(object_field[:, :side, :side], object_field)
    first = shifted(strip, "row", -1)
    second = shifted(rest[:, :side, side:], "row", -1)
    right = shifted(object_field[:, :, :side], "col", -1)
    near = jnp.concatenate([shifted(offsets, "row", 1), offsets, shifted(offsets, "row", -1)], axis=0)
    first, near = tied(first, near)
    corner = shifted(first, "col", -1)
    pieces = (object_field, right, first, second, corner)

    kept, sent, own = scan_step(0, False, offsets, probe, measured, table, *pieces)
    total, middle_inner, middle_outer = place(0, offsets, own, tile, 2)
    around = jnp.concatenate([shifted(near, "col", 1), near, shifted(near, "col", -1)], axis=1)
    dense = density(0, True, around, probe, tile)
    partner = swapped(own, "row", 1)
    came = swapped(sent, "col", 1)
    for bit in range(1, col_bits):
        kept, sent = fold(bit, kept, came)
        came = swapped(sent, "col", 1 << bit)
    came, around = tied(came, around)
    sums = kept + came
    for bit in reversed(range(1, row_bits)):
        came = swapped(sums, "row", 1 << bit)
        if bit == row_bits - 1:
            came, dense, middle_inner, middle_outer = tied(came, dense, middle_inner, middle_outer)
        sums = sums + came
    inner_strips = [swapped(middle_inner, "col", 1)]
    outer_strips = [swapped_outward(middle_outer, "col")]
    sums, partner = tied(sums, partner)
    passed = handed_on(partner, "row")
    near_all, near_inner, near_outer = gather(0, partner_below, near, total, partner, 2)
    inner_strips.append(swapped(near_inner, "col", 1))
    outer_strips.append(swapped_outward(near_outer, "col"))
    sums = sums + swapped(sums, "row", 1)
    probe = illuminate(col_bits, sums, probe)
    for bit in reversed(range(col_bits)):
        other = swapped(probe, "col", 1 << bit)
        if bit == col_bits - 1:
            other, outer_strips[0], inner_strips[0] = tied(other, outer_strips[0], inner_strips[0])
        probe = join(bit, probe, other)
    passed, probe, outer_strips[1], inner_strips[1] = tied(passed, probe, outer_strips[1], inner_strips[1])
    far_all, far_inner, far_outer = gather(0, other_below, near, total, passed, 2)
    inner_strips.append(swapped(far_inner, "col", 1))
    outer_strips.append(swapped_outward(far_outer, "col"))
    field = widen(pieces, dense, total, near_all, far_all, inner_strips, outer_strips)

    kept, sent, own = scan_step(1, True, offsets, probe, measured, table, field)
    total, middle_right = place(1, offsets, own, tile, 1)
    dense = density(1, False, around, probe, tile)
    upper = shifted(own, "row", 1)
    came = swapped(sent, "col", 1)
    for bit in range(1, col_bits):
        kept, sent = fold(bit, kept, came)
        came = swapped(sent, "col", 1 << bit)
    came, middle_right, dense = tied(came, middle_right, dense)
    sums = kept + came
    left_rest = shifted(middle_right, "col", 1)
    sums, upper, left_rest = tied(sums, upper, left_rest)
    top, right_top = gather(1, never_below, near, total, upper, 1)
    left_top = shifted(right_top, "col", 1)
    for bit in range(row_bits):
        sums = sums + swapped(sums, "row", 1 << bit)
    sums, left_top = tied(sums, left_top)
    field = renew(field, dense, total, top, left_top, left_rest)
    probe = illuminate(col_bits, sums, probe)
    for bit in reversed(range(col_bits)):
        other = swapped(probe, "col", 1 << bit)
        if bit == 1:
            other, field = tied(other, field)
        probe = join(bit, probe, other)
    return field, probe


def solution(mesh):
    placed = (
        P(None, "row", "col"),
        P(),
        P("row", "col", None, None, None, None),
        P("row", "col", None, None, None),
    )

    def whole(object_field, probe, amplitudes, offsets):
        table = jnp.asarray(dft_tables(probe.shape[1]))
        body = jax.shard_map(
            local,
            mesh=mesh,
            in_specs=(P(),) + placed,
            out_specs=(P(None, "row", "col"), P()),
            check_vma=False,
        )
        return body(table, object_field, probe, amplitudes, offsets)

    return whole
```

```python
import functools
import math

import jax
import jax.numpy as jnp
import ml_dtypes
import numpy as np
from jax import lax
from jax.experimental import pallas as pl
from jax.experimental.pallas import tpu as pltpu
from jax.sharding import PartitionSpec as P

softening = 0.1
object_damping = 0.5
probe_damping = 1.0
MIB = 1 << 20
lane = 128
SCAN_LIMIT = 24 * MIB
VMEM = pltpu.VMEM
SMEM = pltpu.SMEM


def shifted(array, axis, by):
    peers = lax.axis_size(axis)
    return lax.ppermute(array, axis, [(i, (i + by) % peers) for i in range(peers)])


def swapped(array, axis, mask):
    peers = lax.axis_size(axis)
    return lax.ppermute(array, axis, [(i, i ^ mask) for i in range(peers)])


def handed_on(array, axis):
    peers = lax.axis_size(axis)
    pairs = [(i, i + 2 - 4 * (i % 2)) for i in range(peers)]
    return lax.ppermute(array, axis, [(i, k) for i, k in pairs if 0 <= k < peers])


def swapped_outward(array, axis):
    peers = lax.axis_size(axis)
    pairs = [(i, i + 1) for i in range(1, peers - 1, 2)]
    return lax.ppermute(array, axis, pairs + [(k, i) for i, k in pairs])


def dft_tables(length):
    half = length // 2
    index = np.arange(half)
    parts = []
    for odd in range(2):
        phase = ((2 * index[:, None] + odd) * index[None, :] % length) * (2.0 * math.pi / length)
        real, imag = np.cos(phase) / math.sqrt(length), -np.sin(phase) / math.sqrt(length)
        full = np.block([[real, -imag], [imag, real]])
        for value in (full, full.T):
            high = value.astype(ml_dtypes.bfloat16)
            parts += [high, (value - high.astype(np.float64)).astype(ml_dtypes.bfloat16)]
    return np.stack(parts)


def halves(value):
    high = value.astype(jnp.bfloat16)
    return high, (value - high.astype(jnp.float32)).astype(jnp.bfloat16)


def product(a, b):
    return jnp.dot(a, b, preferred_element_type=jnp.float32)


def left_product(table_ref, number, data):
    top, rest = halves(data)
    high, low = table_ref[2 * number], table_ref[2 * number + 1]
    return product(high, top) + product(high, rest) + product(low, top)


def right_product(data, table_ref, number):
    top, rest = halves(data)
    high, low = table_ref[2 * number], table_ref[2 * number + 1]
    return product(top, high) + product(rest, high) + product(top, low)


def stacked(values, axis):
    return jnp.concatenate(values, axis=axis)


def forward(table_ref, real, imag):
    half = real.shape[0] // 2
    even = stacked([real[:half] + real[half:], imag[:half] + imag[half:]], 0)
    odd = stacked([real[:half] - real[half:], imag[:half] - imag[half:]], 0)
    even, odd = left_product(table_ref, 0, even), left_product(table_ref, 2, odd)
    real, imag = stacked([even[:half], odd[:half]], 0), stacked([even[half:], odd[half:]], 0)
    even = stacked([real[:, :half] + real[:, half:], imag[:, :half] + imag[:, half:]], 1)
    odd = stacked([real[:, :half] - real[:, half:], imag[:, :half] - imag[:, half:]], 1)
    even, odd = right_product(even, table_ref, 1), right_product(odd, table_ref, 3)
    return stacked([even[:, :half], odd[:, :half]], 1), stacked([even[:, half:], odd[:, half:]], 1)


def backward(table_ref, real, imag):
    half = real.shape[0] // 2
    even = left_product(table_ref, 1, stacked([real[:half], imag[:half]], 0))
    odd = left_product(table_ref, 3, stacked([real[half:], imag[half:]], 0))
    one, two = even + odd, even - odd
    real, imag = stacked([one[:half], two[:half]], 0), stacked([one[half:], two[half:]], 0)
    even = right_product(stacked([real[:, :half], imag[:, :half]], 1), table_ref, 0)
    odd = right_product(stacked([real[:, half:], imag[:, half:]], 1), table_ref, 2)
    one, two = even + odd, even - odd
    return stacked([one[:, :half], two[:, :half]], 1), stacked([one[:, half:], two[:, half:]], 1)


def reorder_kernel(amplitude_ref, out_ref):
    side = amplitude_ref.shape[3]
    half = side // 2

    def choice(axis):
        target = lax.broadcasted_iota(jnp.int32, (side, side), axis)
        source = lax.broadcasted_iota(jnp.int32, (side, side), 1 - axis)
        wanted = jnp.where(target < half, 2 * target, 2 * (target - half) + 1)
        return jnp.where(source == wanted, 1.0, 0.0).astype(jnp.bfloat16)

    rows, cols = choice(0), choice(1)
    for sweep in range(amplitude_ref.shape[0]):
        for scan in range(amplitude_ref.shape[1]):
            moved = product(rows, amplitude_ref[sweep, scan]).astype(jnp.bfloat16)
            out_ref[sweep, scan] = product(moved, cols).astype(jnp.bfloat16)


def reorder(amplitudes):
    return pl.pallas_call(
        reorder_kernel,
        out_shape=jax.ShapeDtypeStruct(amplitudes.shape, amplitudes.dtype),
        in_specs=[pl.BlockSpec(memory_space=VMEM)],
        out_specs=pl.BlockSpec(memory_space=VMEM),
        compiler_params=pltpu.CompilerParams(vmem_limit_bytes=8 * MIB),
        cost_estimate=pl.CostEstimate(flops=300_000_000, bytes_accessed=MIB, transcendentals=0),
        name="reorder",
    )(amplitudes)


def split_column(column):
    return lax.div(column, lane), lax.rem(column, lane)


def taken(ref, plane, row, column, side):
    first, shift = split_column(column)
    count = side // lane + 1
    slabs = [ref[plane, first + k, pl.ds(row, side), :] for k in range(count)]
    return pltpu.roll(jnp.concatenate(slabs, axis=1), count * lane - shift, 1)[:, :side]


def turned(value, shift):
    side = value.shape[0]
    wide = jnp.concatenate([value, jnp.zeros((side, lane), jnp.float32)], axis=1)
    return pltpu.roll(wide, shift, 1)


def add_slabs(ref, lead, row, first, wide):
    side = wide.shape[0]
    for k in range(wide.shape[1] // lane):
        spot = lead + (first + k, pl.ds(row, side), slice(None))
        ref[spot] += wide[:, k * lane : (k + 1) * lane]


def columns(number):
    return slice(number * lane, (number + 1) * lane)


def whole_spec(count):
    return [pl.BlockSpec(memory_space=VMEM)] * count


def offsets_spec():
    return pl.BlockSpec(memory_space=SMEM)


def shape_of(*dims):
    return jax.ShapeDtypeStruct(dims, jnp.float32)


def cost(flops, moved):
    return pl.CostEstimate(flops=flops, bytes_accessed=moved, transcendentals=0)


def corner_of(offsets_ref, down, along, sweep, scan):
    spot = (down + 1, along + 1, sweep, scan)
    return offsets_ref[spot + (0,)], offsets_ref[spot + (1,)]


def halves_of(bit, half):
    mine = lax.rem(lax.axis_index("col") >> bit, 2)
    kept = pl.ds(pl.multiple_of(mine * half, 8), half)
    return kept, pl.ds(pl.multiple_of((1 - mine) * half, 8), half)


def scan_kernel(sweep, last, counts, offsets_ref, *refs):
    inputs, outputs, scratch = counts
    probe_hbm, amplitude_hbm, table_hbm = refs[:3]
    field_in = refs[3:inputs]
    outs_hbm = refs[inputs : inputs + outputs]
    rest = refs[inputs + outputs :]
    probe_ref, amplitude_ref, table_ref, sums_ref, windows_ref = rest[:5]
    small_sem, field_sem, out_sem = rest[5:8]
    side = probe_ref.shape[1]
    copies = []

    def fetch(source, target):
        copies.append(pltpu.make_async_copy(source, target, field_sem))

    small = [
        pltpu.make_async_copy(table_hbm, table_ref, small_sem.at[0]),
        pltpu.make_async_copy(probe_hbm, probe_ref, small_sem.at[1]),
        pltpu.make_async_copy(amplitude_hbm.at[sweep], amplitude_ref, small_sem.at[2]),
    ]
    if last:
        field_ref = field_in[0]
    else:
        own_hbm, right_hbm, first_hbm, second_hbm, corner_hbm = field_in
        field_ref = rest[8]
        rows, edge = own_hbm.shape[1], side // lane
        slabs = own_hbm.shape[2] // lane
        for k in range(slabs):
            fetch(own_hbm.at[:, :, columns(k)], field_ref.at[:, k, :rows])
        for k in range(edge):
            fetch(right_hbm.at[:, :, columns(k)], field_ref.at[:, slabs + k, :rows])
            fetch(first_hbm.at[:, :, columns(k)], field_ref.at[:, k, rows:])
            fetch(corner_hbm.at[:, :, columns(k)], field_ref.at[:, slabs + k, rows:])
        for k in range(edge, slabs):
            fetch(second_hbm.at[:, :, columns(k - edge)], field_ref.at[:, k, rows:])
    small[0].start()
    for copy in copies:
        copy.start()
    for copy in small[1:]:
        copy.start()
    small[0].wait()
    for copy in small[1:]:
        copy.wait()
    for copy in copies:
        copy.wait()
    probe_real, probe_imag = probe_ref[0], probe_ref[1]
    pending = []
    for scan in range(2):
        row, column = offsets_ref[0, 0, sweep, scan, 0], offsets_ref[0, 0, sweep, scan, 1]
        patch_real = taken(field_ref, 0, row, column, side)
        patch_imag = taken(field_ref, 1, row, column, side)
        wave_real = probe_real * patch_real - probe_imag * patch_imag
        wave_imag = probe_real * patch_imag + probe_imag * patch_real
        far_real, far_imag = forward(table_ref, wave_real, wave_imag)
        scale = amplitude_ref[scan].astype(jnp.float32) * lax.rsqrt(
            far_real * far_real + far_imag * far_imag + softening
        )
        back_real, back_imag = backward(table_ref, far_real * scale, far_imag * scale)
        diff_real = back_real - wave_real
        diff_imag = back_imag - wave_imag
        term_real = probe_real * diff_real + probe_imag * diff_imag
        term_imag = probe_real * diff_imag - probe_imag * diff_real
        windows_ref[scan, 0] = term_real
        windows_ref[scan, 1] = term_imag
        copy = pltpu.make_async_copy(windows_ref.at[scan], outs_hbm[2].at[scan], out_sem)
        copy.start()
        pending.append(copy)
        sums = (
            patch_real * diff_real + patch_imag * diff_imag,
            patch_real * diff_imag - patch_imag * diff_real,
            patch_real * patch_real + patch_imag * patch_imag,
        )
        for number, value in enumerate(sums):
            if scan == 0:
                sums_ref[number] = value
            else:
                sums_ref[number] += value
    kept, sent = halves_of(0, outs_hbm[0].shape[1])
    outs = [(sums_ref.at[:, sent], outs_hbm[1]), (sums_ref.at[:, kept], outs_hbm[0])]
    outs = [pltpu.make_async_copy(source, target, out_sem) for source, target in outs]
    for copy in outs:
        copy.start()
    for copy in pending + outs:
        copy.wait()


def scan_step(sweep, last, offsets, probe, amplitudes, table, *field):
    side = probe.shape[1]
    shapes = [shape_of(3, side // 2, side)] * 2 + [shape_of(2, 2, side, side)]
    scratch = [
        VMEM(probe.shape, jnp.float32),
        VMEM(amplitudes.shape[1:], amplitudes.dtype),
        VMEM(table.shape, table.dtype),
        VMEM((3, side, side), jnp.float32),
        VMEM((2, 2, side, side), jnp.float32),
        pltpu.SemaphoreType.DMA((3,)),
        pltpu.SemaphoreType.DMA,
        pltpu.SemaphoreType.DMA,
    ]
    if not last:
        rows, cols = field[0].shape[1:]
        scratch.append(VMEM((2, (cols + side) // lane, rows + side, lane), jnp.float32))
    anywhere = pl.BlockSpec(memory_space=pl.ANY)
    counts = (3 + len(field), len(shapes), len(scratch))
    return pl.pallas_call(
        functools.partial(scan_kernel, sweep, last, counts),
        out_shape=shapes,
        in_specs=[offsets_spec()] + [anywhere] * 3 + (whole_spec(1) if last else [anywhere] * len(field)),
        out_specs=[anywhere] * len(shapes),
        scratch_shapes=scratch,
        compiler_params=pltpu.CompilerParams(vmem_limit_bytes=SCAN_LIMIT),
        cost_estimate=cost(7_000_000_000, 12 * MIB),
        name="scan",
    )(offsets, probe, amplitudes, table, *field)


def edge_starts(count, slabs, edge):
    if count < 2:
        return [slabs - edge] * count
    odd = lax.rem(lax.axis_index("col"), 2)
    return [(1 - odd) * (slabs - edge), odd * (slabs - edge)]


def place_kernel(sweep, offsets_ref, windows_ref, total_ref, *edge_refs):
    side = windows_ref.shape[2]
    edge = side // lane
    slabs, height = total_ref.shape[1:3]
    total_ref[...] = jnp.zeros_like(total_ref)
    for scan in range(2):
        row, column = offsets_ref[0, 0, sweep, scan, 0], offsets_ref[0, 0, sweep, scan, 1]
        first, shift = split_column(column)
        for plane in range(2):
            add_slabs(total_ref, (plane,), row, first, turned(windows_ref[scan, plane], shift))
    for ref, start in zip(edge_refs, edge_starts(len(edge_refs), slabs, edge)):
        ref[...] = total_ref[:, pl.ds(start, edge), side : height - side]


def place(sweep, offsets, windows, tile, sides):
    side = windows.shape[2]
    edge = side // lane
    height, slabs = tile[0] + side, tile[1] // lane + edge
    shapes = [shape_of(2, slabs, height, lane)] + [shape_of(2, edge, height - 2 * side, lane)] * sides
    return pl.pallas_call(
        functools.partial(place_kernel, sweep),
        out_shape=shapes,
        in_specs=[offsets_spec()] + whole_spec(1),
        out_specs=whole_spec(len(shapes)),
        compiler_params=pltpu.CompilerParams(vmem_limit_bytes=4 * MIB),
        cost_estimate=cost(1_000_000, 6 * MIB),
        name="place",
    )(offsets, windows)


def density_kernel(sweep, reach, offsets_ref, probe_ref, out_ref, total_ref):
    side = probe_ref.shape[1]
    slabs, height = out_ref.shape[:2]
    breadth = slabs * lane
    tile = height - side if reach else height
    span = breadth - side if reach else breadth
    total_ref[...] = jnp.zeros_like(total_ref)
    power = probe_ref[0] * probe_ref[0] + probe_ref[1] * probe_ref[1]
    steps = (-1, 0, 1) if reach else (-1, 0)
    for down in steps:
        for along in steps:
            for scan in range(2):
                row, column = corner_of(offsets_ref, down, along, sweep, scan)
                row += side + down * tile
                column += side + along * span

                @pl.when((row > 0) & (row < side + height) & (column > 0) & (column < side + breadth))
                def _():
                    first, shift = split_column(column)
                    add_slabs(total_ref, (), row, first, turned(power, shift))

    out_ref[...] = total_ref[side // lane : side // lane + slabs, side : side + height]


def density(sweep, reach, offsets, probe, tile):
    side = probe.shape[1]
    extra = side if reach else 0
    height, slabs = tile[0] + extra, (tile[1] + extra) // lane
    return pl.pallas_call(
        functools.partial(density_kernel, sweep, reach),
        out_shape=shape_of(slabs, height, lane),
        in_specs=[offsets_spec()] + whole_spec(1),
        out_specs=whole_spec(1)[0],
        scratch_shapes=[VMEM((slabs + 2 * side // lane, height + 2 * side, lane), jnp.float32)],
        compiler_params=pltpu.CompilerParams(vmem_limit_bytes=10 * MIB),
        cost_estimate=cost(1_000_000, 6 * MIB),
        name="density",
    )(offsets, probe)


def gather_kernel(sweep, below_of, offsets_ref, total_ref, windows_ref, all_ref, *refs):
    edge_refs, strip_ref = refs[:-1], refs[-1]
    slabs, side = all_ref.shape[1:3]
    height = total_ref.shape[2]
    edge = side // lane
    below = below_of()
    strip_ref[...] = jnp.zeros_like(strip_ref)
    for scan in range(2):
        row, column = corner_of(offsets_ref, 2 * below - 1, -1, sweep, scan)
        row += (2 * below - 1) * side
        first, shift = split_column(column)

        @pl.when((row > 0) & (row < 2 * side))
        def _():
            for plane in range(2):
                add_slabs(strip_ref, (plane,), row, first, turned(windows_ref[scan, plane], shift))

    base = pl.multiple_of(below * (height - side), 8)
    for plane in range(2):
        for k in range(slabs):
            all_ref[plane, k] = strip_ref[plane, k, side : 2 * side] + total_ref[plane, k, pl.ds(base, side)]
    for ref, start in zip(edge_refs, edge_starts(len(edge_refs), slabs, edge)):
        ref[...] = all_ref[:, pl.ds(start, edge)]


def partner_below():
    return 1 - lax.rem(lax.axis_index("row"), 2)


def other_below():
    return lax.rem(lax.axis_index("row"), 2)


def never_below():
    return jnp.int32(0)


def gather(sweep, below_of, offsets, total, windows, sides):
    side = windows.shape[2]
    slabs = total.shape[1]
    return pl.pallas_call(
        functools.partial(gather_kernel, sweep, below_of),
        out_shape=[shape_of(2, slabs, side, lane)] + [shape_of(2, side // lane, side, lane)] * sides,
        in_specs=[offsets_spec()] + whole_spec(2),
        out_specs=whole_spec(1 + sides),
        scratch_shapes=[VMEM((2, slabs, 3 * side, lane), jnp.float32)],
        compiler_params=pltpu.CompilerParams(vmem_limit_bytes=8 * MIB),
        cost_estimate=cost(1_000_000, 6 * MIB),
        name="gather",
    )(offsets, total, windows)


def widen_kernel(*refs):
    own_ref, right_ref, first_ref, second_ref, corner_ref, density_ref, total_ref = refs[:7]
    near_ref, far_ref, inner_refs, outer_refs, out_ref = refs[7], refs[8], refs[9:12], refs[12:15], refs[15]
    side = near_ref.shape[2]
    edge = side // lane
    slabs = out_ref.shape[1] - edge
    rows = out_ref.shape[2] - side
    odd = lax.rem(lax.axis_index("row"), 2) == 1
    odd_col = lax.rem(lax.axis_index("col"), 2) == 1
    even_col = jnp.logical_not(odd_col)
    for k in range(slabs + edge):
        for top, bottom in ((0, side), (side, rows), (rows, rows + side)):
            part = 1.0 / (density_ref[k, top:bottom] + object_damping)
            for plane in range(2):
                if top == rows:
                    if k < edge:
                        before = first_ref[plane, :, columns(k)]
                    elif k < slabs:
                        before = second_ref[plane, :, columns(k - edge)]
                    else:
                        before = corner_ref[plane, :, columns(k - slabs)]
                elif k < slabs:
                    before = own_ref[plane, top:bottom, columns(k)]
                else:
                    before = right_ref[plane, top:bottom, columns(k - slabs)]

                def picked(near, far):
                    return jnp.where(odd, near, far) if top == 0 else jnp.where(odd, far, near)

                def beside(outward, at):
                    if top == side:
                        return jnp.where(outward, outer_refs[0][plane, at], inner_refs[0][plane, at])
                    near = jnp.where(outward, outer_refs[1][plane, at], inner_refs[1][plane, at])
                    far = jnp.where(outward, outer_refs[2][plane, at], inner_refs[2][plane, at])
                    return picked(near, far)

                if top == side:
                    terms = total_ref[plane, k, top:bottom]
                else:
                    terms = picked(near_ref[plane, k], far_ref[plane, k])
                if k < edge:
                    terms += beside(even_col, k)
                if k >= slabs:
                    terms += beside(odd_col, k - slabs)
                out_ref[plane, k, top:bottom] = before + terms * part


def widen(pieces, dense, total, near, far, inner, outer):
    return pl.pallas_call(
        widen_kernel,
        out_shape=shape_of(*total.shape),
        in_specs=whole_spec(15),
        out_specs=whole_spec(1)[0],
        compiler_params=pltpu.CompilerParams(vmem_limit_bytes=6 * MIB),
        cost_estimate=cost(4_000_000, 20 * MIB),
        name="widen",
    )(*pieces, dense, total, near, far, *inner, *outer)


def renew_kernel(field_ref, density_ref, total_ref, top_ref, left_top_ref, left_rest_ref, out_ref):
    slabs, rows = density_ref.shape[:2]
    edge, side = left_top_ref.shape[1:3]
    for k in range(slabs):
        part = 1.0 / (density_ref[k] + object_damping)
        for plane in range(2):
            top = top_ref[plane, k]
            rest = total_ref[plane, k, side:rows]
            if k < edge:
                top += left_top_ref[plane, k]
                rest += left_rest_ref[plane, k]
            out_ref[plane, :side, columns(k)] = field_ref[plane, k, :side] + top * part[:side]
            out_ref[plane, side:, columns(k)] = field_ref[plane, k, side:rows] + rest * part[side:]


def renew(field, dense, total, top, left_top, left_rest):
    slabs, rows = dense.shape[:2]
    return pl.pallas_call(
        renew_kernel,
        out_shape=shape_of(2, rows, slabs * lane),
        in_specs=whole_spec(6),
        out_specs=whole_spec(1)[0],
        compiler_params=pltpu.CompilerParams(vmem_limit_bytes=4 * MIB),
        cost_estimate=cost(4_000_000, 10 * MIB),
        name="renew",
    )(field, dense, total, top, left_top, left_rest)


def fold_kernel(bit, value_ref, came_ref, kept_ref, sent_ref, total_ref):
    total_ref[...] = value_ref[...] + came_ref[...]
    kept, sent = halves_of(bit, kept_ref.shape[1])
    kept_ref[...] = total_ref[:, kept]
    sent_ref[...] = total_ref[:, sent]


def fold(bit, value, came):
    planes, rows, side = value.shape
    return pl.pallas_call(
        functools.partial(fold_kernel, bit),
        out_shape=[shape_of(planes, rows // 2, side)] * 2,
        in_specs=whole_spec(2),
        out_specs=whole_spec(2),
        scratch_shapes=[VMEM(value.shape, jnp.float32)],
        compiler_params=pltpu.CompilerParams(vmem_limit_bytes=4 * MIB),
        cost_estimate=cost(100_000, MIB),
        name="fold",
    )(value, came)


def join_kernel(bit, value_ref, other_ref, out_ref):
    kept, sent = halves_of(bit, value_ref.shape[1])
    out_ref[:, kept] = value_ref[...]
    out_ref[:, sent] = other_ref[...]


def join(bit, value, other):
    planes, rows, side = value.shape
    return pl.pallas_call(
        functools.partial(join_kernel, bit),
        out_shape=shape_of(planes, 2 * rows, side),
        in_specs=whole_spec(2),
        out_specs=whole_spec(1)[0],
        compiler_params=pltpu.CompilerParams(vmem_limit_bytes=4 * MIB),
        cost_estimate=cost(100_000, MIB),
        name="join",
    )(value, other)


def illuminate_kernel(bits, sums_ref, probe_ref, out_ref):
    rows = sums_ref.shape[1]
    start, half = 0, probe_ref.shape[1]
    for bit in range(bits):
        half //= 2
        start += lax.rem(lax.axis_index("col") >> bit, 2) * half
    spot = pl.ds(pl.multiple_of(start, 8), rows)
    part = 1.0 / (sums_ref[2] + probe_damping)
    for plane in range(2):
        out_ref[plane] = probe_ref[plane, spot] + sums_ref[plane] * part


def illuminate(bits, sums, probe):
    return pl.pallas_call(
        functools.partial(illuminate_kernel, bits),
        out_shape=shape_of(2, *sums.shape[1:]),
        in_specs=whole_spec(2),
        out_specs=whole_spec(1)[0],
        compiler_params=pltpu.CompilerParams(vmem_limit_bytes=4 * MIB),
        cost_estimate=cost(100_000, MIB),
        name="illuminate",
    )(sums, probe)


def tied(*values):
    return lax.optimization_barrier(values)


def local(table, object_field, probe, amplitudes, offsets):
    side = probe.shape[1]
    tile = object_field.shape[1:]
    measured = reorder(amplitudes[0, 0])
    col_bits = int(math.log2(lax.axis_size("col")))
    row_bits = int(math.log2(lax.axis_size("row")))

    strip, rest = tied(object_field[:, :side, :side], object_field)
    first = shifted(strip, "row", -1)
    second = shifted(rest[:, :side, side:], "row", -1)
    right = shifted(object_field[:, :, :side], "col", -1)
    near = jnp.concatenate([shifted(offsets, "row", 1), offsets, shifted(offsets, "row", -1)], axis=0)
    first, near = tied(first, near)
    corner = shifted(first, "col", -1)
    pieces = (object_field, right, first, second, corner)

    kept, sent, own = scan_step(0, False, offsets, probe, measured, table, *pieces)
    total, middle_inner, middle_outer = place(0, offsets, own, tile, 2)
    around = jnp.concatenate([shifted(near, "col", 1), near, shifted(near, "col", -1)], axis=1)
    dense = density(0, True, around, probe, tile)
    partner = swapped(own, "row", 1)
    came = swapped(sent, "col", 1)
    for bit in range(1, col_bits):
        kept, sent = fold(bit, kept, came)
        came = swapped(sent, "col", 1 << bit)
    came, around = tied(came, around)
    sums = kept + came
    for bit in reversed(range(1, row_bits)):
        came = swapped(sums, "row", 1 << bit)
        if bit == row_bits - 1:
            came, dense, middle_inner, middle_outer = tied(came, dense, middle_inner, middle_outer)
        sums = sums + came
    inner_strips = [swapped(middle_inner, "col", 1)]
    outer_strips = [swapped_outward(middle_outer, "col")]
    sums, partner = tied(sums, partner)
    passed = handed_on(partner, "row")
    near_all, near_inner, near_outer = gather(0, partner_below, near, total, partner, 2)
    inner_strips.append(swapped(near_inner, "col", 1))
    outer_strips.append(swapped_outward(near_outer, "col"))
    sums = sums + swapped(sums, "row", 1)
    probe = illuminate(col_bits, sums, probe)
    for bit in reversed(range(col_bits)):
        other = swapped(probe, "col", 1 << bit)
        if bit == col_bits - 1:
            other, outer_strips[0], inner_strips[0] = tied(other, outer_strips[0], inner_strips[0])
        probe = join(bit, probe, other)
    passed, probe, outer_strips[1], inner_strips[1] = tied(passed, probe, outer_strips[1], inner_strips[1])
    far_all, far_inner, far_outer = gather(0, other_below, near, total, passed, 2)
    inner_strips.append(swapped(far_inner, "col", 1))
    outer_strips.append(swapped_outward(far_outer, "col"))
    field = widen(pieces, dense, total, near_all, far_all, inner_strips, outer_strips)

    kept, sent, own = scan_step(1, True, offsets, probe, measured, table, field)
    total, middle_right = place(1, offsets, own, tile, 1)
    dense = density(1, False, around, probe, tile)
    upper = shifted(own, "row", 1)
    came = swapped(sent, "col", 1)
    for bit in range(1, col_bits):
        kept, sent = fold(bit, kept, came)
        came = swapped(sent, "col", 1 << bit)
    came, middle_right, dense = tied(came, middle_right, dense)
    sums = kept + came
    left_rest = shifted(middle_right, "col", 1)
    sums, upper, left_rest = tied(sums, upper, left_rest)
    top, right_top = gather(1, never_below, near, total, upper, 1)
    left_top = shifted(right_top, "col", 1)
    for bit in range(row_bits):
        sums = sums + swapped(sums, "row", 1 << bit)
    sums, left_top = tied(sums, left_top)
    field = renew(field, dense, total, top, left_top, left_rest)
    probe = illuminate(col_bits, sums, probe)
    for bit in reversed(range(col_bits)):
        other = swapped(probe, "col", 1 << bit)
        if bit == 1:
            other, field = tied(other, field)
        probe = join(bit, probe, other)
    return field, probe


def solution(mesh):
    placed = (
        P(None, "row", "col"),
        P(),
        P("row", "col", None, None, None, None),
        P("row", "col", None, None, None),
    )

    def whole(object_field, probe, amplitudes, offsets):
        table = jnp.asarray(dft_tables(probe.shape[1]))
        body = jax.shard_map(
            local,
            mesh=mesh,
            in_specs=(P(),) + placed,
            out_specs=(P(None, "row", "col"), P()),
            check_vma=False,
        )
        return body(table, object_field, probe, amplitudes, offsets)

    return whole
```

```python
import functools
import math

import jax
import jax.numpy as jnp
import ml_dtypes
import numpy as np
from jax import lax
from jax.experimental import pallas as pl
from jax.experimental.pallas import tpu as pltpu
from jax.sharding import PartitionSpec as P

softening = 0.1
object_damping = 0.5
probe_damping = 1.0
MIB = 1 << 20
lane = 128
SCAN_LIMIT = 24 * MIB
VMEM = pltpu.VMEM
SMEM = pltpu.SMEM


def shifted(array, axis, by):
    peers = lax.axis_size(axis)
    return lax.ppermute(array, axis, [(i, (i + by) % peers) for i in range(peers)])


def moved_down(array):
    peers = lax.axis_size("row")
    return lax.ppermute(array, "row", [(i, i + 1) for i in range(peers - 1)])


def swapped(array, axis, mask):
    peers = lax.axis_size(axis)
    return lax.ppermute(array, axis, [(i, i ^ mask) for i in range(peers)])


def handed_on(array, axis):
    peers = lax.axis_size(axis)
    return lax.ppermute(array, axis, [(i, (i + 2 - 4 * (i % 2)) % peers) for i in range(peers)])


def swapped_outward(array, axis):
    peers = lax.axis_size(axis)
    pairs = [(i, i + 1) for i in range(1, peers - 1, 2)]
    return lax.ppermute(array, axis, pairs + [(k, i) for i, k in pairs])


def dft_tables(length):
    half = length // 2
    index = np.arange(half)
    parts = []
    for odd in range(2):
        phase = ((2 * index[:, None] + odd) * index[None, :] % length) * (2.0 * math.pi / length)
        real, imag = np.cos(phase) / math.sqrt(length), -np.sin(phase) / math.sqrt(length)
        full = np.block([[real, -imag], [imag, real]])
        for value in (full, full.T):
            high = value.astype(ml_dtypes.bfloat16)
            parts += [high, (value - high.astype(np.float64)).astype(ml_dtypes.bfloat16)]
    return np.stack(parts)


def halves(value):
    high = value.astype(jnp.bfloat16)
    return high, (value - high.astype(jnp.float32)).astype(jnp.bfloat16)


def product(a, b):
    return jnp.dot(a, b, preferred_element_type=jnp.float32)


def left_product(table_ref, number, data):
    top, rest = halves(data)
    high, low = table_ref[2 * number], table_ref[2 * number + 1]
    return product(high, top) + product(high, rest) + product(low, top)


def right_product(data, table_ref, number):
    top, rest = halves(data)
    high, low = table_ref[2 * number], table_ref[2 * number + 1]
    return product(top, high) + product(rest, high) + product(top, low)


def stacked(values, axis):
    return jnp.concatenate(values, axis=axis)


def forward(table_ref, real, imag):
    half = real.shape[0] // 2
    even = stacked([real[:half] + real[half:], imag[:half] + imag[half:]], 0)
    odd = stacked([real[:half] - real[half:], imag[:half] - imag[half:]], 0)
    even, odd = left_product(table_ref, 0, even), left_product(table_ref, 2, odd)
    real, imag = stacked([even[:half], odd[:half]], 0), stacked([even[half:], odd[half:]], 0)
    even = stacked([real[:, :half] + real[:, half:], imag[:, :half] + imag[:, half:]], 1)
    odd = stacked([real[:, :half] - real[:, half:], imag[:, :half] - imag[:, half:]], 1)
    even, odd = right_product(even, table_ref, 1), right_product(odd, table_ref, 3)
    return stacked([even[:, :half], odd[:, :half]], 1), stacked([even[:, half:], odd[:, half:]], 1)


def backward(table_ref, real, imag):
    half = real.shape[0] // 2
    even = left_product(table_ref, 1, stacked([real[:half], imag[:half]], 0))
    odd = left_product(table_ref, 3, stacked([real[half:], imag[half:]], 0))
    one, two = even + odd, even - odd
    real, imag = stacked([one[:half], two[:half]], 0), stacked([one[half:], two[half:]], 0)
    even = right_product(stacked([real[:, :half], imag[:, :half]], 1), table_ref, 0)
    odd = right_product(stacked([real[:, half:], imag[:, half:]], 1), table_ref, 2)
    one, two = even + odd, even - odd
    return stacked([one[:, :half], two[:, :half]], 1), stacked([one[:, half:], two[:, half:]], 1)


def reorder_kernel(amplitude_ref, out_ref):
    side = amplitude_ref.shape[3]
    half = side // 2

    def choice(axis):
        target = lax.broadcasted_iota(jnp.int32, (side, side), axis)
        source = lax.broadcasted_iota(jnp.int32, (side, side), 1 - axis)
        wanted = jnp.where(target < half, 2 * target, 2 * (target - half) + 1)
        return jnp.where(source == wanted, 1.0, 0.0).astype(jnp.bfloat16)

    rows, cols = choice(0), choice(1)
    for sweep in range(amplitude_ref.shape[0]):
        for scan in range(amplitude_ref.shape[1]):
            moved = product(rows, amplitude_ref[sweep, scan]).astype(jnp.bfloat16)
            out_ref[sweep, scan] = product(moved, cols).astype(jnp.bfloat16)


def reorder(amplitudes):
    return pl.pallas_call(
        reorder_kernel,
        out_shape=jax.ShapeDtypeStruct(amplitudes.shape, amplitudes.dtype),
        in_specs=[pl.BlockSpec(memory_space=VMEM)],
        out_specs=pl.BlockSpec(memory_space=VMEM),
        compiler_params=pltpu.CompilerParams(vmem_limit_bytes=8 * MIB),
        cost_estimate=pl.CostEstimate(flops=300_000_000, bytes_accessed=MIB, transcendentals=0),
        name="reorder",
    )(amplitudes)


def split_column(column):
    return lax.div(column, lane), lax.rem(column, lane)


def taken(ref, plane, row, column, side):
    first, shift = split_column(column)
    count = side // lane + 1
    slabs = [ref[plane, first + k, pl.ds(row, side), :] for k in range(count)]
    return pltpu.roll(jnp.concatenate(slabs, axis=1), count * lane - shift, 1)[:, :side]


def turned(value, shift):
    side = value.shape[0]
    wide = jnp.concatenate([value, jnp.zeros((side, lane), jnp.float32)], axis=1)
    return pltpu.roll(wide, shift, 1)


def add_slabs(ref, lead, row, first, wide):
    side = wide.shape[0]
    for k in range(wide.shape[1] // lane):
        spot = lead + (first + k, pl.ds(row, side), slice(None))
        ref[spot] += wide[:, k * lane : (k + 1) * lane]


def columns(number):
    return slice(number * lane, (number + 1) * lane)


def whole_spec(count):
    return [pl.BlockSpec(memory_space=VMEM)] * count


def offsets_spec():
    return pl.BlockSpec(memory_space=SMEM)


def shape_of(*dims):
    return jax.ShapeDtypeStruct(dims, jnp.float32)


def cost(flops, moved):
    return pl.CostEstimate(flops=flops, bytes_accessed=moved, transcendentals=0)


def corner_of(offsets_ref, down, along, sweep, scan):
    spot = (down + 1, along + 1, sweep, scan)
    return offsets_ref[spot + (0,)], offsets_ref[spot + (1,)]


def halves_of(bit, half):
    mine = lax.rem(lax.axis_index("col") >> bit, 2)
    kept = pl.ds(pl.multiple_of(mine * half, 8), half)
    return kept, pl.ds(pl.multiple_of((1 - mine) * half, 8), half)


def scan_kernel(sweep, last, counts, offsets_ref, *refs):
    inputs, outputs, scratch = counts
    probe_hbm, amplitude_hbm, table_hbm = refs[:3]
    field_in = refs[3:inputs]
    outs_hbm = refs[inputs : inputs + outputs]
    rest = refs[inputs + outputs :]
    probe_ref, amplitude_ref, table_ref, sums_ref, windows_ref = rest[:5]
    small_sem, field_sem, out_sem = rest[5:8]
    side = probe_ref.shape[1]
    copies = []

    def fetch(source, target):
        copies.append(pltpu.make_async_copy(source, target, field_sem))

    small = [
        pltpu.make_async_copy(table_hbm, table_ref, small_sem.at[0]),
        pltpu.make_async_copy(probe_hbm, probe_ref, small_sem.at[1]),
        pltpu.make_async_copy(amplitude_hbm.at[sweep], amplitude_ref, small_sem.at[2]),
    ]
    if last:
        field_ref = field_in[0]
    else:
        own_hbm, right_hbm, first_hbm, second_hbm, corner_hbm = field_in
        field_ref = rest[8]
        rows, edge = own_hbm.shape[1], side // lane
        slabs = own_hbm.shape[2] // lane
        for k in range(slabs):
            fetch(own_hbm.at[:, :, columns(k)], field_ref.at[:, k, :rows])
        for k in range(edge):
            fetch(right_hbm.at[:, :, columns(k)], field_ref.at[:, slabs + k, :rows])
            fetch(first_hbm.at[:, :, columns(k)], field_ref.at[:, k, rows:])
            fetch(corner_hbm.at[:, :, columns(k)], field_ref.at[:, slabs + k, rows:])
        for k in range(edge, slabs):
            fetch(second_hbm.at[:, :, columns(k - edge)], field_ref.at[:, k, rows:])
    small[0].start()
    for copy in copies:
        copy.start()
    for copy in small[1:]:
        copy.start()
    small[0].wait()
    for copy in small[1:]:
        copy.wait()
    for copy in copies:
        copy.wait()
    probe_real, probe_imag = probe_ref[0], probe_ref[1]
    pending = []
    for scan in range(2):
        row, column = offsets_ref[0, 0, sweep, scan, 0], offsets_ref[0, 0, sweep, scan, 1]
        patch_real = taken(field_ref, 0, row, column, side)
        patch_imag = taken(field_ref, 1, row, column, side)
        wave_real = probe_real * patch_real - probe_imag * patch_imag
        wave_imag = probe_real * patch_imag + probe_imag * patch_real
        far_real, far_imag = forward(table_ref, wave_real, wave_imag)
        scale = amplitude_ref[scan].astype(jnp.float32) * lax.rsqrt(
            far_real * far_real + far_imag * far_imag + softening
        )
        back_real, back_imag = backward(table_ref, far_real * scale, far_imag * scale)
        diff_real = back_real - wave_real
        diff_imag = back_imag - wave_imag
        term_real = probe_real * diff_real + probe_imag * diff_imag
        term_imag = probe_real * diff_imag - probe_imag * diff_real
        windows_ref[scan, 0] = term_real
        windows_ref[scan, 1] = term_imag
        copy = pltpu.make_async_copy(windows_ref.at[scan], outs_hbm[2].at[scan], out_sem)
        copy.start()
        pending.append(copy)
        sums = (
            patch_real * diff_real + patch_imag * diff_imag,
            patch_real * diff_imag - patch_imag * diff_real,
            patch_real * patch_real + patch_imag * patch_imag,
        )
        for number, value in enumerate(sums):
            if scan == 0:
                sums_ref[number] = value
            else:
                sums_ref[number] += value
    kept, sent = halves_of(0, outs_hbm[0].shape[1])
    outs = [(sums_ref.at[:, sent], outs_hbm[1]), (sums_ref.at[:, kept], outs_hbm[0])]
    outs = [pltpu.make_async_copy(source, target, out_sem) for source, target in outs]
    for copy in outs:
        copy.start()
    for copy in pending + outs:
        copy.wait()


def scan_step(sweep, last, offsets, probe, amplitudes, table, *field):
    side = probe.shape[1]
    shapes = [shape_of(3, side // 2, side)] * 2 + [shape_of(2, 2, side, side)]
    scratch = [
        VMEM(probe.shape, jnp.float32),
        VMEM(amplitudes.shape[1:], amplitudes.dtype),
        VMEM(table.shape, table.dtype),
        VMEM((3, side, side), jnp.float32),
        VMEM((2, 2, side, side), jnp.float32),
        pltpu.SemaphoreType.DMA((3,)),
        pltpu.SemaphoreType.DMA,
        pltpu.SemaphoreType.DMA,
    ]
    if not last:
        rows, cols = field[0].shape[1:]
        scratch.append(VMEM((2, (cols + side) // lane, rows + side, lane), jnp.float32))
    anywhere = pl.BlockSpec(memory_space=pl.ANY)
    counts = (3 + len(field), len(shapes), len(scratch))
    return pl.pallas_call(
        functools.partial(scan_kernel, sweep, last, counts),
        out_shape=shapes,
        in_specs=[offsets_spec()] + [anywhere] * 3 + (whole_spec(1) if last else [anywhere] * len(field)),
        out_specs=[anywhere] * len(shapes),
        scratch_shapes=scratch,
        compiler_params=pltpu.CompilerParams(vmem_limit_bytes=SCAN_LIMIT),
        cost_estimate=cost(7_000_000_000, 12 * MIB),
        name="scan",
    )(offsets, probe, amplitudes, table, *field)


def edge_starts(count, slabs, edge):
    if count < 2:
        return [slabs - edge] * count
    odd = lax.rem(lax.axis_index("col"), 2)
    return [(1 - odd) * (slabs - edge), odd * (slabs - edge)]


def place_kernel(sweep, offsets_ref, windows_ref, total_ref, *edge_refs):
    side = windows_ref.shape[2]
    edge = side // lane
    slabs, height = total_ref.shape[1:3]
    total_ref[...] = jnp.zeros_like(total_ref)
    for scan in range(2):
        row, column = offsets_ref[0, 0, sweep, scan, 0], offsets_ref[0, 0, sweep, scan, 1]
        first, shift = split_column(column)
        for plane in range(2):
            add_slabs(total_ref, (plane,), row, first, turned(windows_ref[scan, plane], shift))
    for ref, start in zip(edge_refs, edge_starts(len(edge_refs), slabs, edge)):
        ref[...] = total_ref[:, pl.ds(start, edge), side : height - side]


def place(sweep, offsets, windows, tile, sides):
    side = windows.shape[2]
    edge = side // lane
    height, slabs = tile[0] + side, tile[1] // lane + edge
    shapes = [shape_of(2, slabs, height, lane)] + [shape_of(2, edge, height - 2 * side, lane)] * sides
    return pl.pallas_call(
        functools.partial(place_kernel, sweep),
        out_shape=shapes,
        in_specs=[offsets_spec()] + whole_spec(1),
        out_specs=whole_spec(len(shapes)),
        compiler_params=pltpu.CompilerParams(vmem_limit_bytes=4 * MIB),
        cost_estimate=cost(1_000_000, 6 * MIB),
        name="place",
    )(offsets, windows)


def density_kernel(sweep, reach, offsets_ref, probe_ref, out_ref, total_ref):
    side = probe_ref.shape[1]
    slabs, height = out_ref.shape[:2]
    breadth = slabs * lane
    tile = height - side if reach else height
    span = breadth - side if reach else breadth
    total_ref[...] = jnp.zeros_like(total_ref)
    power = probe_ref[0] * probe_ref[0] + probe_ref[1] * probe_ref[1]
    steps = (-1, 0, 1) if reach else (-1, 0)
    for down in steps:
        for along in steps:
            for scan in range(2):
                row, column = corner_of(offsets_ref, down, along, sweep, scan)
                row += side + down * tile
                column += side + along * span

                @pl.when((row > 0) & (row < side + height) & (column > 0) & (column < side + breadth))
                def _():
                    first, shift = split_column(column)
                    add_slabs(total_ref, (), row, first, turned(power, shift))

    out_ref[...] = total_ref[side // lane : side // lane + slabs, side : side + height]


def density(sweep, reach, offsets, probe, tile):
    side = probe.shape[1]
    extra = side if reach else 0
    height, slabs = tile[0] + extra, (tile[1] + extra) // lane
    return pl.pallas_call(
        functools.partial(density_kernel, sweep, reach),
        out_shape=shape_of(slabs, height, lane),
        in_specs=[offsets_spec()] + whole_spec(1),
        out_specs=whole_spec(1)[0],
        scratch_shapes=[VMEM((slabs + 2 * side // lane, height + 2 * side, lane), jnp.float32)],
        compiler_params=pltpu.CompilerParams(vmem_limit_bytes=10 * MIB),
        cost_estimate=cost(1_000_000, 6 * MIB),
        name="density",
    )(offsets, probe)


def gather_kernel(sweep, below_of, offsets_ref, total_ref, windows_ref, all_ref, *refs):
    edge_refs, strip_ref = refs[:-1], refs[-1]
    slabs, side = all_ref.shape[1:3]
    height = total_ref.shape[2]
    edge = side // lane
    below = below_of()
    strip_ref[...] = jnp.zeros_like(strip_ref)
    for scan in range(2):
        row, column = corner_of(offsets_ref, 2 * below - 1, -1, sweep, scan)
        row += (2 * below - 1) * side
        first, shift = split_column(column)

        @pl.when((row > 0) & (row < 2 * side))
        def _():
            for plane in range(2):
                add_slabs(strip_ref, (plane,), row, first, turned(windows_ref[scan, plane], shift))

    base = pl.multiple_of(below * (height - side), 8)
    for plane in range(2):
        for k in range(slabs):
            all_ref[plane, k] = strip_ref[plane, k, side : 2 * side] + total_ref[plane, k, pl.ds(base, side)]
    for ref, start in zip(edge_refs, edge_starts(len(edge_refs), slabs, edge)):
        ref[...] = all_ref[:, pl.ds(start, edge)]


def partner_below():
    return 1 - lax.rem(lax.axis_index("row"), 2)


def other_below():
    return lax.rem(lax.axis_index("row"), 2)


def never_below():
    return jnp.int32(0)


def gather(sweep, below_of, offsets, total, windows, sides):
    side = windows.shape[2]
    slabs = total.shape[1]
    return pl.pallas_call(
        functools.partial(gather_kernel, sweep, below_of),
        out_shape=[shape_of(2, slabs, side, lane)] + [shape_of(2, side // lane, side, lane)] * sides,
        in_specs=[offsets_spec()] + whole_spec(2),
        out_specs=whole_spec(1 + sides),
        scratch_shapes=[VMEM((2, slabs, 3 * side, lane), jnp.float32)],
        compiler_params=pltpu.CompilerParams(vmem_limit_bytes=8 * MIB),
        cost_estimate=cost(1_000_000, 6 * MIB),
        name="gather",
    )(offsets, total, windows)


def widen_kernel(*refs):
    own_ref, right_ref, first_ref, second_ref, corner_ref, density_ref, total_ref = refs[:7]
    near_ref, far_ref, inner_refs, outer_refs, out_ref = refs[7], refs[8], refs[9:12], refs[12:15], refs[15]
    side = near_ref.shape[2]
    edge = side // lane
    slabs = out_ref.shape[1] - edge
    rows = out_ref.shape[2] - side
    odd = lax.rem(lax.axis_index("row"), 2) == 1
    odd_col = lax.rem(lax.axis_index("col"), 2) == 1
    even_col = jnp.logical_not(odd_col)
    for k in range(slabs + edge):
        for top, bottom in ((0, side), (side, rows), (rows, rows + side)):
            part = 1.0 / (density_ref[k, top:bottom] + object_damping)
            for plane in range(2):
                if top == rows:
                    if k < edge:
                        before = first_ref[plane, :, columns(k)]
                    elif k < slabs:
                        before = second_ref[plane, :, columns(k - edge)]
                    else:
                        before = corner_ref[plane, :, columns(k - slabs)]
                elif k < slabs:
                    before = own_ref[plane, top:bottom, columns(k)]
                else:
                    before = right_ref[plane, top:bottom, columns(k - slabs)]

                def picked(near, far):
                    return jnp.where(odd, near, far) if top == 0 else jnp.where(odd, far, near)

                def beside(outward, at):
                    if top == side:
                        return jnp.where(outward, outer_refs[0][plane, at], inner_refs[0][plane, at])
                    near = jnp.where(outward, outer_refs[1][plane, at], inner_refs[1][plane, at])
                    far = jnp.where(outward, outer_refs[2][plane, at], inner_refs[2][plane, at])
                    return picked(near, far)

                if top == side:
                    terms = total_ref[plane, k, top:bottom]
                else:
                    terms = picked(near_ref[plane, k], far_ref[plane, k])
                if k < edge:
                    terms += beside(even_col, k)
                if k >= slabs:
                    terms += beside(odd_col, k - slabs)
                out_ref[plane, k, top:bottom] = before + terms * part


def widen(pieces, dense, total, near, far, inner, outer):
    return pl.pallas_call(
        widen_kernel,
        out_shape=shape_of(*total.shape),
        in_specs=whole_spec(15),
        out_specs=whole_spec(1)[0],
        compiler_params=pltpu.CompilerParams(vmem_limit_bytes=6 * MIB),
        cost_estimate=cost(4_000_000, 20 * MIB),
        name="widen",
    )(*pieces, dense, total, near, far, *inner, *outer)


def renew_kernel(field_ref, density_ref, total_ref, top_ref, left_top_ref, left_rest_ref, out_ref):
    slabs, rows = density_ref.shape[:2]
    edge, side = left_top_ref.shape[1:3]
    for k in range(slabs):
        part = 1.0 / (density_ref[k] + object_damping)
        for plane in range(2):
            top = top_ref[plane, k]
            rest = total_ref[plane, k, side:rows]
            if k < edge:
                top += left_top_ref[plane, k]
                rest += left_rest_ref[plane, k]
            out_ref[plane, :side, columns(k)] = field_ref[plane, k, :side] + top * part[:side]
            out_ref[plane, side:, columns(k)] = field_ref[plane, k, side:rows] + rest * part[side:]


def renew(field, dense, total, top, left_top, left_rest):
    slabs, rows = dense.shape[:2]
    return pl.pallas_call(
        renew_kernel,
        out_shape=shape_of(2, rows, slabs * lane),
        in_specs=whole_spec(6),
        out_specs=whole_spec(1)[0],
        compiler_params=pltpu.CompilerParams(vmem_limit_bytes=4 * MIB),
        cost_estimate=cost(4_000_000, 10 * MIB),
        name="renew",
    )(field, dense, total, top, left_top, left_rest)


def fold_kernel(bit, value_ref, came_ref, kept_ref, sent_ref, total_ref):
    total_ref[...] = value_ref[...] + came_ref[...]
    kept, sent = halves_of(bit, kept_ref.shape[1])
    kept_ref[...] = total_ref[:, kept]
    sent_ref[...] = total_ref[:, sent]


def fold(bit, value, came):
    planes, rows, side = value.shape
    return pl.pallas_call(
        functools.partial(fold_kernel, bit),
        out_shape=[shape_of(planes, rows // 2, side)] * 2,
        in_specs=whole_spec(2),
        out_specs=whole_spec(2),
        scratch_shapes=[VMEM(value.shape, jnp.float32)],
        compiler_params=pltpu.CompilerParams(vmem_limit_bytes=4 * MIB),
        cost_estimate=cost(100_000, MIB),
        name="fold",
    )(value, came)


def join_kernel(bit, value_ref, other_ref, out_ref):
    kept, sent = halves_of(bit, value_ref.shape[1])
    out_ref[:, kept] = value_ref[...]
    out_ref[:, sent] = other_ref[...]


def join(bit, value, other):
    planes, rows, side = value.shape
    return pl.pallas_call(
        functools.partial(join_kernel, bit),
        out_shape=shape_of(planes, 2 * rows, side),
        in_specs=whole_spec(2),
        out_specs=whole_spec(1)[0],
        compiler_params=pltpu.CompilerParams(vmem_limit_bytes=4 * MIB),
        cost_estimate=cost(100_000, MIB),
        name="join",
    )(value, other)


def illuminate_kernel(bits, sums_ref, probe_ref, out_ref):
    rows = sums_ref.shape[1]
    start, half = 0, probe_ref.shape[1]
    for bit in range(bits):
        half //= 2
        start += lax.rem(lax.axis_index("col") >> bit, 2) * half
    spot = pl.ds(pl.multiple_of(start, 8), rows)
    part = 1.0 / (sums_ref[2] + probe_damping)
    for plane in range(2):
        out_ref[plane] = probe_ref[plane, spot] + sums_ref[plane] * part


def illuminate(bits, sums, probe):
    return pl.pallas_call(
        functools.partial(illuminate_kernel, bits),
        out_shape=shape_of(2, *sums.shape[1:]),
        in_specs=whole_spec(2),
        out_specs=whole_spec(1)[0],
        compiler_params=pltpu.CompilerParams(vmem_limit_bytes=4 * MIB),
        cost_estimate=cost(100_000, MIB),
        name="illuminate",
    )(sums, probe)


def tied(*values):
    return lax.optimization_barrier(values)


def local(table, object_field, probe, amplitudes, offsets):
    side = probe.shape[1]
    tile = object_field.shape[1:]
    measured = reorder(amplitudes[0, 0])
    col_bits = int(math.log2(lax.axis_size("col")))
    row_bits = int(math.log2(lax.axis_size("row")))

    strip, rest = tied(object_field[:, :side, :side], object_field)
    first = shifted(strip, "row", -1)
    second = shifted(rest[:, :side, side:], "row", -1)
    right = shifted(object_field[:, :, :side], "col", -1)
    near = jnp.concatenate([shifted(offsets, "row", 1), offsets, shifted(offsets, "row", -1)], axis=0)
    first, near = tied(first, near)
    corner = shifted(first, "col", -1)
    pieces = (object_field, right, first, second, corner)

    kept, sent, own = scan_step(0, False, offsets, probe, measured, table, *pieces)
    total, middle_inner, middle_outer = place(0, offsets, own, tile, 2)
    around = jnp.concatenate([shifted(near, "col", 1), near, shifted(near, "col", -1)], axis=1)
    dense = density(0, True, around, probe, tile)
    partner = swapped(own, "row", 1)
    came = swapped(sent, "col", 1)
    for bit in range(1, col_bits):
        kept, sent = fold(bit, kept, came)
        came = swapped(sent, "col", 1 << bit)
    came, around = tied(came, around)
    sums = kept + came
    for bit in reversed(range(1, row_bits)):
        came = swapped(sums, "row", 1 << bit)
        if bit == row_bits - 1:
            came, dense, middle_inner, middle_outer = tied(came, dense, middle_inner, middle_outer)
        sums = sums + came
    inner_strips = [swapped(middle_inner, "col", 1)]
    outer_strips = [swapped_outward(middle_outer, "col")]
    sums, partner = tied(sums, partner)
    passed = handed_on(partner, "row")
    near_all, near_inner, near_outer = gather(0, partner_below, near, total, partner, 2)
    inner_strips.append(swapped(near_inner, "col", 1))
    outer_strips.append(swapped_outward(near_outer, "col"))
    sums = sums + swapped(sums, "row", 1)
    probe = illuminate(col_bits, sums, probe)
    for bit in reversed(range(col_bits)):
        other = swapped(probe, "col", 1 << bit)
        if bit == col_bits - 1:
            other, outer_strips[0], inner_strips[0] = tied(other, outer_strips[0], inner_strips[0])
        probe = join(bit, probe, other)
    passed, probe, outer_strips[1], inner_strips[1] = tied(passed, probe, outer_strips[1], inner_strips[1])
    far_all, far_inner, far_outer = gather(0, other_below, near, total, passed, 2)
    inner_strips.append(swapped(far_inner, "col", 1))
    outer_strips.append(swapped_outward(far_outer, "col"))
    field = widen(pieces, dense, total, near_all, far_all, inner_strips, outer_strips)

    kept, sent, own = scan_step(1, True, offsets, probe, measured, table, field)
    total, middle_right = place(1, offsets, own, tile, 1)
    dense = density(1, False, around, probe, tile)
    upper = moved_down(own)
    came = swapped(sent, "col", 1)
    for bit in range(1, col_bits):
        kept, sent = fold(bit, kept, came)
        came = swapped(sent, "col", 1 << bit)
    came, middle_right, dense = tied(came, middle_right, dense)
    sums = kept + came
    left_rest = shifted(middle_right, "col", 1)
    sums, upper, left_rest = tied(sums, upper, left_rest)
    top, right_top = gather(1, never_below, near, total, upper, 1)
    left_top = shifted(right_top, "col", 1)
    for bit in range(row_bits):
        sums = sums + swapped(sums, "row", 1 << bit)
    sums, left_top = tied(sums, left_top)
    field = renew(field, dense, total, top, left_top, left_rest)
    probe = illuminate(col_bits, sums, probe)
    for bit in reversed(range(col_bits)):
        other = swapped(probe, "col", 1 << bit)
        if bit == 1:
            other, field = tied(other, field)
        probe = join(bit, probe, other)
    return field, probe


def solution(mesh):
    placed = (
        P(None, "row", "col"),
        P(),
        P("row", "col", None, None, None, None),
        P("row", "col", None, None, None),
    )

    def whole(object_field, probe, amplitudes, offsets):
        table = jnp.asarray(dft_tables(probe.shape[1]))
        body = jax.shard_map(
            local,
            mesh=mesh,
            in_specs=(P(),) + placed,
            out_specs=(P(None, "row", "col"), P()),
            check_vma=False,
        )
        return body(table, object_field, probe, amplitudes, offsets)

    return whole
```

```python
import functools
import math

import jax
import jax.numpy as jnp
import ml_dtypes
import numpy as np
from jax import lax
from jax.experimental import pallas as pl
from jax.experimental.pallas import tpu as pltpu
from jax.sharding import PartitionSpec as P

softening = 0.1
object_damping = 0.5
probe_damping = 1.0
MIB = 1 << 20
lane = 128
SCAN_LIMIT = 24 * MIB
VMEM = pltpu.VMEM
SMEM = pltpu.SMEM


def shifted(array, axis, by):
    peers = lax.axis_size(axis)
    return lax.ppermute(array, axis, [(i, (i + by) % peers) for i in range(peers)])


def moved_on(array, axis):
    peers = lax.axis_size(axis)
    return lax.ppermute(array, axis, [(i, i + 1) for i in range(peers - 1)])


def swapped(array, axis, mask):
    peers = lax.axis_size(axis)
    return lax.ppermute(array, axis, [(i, i ^ mask) for i in range(peers)])


def handed_on(array, axis):
    peers = lax.axis_size(axis)
    return lax.ppermute(array, axis, [(i, (i + 2 - 4 * (i % 2)) % peers) for i in range(peers)])


def swapped_outward(array, axis):
    peers = lax.axis_size(axis)
    pairs = [(i, i + 1) for i in range(1, peers - 1, 2)]
    return lax.ppermute(array, axis, pairs + [(k, i) for i, k in pairs])


def dft_tables(length):
    half = length // 2
    index = np.arange(half)
    parts = []
    for odd in range(2):
        phase = ((2 * index[:, None] + odd) * index[None, :] % length) * (2.0 * math.pi / length)
        real, imag = np.cos(phase) / math.sqrt(length), -np.sin(phase) / math.sqrt(length)
        full = np.block([[real, -imag], [imag, real]])
        for value in (full, full.T):
            high = value.astype(ml_dtypes.bfloat16)
            parts += [high, (value - high.astype(np.float64)).astype(ml_dtypes.bfloat16)]
    return np.stack(parts)


def halves(value):
    high = value.astype(jnp.bfloat16)
    return high, (value - high.astype(jnp.float32)).astype(jnp.bfloat16)


def product(a, b):
    return jnp.dot(a, b, preferred_element_type=jnp.float32)


def left_product(table_ref, number, data):
    top, rest = halves(data)
    high, low = table_ref[2 * number], table_ref[2 * number + 1]
    return product(high, top) + product(high, rest) + product(low, top)


def right_product(data, table_ref, number):
    top, rest = halves(data)
    high, low = table_ref[2 * number], table_ref[2 * number + 1]
    return product(top, high) + product(rest, high) + product(top, low)


def stacked(values, axis):
    return jnp.concatenate(values, axis=axis)


def forward(table_ref, real, imag):
    half = real.shape[0] // 2
    even = stacked([real[:half] + real[half:], imag[:half] + imag[half:]], 0)
    odd = stacked([real[:half] - real[half:], imag[:half] - imag[half:]], 0)
    even, odd = left_product(table_ref, 0, even), left_product(table_ref, 2, odd)
    real, imag = stacked([even[:half], odd[:half]], 0), stacked([even[half:], odd[half:]], 0)
    even = stacked([real[:, :half] + real[:, half:], imag[:, :half] + imag[:, half:]], 1)
    odd = stacked([real[:, :half] - real[:, half:], imag[:, :half] - imag[:, half:]], 1)
    even, odd = right_product(even, table_ref, 1), right_product(odd, table_ref, 3)
    return stacked([even[:, :half], odd[:, :half]], 1), stacked([even[:, half:], odd[:, half:]], 1)


def backward(table_ref, real, imag):
    half = real.shape[0] // 2
    even = left_product(table_ref, 1, stacked([real[:half], imag[:half]], 0))
    odd = left_product(table_ref, 3, stacked([real[half:], imag[half:]], 0))
    one, two = even + odd, even - odd
    real, imag = stacked([one[:half], two[:half]], 0), stacked([one[half:], two[half:]], 0)
    even = right_product(stacked([real[:, :half], imag[:, :half]], 1), table_ref, 0)
    odd = right_product(stacked([real[:, half:], imag[:, half:]], 1), table_ref, 2)
    one, two = even + odd, even - odd
    return stacked([one[:, :half], two[:, :half]], 1), stacked([one[:, half:], two[:, half:]], 1)


def reorder_kernel(amplitude_ref, out_ref):
    side = amplitude_ref.shape[3]
    half = side // 2

    def choice(axis):
        target = lax.broadcasted_iota(jnp.int32, (side, side), axis)
        source = lax.broadcasted_iota(jnp.int32, (side, side), 1 - axis)
        wanted = jnp.where(target < half, 2 * target, 2 * (target - half) + 1)
        return jnp.where(source == wanted, 1.0, 0.0).astype(jnp.bfloat16)

    rows, cols = choice(0), choice(1)
    for sweep in range(amplitude_ref.shape[0]):
        for scan in range(amplitude_ref.shape[1]):
            moved = product(rows, amplitude_ref[sweep, scan]).astype(jnp.bfloat16)
            out_ref[sweep, scan] = product(moved, cols).astype(jnp.bfloat16)


def reorder(amplitudes):
    return pl.pallas_call(
        reorder_kernel,
        out_shape=jax.ShapeDtypeStruct(amplitudes.shape, amplitudes.dtype),
        in_specs=[pl.BlockSpec(memory_space=VMEM)],
        out_specs=pl.BlockSpec(memory_space=VMEM),
        compiler_params=pltpu.CompilerParams(vmem_limit_bytes=8 * MIB),
        cost_estimate=pl.CostEstimate(flops=300_000_000, bytes_accessed=MIB, transcendentals=0),
        name="reorder",
    )(amplitudes)


def split_column(column):
    return lax.div(column, lane), lax.rem(column, lane)


def taken(ref, plane, row, column, side):
    first, shift = split_column(column)
    count = side // lane + 1
    slabs = [ref[plane, first + k, pl.ds(row, side), :] for k in range(count)]
    return pltpu.roll(jnp.concatenate(slabs, axis=1), count * lane - shift, 1)[:, :side]


def turned(value, shift):
    side = value.shape[0]
    wide = jnp.concatenate([value, jnp.zeros((side, lane), jnp.float32)], axis=1)
    return pltpu.roll(wide, shift, 1)


def add_slabs(ref, lead, row, first, wide):
    side = wide.shape[0]
    for k in range(wide.shape[1] // lane):
        spot = lead + (first + k, pl.ds(row, side), slice(None))
        ref[spot] += wide[:, k * lane : (k + 1) * lane]


def columns(number):
    return slice(number * lane, (number + 1) * lane)


def whole_spec(count):
    return [pl.BlockSpec(memory_space=VMEM)] * count


def offsets_spec():
    return pl.BlockSpec(memory_space=SMEM)


def shape_of(*dims):
    return jax.ShapeDtypeStruct(dims, jnp.float32)


def cost(flops, moved):
    return pl.CostEstimate(flops=flops, bytes_accessed=moved, transcendentals=0)


def corner_of(offsets_ref, down, along, sweep, scan):
    spot = (down + 1, along + 1, sweep, scan)
    return offsets_ref[spot + (0,)], offsets_ref[spot + (1,)]


def halves_of(bit, half):
    mine = lax.rem(lax.axis_index("col") >> bit, 2)
    kept = pl.ds(pl.multiple_of(mine * half, 8), half)
    return kept, pl.ds(pl.multiple_of((1 - mine) * half, 8), half)


def scan_kernel(sweep, last, counts, offsets_ref, *refs):
    inputs, outputs, scratch = counts
    probe_hbm, amplitude_hbm, table_hbm = refs[:3]
    field_in = refs[3:inputs]
    outs_hbm = refs[inputs : inputs + outputs]
    rest = refs[inputs + outputs :]
    probe_ref, amplitude_ref, table_ref, sums_ref, windows_ref = rest[:5]
    small_sem, field_sem, out_sem = rest[5:8]
    side = probe_ref.shape[1]
    copies = []

    def fetch(source, target):
        copies.append(pltpu.make_async_copy(source, target, field_sem))

    small = [
        pltpu.make_async_copy(table_hbm, table_ref, small_sem.at[0]),
        pltpu.make_async_copy(probe_hbm, probe_ref, small_sem.at[1]),
        pltpu.make_async_copy(amplitude_hbm.at[sweep], amplitude_ref, small_sem.at[2]),
    ]
    if last:
        field_ref = field_in[0]
    else:
        own_hbm, right_hbm, first_hbm, second_hbm, corner_hbm = field_in
        field_ref = rest[8]
        rows, edge = own_hbm.shape[1], side // lane
        slabs = own_hbm.shape[2] // lane
        for k in range(slabs):
            fetch(own_hbm.at[:, :, columns(k)], field_ref.at[:, k, :rows])
        for k in range(edge):
            fetch(right_hbm.at[:, :, columns(k)], field_ref.at[:, slabs + k, :rows])
            fetch(first_hbm.at[:, :, columns(k)], field_ref.at[:, k, rows:])
            fetch(corner_hbm.at[:, :, columns(k)], field_ref.at[:, slabs + k, rows:])
        for k in range(edge, slabs):
            fetch(second_hbm.at[:, :, columns(k - edge)], field_ref.at[:, k, rows:])
    small[0].start()
    for copy in copies:
        copy.start()
    for copy in small[1:]:
        copy.start()
    small[0].wait()
    for copy in small[1:]:
        copy.wait()
    for copy in copies:
        copy.wait()
    probe_real, probe_imag = probe_ref[0], probe_ref[1]
    pending = []
    for scan in range(2):
        row, column = offsets_ref[0, 0, sweep, scan, 0], offsets_ref[0, 0, sweep, scan, 1]
        patch_real = taken(field_ref, 0, row, column, side)
        patch_imag = taken(field_ref, 1, row, column, side)
        wave_real = probe_real * patch_real - probe_imag * patch_imag
        wave_imag = probe_real * patch_imag + probe_imag * patch_real
        far_real, far_imag = forward(table_ref, wave_real, wave_imag)
        scale = amplitude_ref[scan].astype(jnp.float32) * lax.rsqrt(
            far_real * far_real + far_imag * far_imag + softening
        )
        back_real, back_imag = backward(table_ref, far_real * scale, far_imag * scale)
        diff_real = back_real - wave_real
        diff_imag = back_imag - wave_imag
        term_real = probe_real * diff_real + probe_imag * diff_imag
        term_imag = probe_real * diff_imag - probe_imag * diff_real
        windows_ref[scan, 0] = term_real
        windows_ref[scan, 1] = term_imag
        copy = pltpu.make_async_copy(windows_ref.at[scan], outs_hbm[2].at[scan], out_sem)
        copy.start()
        pending.append(copy)
        sums = (
            patch_real * diff_real + patch_imag * diff_imag,
            patch_real * diff_imag - patch_imag * diff_real,
            patch_real * patch_real + patch_imag * patch_imag,
        )
        for number, value in enumerate(sums):
            if scan == 0:
                sums_ref[number] = value
            else:
                sums_ref[number] += value
    kept, sent = halves_of(0, outs_hbm[0].shape[1])
    outs = [(sums_ref.at[:, sent], outs_hbm[1]), (sums_ref.at[:, kept], outs_hbm[0])]
    outs = [pltpu.make_async_copy(source, target, out_sem) for source, target in outs]
    for copy in outs:
        copy.start()
    for copy in pending + outs:
        copy.wait()


def scan_step(sweep, last, offsets, probe, amplitudes, table, *field):
    side = probe.shape[1]
    shapes = [shape_of(3, side // 2, side)] * 2 + [shape_of(2, 2, side, side)]
    scratch = [
        VMEM(probe.shape, jnp.float32),
        VMEM(amplitudes.shape[1:], amplitudes.dtype),
        VMEM(table.shape, table.dtype),
        VMEM((3, side, side), jnp.float32),
        VMEM((2, 2, side, side), jnp.float32),
        pltpu.SemaphoreType.DMA((3,)),
        pltpu.SemaphoreType.DMA,
        pltpu.SemaphoreType.DMA,
    ]
    if not last:
        rows, cols = field[0].shape[1:]
        scratch.append(VMEM((2, (cols + side) // lane, rows + side, lane), jnp.float32))
    anywhere = pl.BlockSpec(memory_space=pl.ANY)
    counts = (3 + len(field), len(shapes), len(scratch))
    return pl.pallas_call(
        functools.partial(scan_kernel, sweep, last, counts),
        out_shape=shapes,
        in_specs=[offsets_spec()] + [anywhere] * 3 + (whole_spec(1) if last else [anywhere] * len(field)),
        out_specs=[anywhere] * len(shapes),
        scratch_shapes=scratch,
        compiler_params=pltpu.CompilerParams(vmem_limit_bytes=SCAN_LIMIT),
        cost_estimate=cost(7_000_000_000, 12 * MIB),
        name="scan",
    )(offsets, probe, amplitudes, table, *field)


def edge_starts(count, slabs, edge):
    if count < 2:
        return [slabs - edge] * count
    odd = lax.rem(lax.axis_index("col"), 2)
    return [(1 - odd) * (slabs - edge), odd * (slabs - edge)]


def place_kernel(sweep, offsets_ref, windows_ref, total_ref, *edge_refs):
    side = windows_ref.shape[2]
    edge = side // lane
    slabs, height = total_ref.shape[1:3]
    total_ref[...] = jnp.zeros_like(total_ref)
    for scan in range(2):
        row, column = offsets_ref[0, 0, sweep, scan, 0], offsets_ref[0, 0, sweep, scan, 1]
        first, shift = split_column(column)
        for plane in range(2):
            add_slabs(total_ref, (plane,), row, first, turned(windows_ref[scan, plane], shift))
    for ref, start in zip(edge_refs, edge_starts(len(edge_refs), slabs, edge)):
        ref[...] = total_ref[:, pl.ds(start, edge), side : height - side]


def place(sweep, offsets, windows, tile, sides):
    side = windows.shape[2]
    edge = side // lane
    height, slabs = tile[0] + side, tile[1] // lane + edge
    shapes = [shape_of(2, slabs, height, lane)] + [shape_of(2, edge, height - 2 * side, lane)] * sides
    return pl.pallas_call(
        functools.partial(place_kernel, sweep),
        out_shape=shapes,
        in_specs=[offsets_spec()] + whole_spec(1),
        out_specs=whole_spec(len(shapes)),
        compiler_params=pltpu.CompilerParams(vmem_limit_bytes=4 * MIB),
        cost_estimate=cost(1_000_000, 6 * MIB),
        name="place",
    )(offsets, windows)


def density_kernel(sweep, reach, offsets_ref, probe_ref, out_ref, total_ref):
    side = probe_ref.shape[1]
    slabs, height = out_ref.shape[:2]
    breadth = slabs * lane
    tile = height - side if reach else height
    span = breadth - side if reach else breadth
    total_ref[...] = jnp.zeros_like(total_ref)
    power = probe_ref[0] * probe_ref[0] + probe_ref[1] * probe_ref[1]
    steps = (-1, 0, 1) if reach else (-1, 0)
    for down in steps:
        for along in steps:
            for scan in range(2):
                row, column = corner_of(offsets_ref, down, along, sweep, scan)
                row += side + down * tile
                column += side + along * span

                @pl.when((row > 0) & (row < side + height) & (column > 0) & (column < side + breadth))
                def _():
                    first, shift = split_column(column)
                    add_slabs(total_ref, (), row, first, turned(power, shift))

    out_ref[...] = total_ref[side // lane : side // lane + slabs, side : side + height]


def density(sweep, reach, offsets, probe, tile):
    side = probe.shape[1]
    extra = side if reach else 0
    height, slabs = tile[0] + extra, (tile[1] + extra) // lane
    return pl.pallas_call(
        functools.partial(density_kernel, sweep, reach),
        out_shape=shape_of(slabs, height, lane),
        in_specs=[offsets_spec()] + whole_spec(1),
        out_specs=whole_spec(1)[0],
        scratch_shapes=[VMEM((slabs + 2 * side // lane, height + 2 * side, lane), jnp.float32)],
        compiler_params=pltpu.CompilerParams(vmem_limit_bytes=10 * MIB),
        cost_estimate=cost(1_000_000, 6 * MIB),
        name="density",
    )(offsets, probe)


def gather_kernel(sweep, below_of, offsets_ref, total_ref, windows_ref, all_ref, *refs):
    edge_refs, strip_ref = refs[:-1], refs[-1]
    slabs, side = all_ref.shape[1:3]
    height = total_ref.shape[2]
    edge = side // lane
    below = below_of()
    strip_ref[...] = jnp.zeros_like(strip_ref)
    for scan in range(2):
        row, column = corner_of(offsets_ref, 2 * below - 1, -1, sweep, scan)
        row += (2 * below - 1) * side
        first, shift = split_column(column)

        @pl.when((row > 0) & (row < 2 * side))
        def _():
            for plane in range(2):
                add_slabs(strip_ref, (plane,), row, first, turned(windows_ref[scan, plane], shift))

    base = pl.multiple_of(below * (height - side), 8)
    for plane in range(2):
        for k in range(slabs):
            all_ref[plane, k] = strip_ref[plane, k, side : 2 * side] + total_ref[plane, k, pl.ds(base, side)]
    for ref, start in zip(edge_refs, edge_starts(len(edge_refs), slabs, edge)):
        ref[...] = all_ref[:, pl.ds(start, edge)]


def partner_below():
    return 1 - lax.rem(lax.axis_index("row"), 2)


def other_below():
    return lax.rem(lax.axis_index("row"), 2)


def never_below():
    return jnp.int32(0)


def gather(sweep, below_of, offsets, total, windows, sides):
    side = windows.shape[2]
    slabs = total.shape[1]
    return pl.pallas_call(
        functools.partial(gather_kernel, sweep, below_of),
        out_shape=[shape_of(2, slabs, side, lane)] + [shape_of(2, side // lane, side, lane)] * sides,
        in_specs=[offsets_spec()] + whole_spec(2),
        out_specs=whole_spec(1 + sides),
        scratch_shapes=[VMEM((2, slabs, 3 * side, lane), jnp.float32)],
        compiler_params=pltpu.CompilerParams(vmem_limit_bytes=8 * MIB),
        cost_estimate=cost(1_000_000, 6 * MIB),
        name="gather",
    )(offsets, total, windows)


def widen_kernel(*refs):
    own_ref, right_ref, first_ref, second_ref, corner_ref, density_ref, total_ref = refs[:7]
    near_ref, far_ref, inner_refs, outer_refs, out_ref = refs[7], refs[8], refs[9:12], refs[12:15], refs[15]
    side = near_ref.shape[2]
    edge = side // lane
    slabs = out_ref.shape[1] - edge
    rows = out_ref.shape[2] - side
    odd = lax.rem(lax.axis_index("row"), 2) == 1
    odd_col = lax.rem(lax.axis_index("col"), 2) == 1
    even_col = jnp.logical_not(odd_col)
    for k in range(slabs + edge):
        for top, bottom in ((0, side), (side, rows), (rows, rows + side)):
            part = 1.0 / (density_ref[k, top:bottom] + object_damping)
            for plane in range(2):
                if top == rows:
                    if k < edge:
                        before = first_ref[plane, :, columns(k)]
                    elif k < slabs:
                        before = second_ref[plane, :, columns(k - edge)]
                    else:
                        before = corner_ref[plane, :, columns(k - slabs)]
                elif k < slabs:
                    before = own_ref[plane, top:bottom, columns(k)]
                else:
                    before = right_ref[plane, top:bottom, columns(k - slabs)]

                def picked(near, far):
                    return jnp.where(odd, near, far) if top == 0 else jnp.where(odd, far, near)

                def beside(outward, at):
                    if top == side:
                        return jnp.where(outward, outer_refs[0][plane, at], inner_refs[0][plane, at])
                    near = jnp.where(outward, outer_refs[1][plane, at], inner_refs[1][plane, at])
                    far = jnp.where(outward, outer_refs[2][plane, at], inner_refs[2][plane, at])
                    return picked(near, far)

                if top == side:
                    terms = total_ref[plane, k, top:bottom]
                else:
                    terms = picked(near_ref[plane, k], far_ref[plane, k])
                if k < edge:
                    terms += beside(even_col, k)
                if k >= slabs:
                    terms += beside(odd_col, k - slabs)
                out_ref[plane, k, top:bottom] = before + terms * part


def widen(pieces, dense, total, near, far, inner, outer):
    return pl.pallas_call(
        widen_kernel,
        out_shape=shape_of(*total.shape),
        in_specs=whole_spec(15),
        out_specs=whole_spec(1)[0],
        compiler_params=pltpu.CompilerParams(vmem_limit_bytes=6 * MIB),
        cost_estimate=cost(4_000_000, 20 * MIB),
        name="widen",
    )(*pieces, dense, total, near, far, *inner, *outer)


def renew_kernel(field_ref, density_ref, total_ref, top_ref, left_top_ref, left_rest_ref, out_ref):
    slabs, rows = density_ref.shape[:2]
    edge, side = left_top_ref.shape[1:3]
    for k in range(slabs):
        part = 1.0 / (density_ref[k] + object_damping)
        for plane in range(2):
            top = top_ref[plane, k]
            rest = total_ref[plane, k, side:rows]
            if k < edge:
                top += left_top_ref[plane, k]
                rest += left_rest_ref[plane, k]
            out_ref[plane, :side, columns(k)] = field_ref[plane, k, :side] + top * part[:side]
            out_ref[plane, side:, columns(k)] = field_ref[plane, k, side:rows] + rest * part[side:]


def renew(field, dense, total, top, left_top, left_rest):
    slabs, rows = dense.shape[:2]
    return pl.pallas_call(
        renew_kernel,
        out_shape=shape_of(2, rows, slabs * lane),
        in_specs=whole_spec(6),
        out_specs=whole_spec(1)[0],
        compiler_params=pltpu.CompilerParams(vmem_limit_bytes=4 * MIB),
        cost_estimate=cost(4_000_000, 10 * MIB),
        name="renew",
    )(field, dense, total, top, left_top, left_rest)


def fold_kernel(bit, value_ref, came_ref, kept_ref, sent_ref, total_ref):
    total_ref[...] = value_ref[...] + came_ref[...]
    kept, sent = halves_of(bit, kept_ref.shape[1])
    kept_ref[...] = total_ref[:, kept]
    sent_ref[...] = total_ref[:, sent]


def fold(bit, value, came):
    planes, rows, side = value.shape
    return pl.pallas_call(
        functools.partial(fold_kernel, bit),
        out_shape=[shape_of(planes, rows // 2, side)] * 2,
        in_specs=whole_spec(2),
        out_specs=whole_spec(2),
        scratch_shapes=[VMEM(value.shape, jnp.float32)],
        compiler_params=pltpu.CompilerParams(vmem_limit_bytes=4 * MIB),
        cost_estimate=cost(100_000, MIB),
        name="fold",
    )(value, came)


def join_kernel(bit, value_ref, other_ref, out_ref):
    kept, sent = halves_of(bit, value_ref.shape[1])
    out_ref[:, kept] = value_ref[...]
    out_ref[:, sent] = other_ref[...]


def join(bit, value, other):
    planes, rows, side = value.shape
    return pl.pallas_call(
        functools.partial(join_kernel, bit),
        out_shape=shape_of(planes, 2 * rows, side),
        in_specs=whole_spec(2),
        out_specs=whole_spec(1)[0],
        compiler_params=pltpu.CompilerParams(vmem_limit_bytes=4 * MIB),
        cost_estimate=cost(100_000, MIB),
        name="join",
    )(value, other)


def illuminate_kernel(bits, sums_ref, probe_ref, out_ref):
    rows = sums_ref.shape[1]
    start, half = 0, probe_ref.shape[1]
    for bit in range(bits):
        half //= 2
        start += lax.rem(lax.axis_index("col") >> bit, 2) * half
    spot = pl.ds(pl.multiple_of(start, 8), rows)
    part = 1.0 / (sums_ref[2] + probe_damping)
    for plane in range(2):
        out_ref[plane] = probe_ref[plane, spot] + sums_ref[plane] * part


def illuminate(bits, sums, probe):
    return pl.pallas_call(
        functools.partial(illuminate_kernel, bits),
        out_shape=shape_of(2, *sums.shape[1:]),
        in_specs=whole_spec(2),
        out_specs=whole_spec(1)[0],
        compiler_params=pltpu.CompilerParams(vmem_limit_bytes=4 * MIB),
        cost_estimate=cost(100_000, MIB),
        name="illuminate",
    )(sums, probe)


def tied(*values):
    return lax.optimization_barrier(values)


def local(table, object_field, probe, amplitudes, offsets):
    side = probe.shape[1]
    tile = object_field.shape[1:]
    measured = reorder(amplitudes[0, 0])
    col_bits = int(math.log2(lax.axis_size("col")))
    row_bits = int(math.log2(lax.axis_size("row")))

    strip, rest = tied(object_field[:, :side, :side], object_field)
    first = shifted(strip, "row", -1)
    second = shifted(rest[:, :side, side:], "row", -1)
    right = shifted(object_field[:, :, :side], "col", -1)
    near = jnp.concatenate([shifted(offsets, "row", 1), offsets, shifted(offsets, "row", -1)], axis=0)
    first, near = tied(first, near)
    corner = shifted(first, "col", -1)
    pieces = (object_field, right, first, second, corner)

    kept, sent, own = scan_step(0, False, offsets, probe, measured, table, *pieces)
    total, middle_inner, middle_outer = place(0, offsets, own, tile, 2)
    around = jnp.concatenate([shifted(near, "col", 1), near, shifted(near, "col", -1)], axis=1)
    dense = density(0, True, around, probe, tile)
    partner = swapped(own, "row", 1)
    came = swapped(sent, "col", 1)
    for bit in range(1, col_bits):
        kept, sent = fold(bit, kept, came)
        came = swapped(sent, "col", 1 << bit)
    came, around = tied(came, around)
    sums = kept + came
    for bit in reversed(range(1, row_bits)):
        came = swapped(sums, "row", 1 << bit)
        if bit == row_bits - 1:
            came, dense, middle_inner, middle_outer = tied(came, dense, middle_inner, middle_outer)
        sums = sums + came
    inner_strips = [swapped(middle_inner, "col", 1)]
    outer_strips = [swapped_outward(middle_outer, "col")]
    sums, partner = tied(sums, partner)
    passed = handed_on(partner, "row")
    near_all, near_inner, near_outer = gather(0, partner_below, near, total, partner, 2)
    inner_strips.append(swapped(near_inner, "col", 1))
    outer_strips.append(swapped_outward(near_outer, "col"))
    sums = sums + swapped(sums, "row", 1)
    probe = illuminate(col_bits, sums, probe)
    for bit in reversed(range(col_bits)):
        other = swapped(probe, "col", 1 << bit)
        if bit == col_bits - 1:
            other, outer_strips[0], inner_strips[0] = tied(other, outer_strips[0], inner_strips[0])
        probe = join(bit, probe, other)
    passed, probe, outer_strips[1], inner_strips[1] = tied(passed, probe, outer_strips[1], inner_strips[1])
    far_all, far_inner, far_outer = gather(0, other_below, near, total, passed, 2)
    inner_strips.append(swapped(far_inner, "col", 1))
    outer_strips.append(swapped_outward(far_outer, "col"))
    field = widen(pieces, dense, total, near_all, far_all, inner_strips, outer_strips)

    kept, sent, own = scan_step(1, True, offsets, probe, measured, table, field)
    total, middle_right = place(1, offsets, own, tile, 1)
    dense = density(1, False, around, probe, tile)
    upper = moved_on(own, "row")
    came = swapped(sent, "col", 1)
    for bit in range(1, col_bits):
        kept, sent = fold(bit, kept, came)
        came = swapped(sent, "col", 1 << bit)
    came, middle_right, dense = tied(came, middle_right, dense)
    sums = kept + came
    left_rest = moved_on(middle_right, "col")
    sums, upper, left_rest = tied(sums, upper, left_rest)
    top, right_top = gather(1, never_below, near, total, upper, 1)
    left_top = moved_on(right_top, "col")
    for bit in range(row_bits):
        sums = sums + swapped(sums, "row", 1 << bit)
    sums, left_top = tied(sums, left_top)
    field = renew(field, dense, total, top, left_top, left_rest)
    probe = illuminate(col_bits, sums, probe)
    for bit in reversed(range(col_bits)):
        other = swapped(probe, "col", 1 << bit)
        if bit == 1:
            other, field = tied(other, field)
        probe = join(bit, probe, other)
    return field, probe


def solution(mesh):
    placed = (
        P(None, "row", "col"),
        P(),
        P("row", "col", None, None, None, None),
        P("row", "col", None, None, None),
    )

    def whole(object_field, probe, amplitudes, offsets):
        table = jnp.asarray(dft_tables(probe.shape[1]))
        body = jax.shard_map(
            local,
            mesh=mesh,
            in_specs=(P(),) + placed,
            out_specs=(P(None, "row", "col"), P()),
            check_vma=False,
        )
        return body(table, object_field, probe, amplitudes, offsets)

    return whole
```
